32 devices in a mesh: lon: 4 (over y, core), batch: 8 (over z, x).
Axes of the slice: x: 2, y: 2, z: 4, core: 2. Of those that a mesh axis runs over, the one named last changes fastest.
Arguments:
- fields: float32 [8, 32, 64, 5], P('batch', None, 'lon'), may hold values from -6 to 6
- velocity: float32 [8, 32, 64, 10], P('batch', None, 'lon'), may hold values from -3 to 3
- context: float32 [8, 32, 64, 75], P('batch', None, 'lon'), may hold values from -6 to 6
- masks: int32 [8, 32, 64], P('batch', None, 'lon'), may hold values from 0 to 1, as said below
- window: int32 [32, 64, 8], P(None, 'lon'), may hold values from 0 to 95
- lift_weight: float32 [3, 3, 100, 128], replicated, may hold values from -0.1875 to 0.1875
- lift_bias: float32 [128], replicated, may hold values from -3 to 3
- norm_gain: float32 [2, 128], replicated, may hold values from 0.5 to 1.5
- norm_shift: float32 [2, 128], replicated, may hold values from -3 to 3
- conv_weight: float32 [2, 3, 3, 128, 128], replicated, may hold values from -0.1875 to 0.1875
- attn_qkv: float32 [128, 384], replicated, may hold values from -0.5 to 0.5
- attn_out: float32 [128, 128], replicated, may hold values from -1 to 1
- head_weight: float32 [128, 10], replicated, may hold values from -0.5 to 0.5
- head_bias: float32 [10], replicated, may hold values from -3 to 3
- cot_fields: float32 [8, 32, 64, 5], P('batch', None, 'lon'), may hold values from -6 to 6
- cot_velocity: float32 [8, 32, 64, 10], P('batch', None, 'lon'), may hold values from -6 to 6
Outputs:
- new_fields: float32 [8, 32, 64, 5], P('batch', None, 'lon')
- new_velocity: float32 [8, 32, 64, 10], P('batch', None, 'lon')
- grad_fields: float32 [8, 32, 64, 5], P('batch', None, 'lon')
- grad_velocity: float32 [8, 32, 64, 10], P('batch', None, 'lon')
- grad_lift_weight: float32 [3, 3, 100, 128], replicated
- grad_lift_bias: float32 [128], replicated
- grad_norm_gain: float32 [2, 128], replicated
- grad_norm_shift: float32 [2, 128], replicated
- grad_conv_weight: float32 [2, 3, 3, 128, 128], replicated
- grad_attn_qkv: float32 [128, 384], replicated
- grad_attn_out: float32 [128, 128], replicated
- grad_head_weight: float32 [128, 10], replicated
- grad_head_bias: float32 [10], replicated
The draws below stay inside these ranges and needn't reach their ends.
Inputs may be any that keep to these rules, and one draw needn't show every extreme that they name: `masks`: 1 marks a pixel counted in the statistics; latitude row 16 is counted in every sample and column. `window`: entry k names the key at latitude k % 32 in the column k // 32 - 1 places east of the query's, around the longitude circle.
All inputs are finite; a program needn't handle non-finite values.
Results may differ from the reference program's by a relative error of at most 0.0003.
Values sent between devices are 32-bit elements; how exact they have to be, the bound alone decides.
A program may use at most 320 MiB of HBM per device.

```python
import jax
import jax.numpy as jnp
from jax import lax

V = 5
CTX = 75
CIN = 100
HID = 128
HEADS = 4
WIN = 8
NBLK = 2
NLAT = 32
NLON = 64
SAMPLES = 8


def draw_masks(key, part):
    key = jax.random.fold_in(key, 11)
    levels = jax.random.randint(key, (SAMPLES, NLAT, NLON), 0, 1000)
    column = jnp.arange(NLON)[None, None, :]
    limits = 250 + 500 * column // max(NLON - 1, 1)
    lat_rows = jnp.arange(NLAT)[None, :, None]
    return jnp.where((levels < limits) | (lat_rows == NLAT // 2), 1, 0).astype(jnp.int32)


def plant(array, stream_key, least, top_value):
    index_at = [jax.random.randint(jax.random.fold_in(stream_key, axis), (), 0, length) for axis, length in enumerate(array.shape)]
    main_axis = array.shape.index(max(array.shape))
    next_to = index_at[:main_axis] + [(index_at[main_axis] + 1) % array.shape[main_axis]] + index_at[main_axis + 1:]
    return array.at[tuple(index_at)].set(least).at[tuple(next_to)].set(top_value)


def shard_levels(rng, dims, pieces, least, top_value):
    def one(position, parts):
        draws = jax.random.uniform(jax.random.fold_in(jax.random.fold_in(rng, 6), position), (parts,), jnp.float32, least / len(pieces), top_value / len(pieces))
        return jnp.repeat(jnp.exp(draws), dims[position] // parts).reshape((-1,) + (1,) * (len(dims) - position - 1))

    factor_of = one(*pieces[0])
    for cut in pieces[1:]:
        factor_of = factor_of * one(*cut)
    return factor_of


def normal_values(rng, extent, width, bound, cuts=(), kind=jnp.bfloat16):
    entries = width * jax.random.normal(rng, extent, jnp.float32)
    if cuts:
        entries = entries * shard_levels(rng, extent, cuts, -0.22, 0.18)
    return jnp.clip(entries, -bound, bound).astype(kind)


def setup_inputs(seed: int = 0) -> dict:
    seeds = jax.random.split(jax.random.key(seed), 17)
    fields = normal_values(seeds[0], (SAMPLES, NLAT, NLON, V), 1.0, 6.0, ((0, 8), (2, 4)), jnp.float32)
    velocity = normal_values(seeds[1], (SAMPLES, NLAT, NLON, 2 * V), 0.5, 3.0, ((0, 8), (2, 4)), jnp.float32)
    context = normal_values(seeds[2], (SAMPLES, NLAT, NLON, CTX), 1.0, 6.0, ((0, 8), (2, 4)), jnp.float32)
    masks = draw_masks(jax.random.fold_in(seeds[16], 71), 0)
    window = plant(jax.random.randint(seeds[4], (NLAT, NLON, WIN), 0, 3 * NLAT), jax.random.fold_in(seeds[4], 1), 0, (3 * NLAT) - 1).astype(jnp.int32)
    lift_weight = normal_values(seeds[5], (3, 3, CIN, HID), (9 * CIN) ** -0.5, 0.1875, (), jnp.float32)
    lift_bias = normal_values(seeds[6], (HID,), 0.5, 3.0, (), jnp.float32)
    norm_gain = jnp.clip(1.0 + 0.1 * jax.random.normal(seeds[7], (NBLK, HID), jnp.float32), 0.5, 1.5)
    norm_shift = normal_values(seeds[8], (NBLK, HID), 0.5, 3.0, (), jnp.float32)
    conv_weight = normal_values(seeds[9], (NBLK, 3, 3, HID, HID), (9 * HID) ** -0.5, 0.1875, (), jnp.float32)
    attn_qkv = normal_values(seeds[10], (HID, 3 * HID), HID ** -0.5, 0.5, (), jnp.float32)
    attn_out = normal_values(seeds[11], (HID, HID), (HID // 4) ** -0.5, 1.0, (), jnp.float32)
    head_weight = normal_values(seeds[12], (HID, 2 * V), HID ** -0.5, 0.5, (), jnp.float32)
    head_bias = normal_values(seeds[13], (2 * V,), 0.5, 3.0, (), jnp.float32)
    cot_fields = normal_values(seeds[14], (SAMPLES, NLAT, NLON, V), 1.0, 6.0, ((0, 8), (2, 4)), jnp.float32)
    cot_velocity = normal_values(seeds[15], (SAMPLES, NLAT, NLON, 2 * V), 1.0, 6.0, ((0, 8), (2, 4)), jnp.float32)
    return {"fields": fields, "velocity": velocity, "context": context, "masks": masks, "window": window, "lift_weight": lift_weight, "lift_bias": lift_bias, "norm_gain": norm_gain, "norm_shift": norm_shift, "conv_weight": conv_weight, "attn_qkv": attn_qkv, "attn_out": attn_out, "head_weight": head_weight, "head_bias": head_bias, "cot_fields": cot_fields, "cot_velocity": cot_velocity}


@jax.custom_vjp
def low(v):
    return lax.optimization_barrier(v.astype(jnp.bfloat16)).astype(jnp.float32)

@jax.custom_vjp
def low_back(v):
    return v

def low_keep(v):
    return (low(v), None)

def low_pass(kept, grad):
    return (grad,)

def back_keep(v):
    return (v, None)

def back_low(kept, grad):
    return (low(grad),)
low.defvjp(low_keep, low_pass)
low_back.defvjp(back_keep, back_low)
highest = lax.Precision.HIGHEST
epsilon = 1e-05
step_size = 0.25

def cycle_pad(values):
    return jnp.concatenate([values[:, :, -1:], values, values[:, :, :1]], axis=2)

def flux_stack(fields, velocity):
    count_var = fields.shape[-1]
    return jnp.concatenate([fields, fields * velocity[..., :count_var], fields * velocity[..., count_var:]], axis=-1)

def state_terms(padded, velocity, context):
    count_var = velocity.shape[-1] // 2
    framed = jnp.pad(padded, ((0, 0), (1, 1), (0, 0), (0, 0)))
    centre = framed[:, 1:-1, 1:-1]
    lat_diff = 0.5 * (framed[:, 2:, 1:-1] - framed[:, :-2, 1:-1])
    lon_diff = 0.5 * (framed[:, 1:-1, 2:] - framed[:, 1:-1, :-2])
    tendency = -(lat_diff[..., count_var:2 * count_var] + lon_diff[..., 2 * count_var:])
    inputs = jnp.concatenate([centre[..., :count_var], lat_diff[..., :count_var], lon_diff[..., :count_var], velocity, context], axis=-1)
    return (inputs, tendency)

def conv_same(padded, kernel):
    return lax.conv_general_dilated(padded, kernel, (1, 1), ((1, 1), (0, 0)), dimension_numbers=('NHWC', 'HWIO', 'NHWC'), precision=highest)

def lift_layer(padded, kernel, bias_vec):
    return conv_same(padded, kernel) + bias_vec

def norm_act(hidden, first_sum, second_sum, gain_row, shift_row, total_count):
    average = first_sum / total_count
    spread = second_sum / total_count - average * average
    scaled = (hidden - average) * lax.rsqrt(spread + epsilon) * gain_row + shift_row
    return jax.nn.gelu(scaled, approximate=False)

def project_keys(hidden, qkv_weight):
    mixing = jnp.einsum('abcd,de->abce', hidden, qkv_weight, precision=highest)
    channels = hidden.shape[-1]
    return (mixing[..., :channels], mixing[..., channels:])

def attend(queries, keyval_padded, out_weight, window_local):
    samples, lat_count, lon_count, channels = queries.shape
    keys_count = window_local.shape[-1]
    padded_width = lon_count + 2
    head_size = channels // HEADS
    column = lax.broadcasted_iota(jnp.int32, window_local.shape, 1)
    flat_index = window_local % lat_count * padded_width + column + window_local // lat_count
    flat_pairs = keyval_padded.reshape(samples, lat_count * padded_width, 2 * channels)
    picked = jnp.take(flat_pairs, flat_index.reshape(-1), axis=1)
    picked = picked.reshape(samples, lat_count, lon_count, keys_count, 2, HEADS, head_size)
    heads_query = queries.reshape(samples, lat_count, lon_count, HEADS, head_size)
    scores = jnp.einsum('abchd,abcwhd->abchw', heads_query, picked[..., 0, :, :], precision=highest) * head_size ** (-0.5)
    weights = jax.nn.softmax(scores, axis=-1)
    blended = jnp.einsum('abchw,abcwhd->abchd', weights, picked[..., 1, :, :], precision=highest)
    return jnp.einsum('abce,ef->abcf', blended.reshape(samples, lat_count, lon_count, channels), out_weight, precision=highest)

def head_layer(hidden, head_weight, bias_vec):
    return jnp.einsum('abcd,de->abce', hidden, head_weight, precision=highest) + bias_vec

def velocity_field(fields, velocity, context, weight_mask, window, params):
    lift_weight, lift_bias, norm_gain, norm_shift, conv_weight, attn_qkv, attn_out, head_weight, head_bias = params
    stacked = flux_stack(fields, velocity)
    inputs, tendency = state_terms(cycle_pad(stacked), velocity, context)
    hidden = lift_layer(cycle_pad(inputs), lift_weight, lift_bias)
    total_count = jnp.sum(weight_mask)
    for block_index in range(NBLK):
        weighted = hidden * weight_mask[..., None]
        first_sum = lax.optimization_barrier(jnp.sum(weighted, axis=(0, 1, 2)))
        second_sum = lax.optimization_barrier(jnp.sum(weighted * hidden, axis=(0, 1, 2)))
        activity = norm_act(hidden, first_sum, second_sum, norm_gain[block_index], norm_shift[block_index], total_count)
        hidden = hidden + conv_same(cycle_pad(activity), conv_weight[block_index])
    queries, keyval = project_keys(hidden, attn_qkv)
    hidden = hidden + attend(queries, cycle_pad(keyval), attn_out, window)
    acceleration = head_layer(hidden, head_weight, head_bias)
    return (tendency, acceleration)

def advance(fields, velocity, context, weight_mask, window, params):
    evaluate = jax.checkpoint(velocity_field)
    factors = (0.5, 0.5, 1.0)
    slopes = []
    current = (fields, velocity)
    for section_index in range(4):
        slope_pair = evaluate(current[0], current[1], context, weight_mask, window, params)
        slopes.append(slope_pair)
        if section_index < 3:
            current = (fields + step_size * factors[section_index] * slope_pair[0], velocity + step_size * factors[section_index] * slope_pair[1])
    new_fields = fields + step_size / 6.0 * (slopes[0][0] + 2.0 * slopes[1][0] + 2.0 * slopes[2][0] + slopes[3][0])
    new_velocity = velocity + step_size / 6.0 * (slopes[0][1] + 2.0 * slopes[1][1] + 2.0 * slopes[2][1] + slopes[3][1])
    return (new_fields, new_velocity)

def reference(fields, velocity, context, masks, window, lift_weight, lift_bias, norm_gain, norm_shift, conv_weight, attn_qkv, attn_out, head_weight, head_bias, cot_fields, cot_velocity):
    weight_mask = masks.astype(jnp.float32)
    params = (lift_weight, lift_bias, norm_gain, norm_shift, conv_weight, attn_qkv, attn_out, head_weight, head_bias)

    def forward(fields_in, velocity_in, params_in):
        return advance(fields_in, velocity_in, context, weight_mask, window, params_in)
    outputs, pull_back = jax.vjp(forward, fields, velocity, params)
    grad_fields, grad_velocity, weight_grads = pull_back((cot_fields, cot_velocity))
    return (outputs[0], outputs[1], grad_fields, grad_velocity, weight_grads[0], weight_grads[1], weight_grads[2], weight_grads[3], weight_grads[4], weight_grads[5], weight_grads[6], weight_grads[7], weight_grads[8])
```

```python
from functools import partial
import math

import jax
import jax.numpy as jnp
from jax import lax
from jax.experimental import pallas as pl
from jax.experimental.pallas import tpu as pltpu
from jax.sharding import PartitionSpec as P

HEADS = 4
SECTIONS = 4
LANES = 128
VARS = 5
MASK_LANE = 127
epsilon = 1e-05
step_size = 0.25
f32 = jnp.float32
bf16 = jnp.bfloat16
MESH = pl.DeviceIdType.MESH


def split(x):
    hi = x.astype(bf16)
    return hi, (x - hi.astype(f32)).astype(bf16)


def dot(a, b, dims=((1,), (0,))):
    return lax.dot_general(a, b, (dims, ((), ())), preferred_element_type=f32)


def lanes_cat(*parts):
    return jnp.concatenate(parts, axis=1)


def factors(n):
    out = []
    while n > 4 and n % 2 == 0:
        out.append(2)
        n //= 2
    if n > 1:
        out.append(n)
    return out


def kernel(
    sizes,
    start_ref,
    window_ref,
    small_ref,
    lift_ref,
    conv_ref,
    qkv_ref,
    out_ref,
    head_ref,
    new_ref,
    grad_ref,
    weights_out,
    norm_out,
    ys,
    xh,
    xl,
    h0,
    h1,
    a1h,
    a1l,
    a2h,
    a2l,
    dg1,
    dg2,
    h2h,
    h2l,
    qh,
    ql,
    kh,
    kl,
    vh,
    vl,
    probs,
    bh,
    bl,
    h3h,
    h3l,
    norms,
    gk,
    acc,
    tend,
    mask,
    mult,
    w3f,
    w3t,
    wq3,
    wqt3,
    wo3,
    wot3,
    wh3,
    wht3,
    tap,
    blend,
    dbh,
    dbl,
    dq,
    dkv,
    dh2,
    de1,
    de0,
    sb,
    rb,
    gw,
    rsb,
    norm_acc,
    bias_acc,
    ar_src,
    ar_buf,
    ar_send,
    ar_recv,
    halo_send,
    halo_recv,
    rs_send,
    rs_recv,
    ag_send,
    ag_recv,
):
    nl, nb, L, W, hid_heads = sizes
    nd = nl * nb
    R = L * W
    R1 = R + 2 * L
    R2 = R + 4 * L
    ch = LANES
    me_l = lax.axis_index("lon")
    me_b = lax.axis_index("batch")
    me = me_l * nb + me_b
    left = (lax.rem(me_l + nl - 1, nl), me_b)
    right = (lax.rem(me_l + 1, nl), me_b)

    def peer(k):
        t = lax.rem(me + k, nd)
        return (t // nb, lax.rem(t, nb))

    barrier = pltpu.get_barrier_semaphore()

    def greet(k, c):
        pl.semaphore_signal(barrier, inc=1, device_id=peer(k), device_id_type=MESH)
        return c

    lax.fori_loop(1, nd, greet, 0)

    def sum_start(a, vals):
        ar_src[a] = vals
        ar_buf[a, me] = vals

        def send(k, c):
            pltpu.make_async_remote_copy(
                ar_src.at[a],
                ar_buf.at[a, me],
                ar_send.at[a],
                ar_recv.at[a],
                device_id=peer(k),
                device_id_type=MESH,
            ).start()
            return c

        lax.fori_loop(1, nd, send, 0)

    def sum_wait(a):
        got = ar_buf.at[a, pl.ds(0, nd - 1)]
        pltpu.make_async_copy(got, got, ar_recv.at[a]).wait()
        pltpu.make_async_copy(got, got, ar_send.at[a]).wait()
        return jnp.sum(ar_buf[a], axis=0)

    def side_copy(h, side, src, dst):
        return pltpu.make_async_remote_copy(
            src,
            dst,
            halo_send.at[h, side],
            halo_recv.at[h, side],
            device_id=left if side == 0 else right,
            device_id_type=MESH,
        )

    def halo_copies(h, buf, s, cols):
        n = cols * L
        lo = 2 * L - n
        to_left = side_copy(
            h, 0, buf.at[s, pl.ds(2 * L, n)], buf.at[s, pl.ds(R + 2 * L, n)]
        )
        to_right = side_copy(
            h, 1, buf.at[s, pl.ds(R + 2 * L - n, n)], buf.at[s, pl.ds(lo, n)]
        )
        return to_left, to_right

    def halo_start(h, buf, s, cols):
        for c in halo_copies(h, buf, s, cols):
            c.start()

    def halo_wait(h, buf, s, cols):
        for c in halo_copies(h, buf, s, cols):
            c.wait()

    def lat_of(n):
        return lax.broadcasted_iota(jnp.int32, (n, LANES), 0) % L

    def north(x):
        n = x.shape[0]
        return jnp.where(lat_of(n) == L - 1, 0.0, pltpu.roll(x, n - 1, 0))

    def south(x):
        n = x.shape[0]
        return jnp.where(lat_of(n) == 0, 0.0, pltpu.roll(x, 1, 0))

    def lat_diff(x):
        return 0.5 * (north(x) - south(x))

    def lane_of(n):
        return lax.broadcasted_iota(jnp.int32, (n, LANES), 1)

    def lroll(x, shift):
        return pltpu.roll(x, shift % LANES, 1)

    def conv(hi, lo, base, n, weights):
        cols_h = [hi[base + j * L : base + j * L + n] for j in range(3)]
        cols_l = [lo[base + j * L : base + j * L + n] for j in range(3)]
        wide = dot(lanes_cat(*cols_h, *cols_l, *cols_h), weights)
        return (
            wide[:, ch : 2 * ch]
            + south(wide[:, :ch])
            + north(wide[:, 2 * ch :])
        )

    def product(x, weights):
        hi, lo = split(x)
        return dot(lanes_cat(hi, lo, hi), weights)

    def rows_product(ah, al, gh, gl):
        t = ((0,), (0,))
        return dot(ah, gh, t) + dot(ah, gl, t) + dot(al, gh, t)

    def lat_triple(x):
        return split(lanes_cat(north(x), x, south(x)))

    def conv_back(gh, gl, n, weights):
        wide = dot(lanes_cat(gh, gl, gh), weights)
        return (
            wide[2 * L : 2 * L + n, :ch]
            + wide[L : L + n, ch : 2 * ch]
            + wide[:n, 2 * ch :]
        )

    def add_conv_grad(base, ah, al, gh, gl):
        for j in range(3):
            part = rows_product(
                ah[j * L : j * L + R], al[j * L : j * L + R], gh, gl
            )
            for i in range(3):
                at = base + (i * 3 + j) * ch
                gw[at : at + ch, :] += part[:, i * ch : (i + 1) * ch]

    lift_base, conv_base = 0, 9 * ch
    qkv_base = 27 * ch
    out_base, head_base = 30 * ch, 31 * ch

    ys[0, 2 * L : 2 * L + R] = start_ref[:, :ch]
    cot = start_ref[:, ch:]
    for s, weight in enumerate((1.0, 2.0, 2.0, 1.0)):
        gk[s] = cot * (weight * step_size / 6.0)
    grad_ref[...] = cot
    acc[...] = jnp.zeros_like(acc)
    gw[...] = jnp.zeros_like(gw)
    norm_acc[...] = jnp.zeros_like(norm_acc)
    bias_acc[...] = jnp.zeros_like(bias_acc)
    mask_own = jnp.broadcast_to(
        start_ref[:, MASK_LANE : MASK_LANE + 1], (R, LANES)
    )
    count_part = jnp.sum(mask_own, axis=0, keepdims=True)

    pl.semaphore_wait(barrier, nd - 1)
    halo_start(0, ys, 0, 2)
    sum_start(4 * SECTIONS, jnp.concatenate([count_part, count_part], axis=0))

    tap[...] = jnp.zeros_like(tap)
    for b in range(3):
        for i in range(3):
            for j in range(3):
                if b == 0:
                    tap[: lift_ref.shape[2]] = lift_ref[i, j]
                    w = tap[...]
                else:
                    w = conv_ref[b - 1, i, j]
                hi, lo = split(w)
                for p, part in enumerate((hi, hi, lo)):
                    at = (p * 3 + j) * ch
                    w3f[b, at : at + ch, i * ch : (i + 1) * ch] = part
                hi, lo = split(w.T)
                for p, part in enumerate((hi, hi, lo)):
                    at = (p * 3 + i) * ch
                    w3t[b, at : at + ch, j * ch : (j + 1) * ch] = part

    def put_three(target, w):
        n = w.shape[0]
        hi, lo = split(w)
        target[:n] = hi
        target[n : 2 * n] = hi
        target[2 * n :] = lo

    put_three(wq3, qkv_ref[...])
    put_three(wqt3, qkv_ref[...].T)
    put_three(wo3, out_ref[...])
    put_three(wot3, out_ref[...].T)
    put_three(wh3, head_ref[...])
    put_three(wht3, head_ref[...].T)

    counted = jnp.zeros((R, LANES), f32)
    key_of = lane_of(R)
    for k in range(window_ref.shape[1]):
        entry = jnp.broadcast_to(window_ref[:, k : k + 1], (R, LANES))
        counted = counted + jnp.where(entry == key_of, 1.0, 0.0)
    mult[...] = counted.reshape(W, L, LANES)
    for s in range(SECTIONS):
        for ref in (kh, kl, vh, vl):
            ref[s, R1:] = jnp.zeros((L, ch), bf16)

    head_rows = lax.broadcasted_iota(jnp.int32, (HEADS * L, ch), 0) // L
    head_lanes = lax.broadcasted_iota(jnp.int32, (HEADS * L, ch), 1) // (ch // HEADS)
    head_mask = jnp.where(head_rows == head_lanes, 1.0, 0.0)
    head_mask_h = head_mask.astype(bf16)
    scale = (ch // HEADS) ** -0.5

    def per_head(x):
        return jnp.concatenate([x] * HEADS, axis=0) * head_mask_h

    def heads_sum(x):
        x = x * head_mask
        return sum(x[h * L : (h + 1) * L] for h in range(1, HEADS)) + x[:L]

    total_count = sum_wait(4 * SECTIONS)[0:1]
    inverse_count = 1.0 / total_count

    lift_bias = small_ref[0:1]
    head_bias = small_ref[1:2]
    gains = [small_ref[2:3], small_ref[3:4]]
    shifts = [small_ref[4:5], small_ref[5:6]]

    def stats(h):
        weighted = h * mask[2 * L : 2 * L + R]
        return jnp.concatenate(
            [
                jnp.sum(weighted, axis=0, keepdims=True),
                jnp.sum(weighted * h, axis=0, keepdims=True),
            ],
            axis=0,
        )

    def normalise(s, b, sums):
        average = sums[0:1] / total_count
        spread = sums[1:2] / total_count - average * average
        inverse = lax.rsqrt(spread + epsilon)
        norms[s, b, 0:1] = average
        norms[s, b, 1:2] = inverse
        return average, inverse

    def activity(h, b, average, inverse):
        z = (h - average) * inverse * gains[b] + shifts[b]
        below = 0.5 * (1.0 + lax.erf(z * (0.5**0.5)))
        slope = below + z * (
            jnp.exp(-0.5 * z * z) * (1.0 / math.sqrt(2.0 * math.pi))
        )
        return z * below, slope

    group = 4

    def forward(s, carry):
        hb = s * 6

        @pl.when(s > 0)
        def _():
            halo_start(hb, ys, s, 2)

        halo_wait(hb, ys, s, 2)

        @pl.when(s == 0)
        def _():
            mask[...] = jnp.broadcast_to(
                ys[0, :, MASK_LANE : MASK_LANE + 1], (R2, LANES)
            )

        y1 = ys[s, L : L + R1]
        lane = lane_of(R1)
        lon = 0.5 * (ys[s, 2 * L : 2 * L + R1] - ys[s, 0:R1])
        x = jnp.where(
            (lane >= VARS) & (lane < 2 * VARS),
            lat_diff(y1),
            jnp.where((lane >= 2 * VARS) & (lane < 3 * VARS), lon, y1),
        )
        hi, lo = split(x)
        xh[s] = hi
        xl[s] = lo
        flux = y1 * lroll(y1, -3 * VARS)
        flux = jnp.where(lane < 2 * VARS, flux, 0.0)
        own_lane = lane_of(R)
        t_lat = jnp.where(own_lane < VARS, lat_diff(flux[L : L + R]), 0.0)
        t_lon = jnp.where(
            own_lane >= VARS, 0.5 * (flux[2 * L : 2 * L + R] - flux[:R]), 0.0
        )
        t = -(t_lat + lroll(t_lon, -VARS))
        tend[...] = t + lroll(t, VARS) + lroll(t, 2 * VARS)

        first = conv(xh.at[s], xl.at[s], 0, R, w3f[0]) + lift_bias
        h0[s, 2 * L : 2 * L + R] = first
        sum_start(s * 4, stats(first))
        halo_start(hb + 1, h0, s, 2)
        average, inverse = normalise(s, 0, sum_wait(s * 4))
        halo_wait(hb + 1, h0, s, 2)
        act, slope = activity(h0[s, L : L + R1], 0, average, inverse)
        dg1[s] = slope[L : L + R]
        hi, lo = split(act)
        a1h[s] = hi
        a1l[s] = lo
        second = h0[s, 2 * L : 2 * L + R] + conv(a1h.at[s], a1l.at[s], 0, R, w3f[1])
        h1[s, 2 * L : 2 * L + R] = second
        sum_start(s * 4 + 1, stats(second))
        halo_start(hb + 2, h1, s, 2)
        average, inverse = normalise(s, 1, sum_wait(s * 4 + 1))
        halo_wait(hb + 2, h1, s, 2)
        act, slope = activity(h1[s], 1, average, inverse)
        dg2[s] = slope[2 * L : 2 * L + R]
        hi, lo = split(act)
        a2h[s] = hi
        a2l[s] = lo
        third = h1[s, L : L + R1] + conv(a2h.at[s], a2l.at[s], 0, R1, w3f[2])
        hi, lo = split(third)
        h2h[s] = hi
        h2l[s] = lo
        mixing = dot(lanes_cat(hi, lo, hi), wq3[...])
        hi, lo = split(mixing[L : L + R, :ch] * scale)
        qh[s] = hi
        ql[s] = lo
        hi, lo = split(mixing[:, ch : 2 * ch])
        kh[s, :R1] = hi
        kl[s, :R1] = lo
        hi, lo = split(mixing[:, 2 * ch :])
        vh[s, :R1] = hi
        vl[s, :R1] = lo

        def attend(g, c):
            cols = [g * group + k for k in range(group)]
            scores = []
            for col in cols:
                at = pl.multiple_of(col * L, L)
                q_h = per_head(qh[s, pl.ds(at, L)])
                q_l = per_head(ql[s, pl.ds(at, L)])
                k_h = kh[s, pl.ds(at, 4 * L)]
                k_l = kl[s, pl.ds(at, 4 * L)]
                scores.append(
                    dot(
                        lanes_cat(q_h, q_l, q_h),
                        lanes_cat(k_h, k_h, k_l),
                        ((1,), (1,)),
                    )
                )
            weights = []
            for col, score in zip(cols, scores):
                m = jnp.concatenate([mult[col]] * HEADS, axis=0)
                score = jnp.where(m > 0.0, score, -1e30)
                top = jnp.max(score, axis=1, keepdims=True)
                e = m * jnp.exp(score - top)
                p = e / jnp.sum(e, axis=1, keepdims=True)
                probs[s, col] = p
                weights.append(p)
            for col, p in zip(cols, weights):
                at = pl.multiple_of(col * L, L)
                p_h, p_l = split(p)
                v_h = vh[s, pl.ds(at, 4 * L)]
                v_l = vl[s, pl.ds(at, 4 * L)]
                o = dot(
                    lanes_cat(p_h, p_l, p_h),
                    jnp.concatenate([v_h, v_h, v_l], axis=0),
                )
                blend[pl.ds(at, L)] = heads_sum(o)
            return c

        lax.fori_loop(0, W // group, attend, 0)
        hi, lo = split(blend[...])
        bh[s] = hi
        bl[s] = lo
        fourth = third[L : L + R] + dot(lanes_cat(hi, lo, hi), wo3[...])
        hi, lo = split(fourth)
        h3h[s] = hi
        h3l[s] = lo
        slope_now = (
            tend[...] + dot(lanes_cat(hi, lo, hi), wh3[...]) + head_bias
        )
        weight = jnp.where((s == 0) | (s == SECTIONS - 1), 1.0, 2.0)
        acc[...] += weight * slope_now

        @pl.when(s < SECTIONS - 1)
        def _():
            factor = jnp.where(s == SECTIONS - 2, 1.0, 0.5) * step_size
            ys[s + 1, 2 * L : 2 * L + R] = (
                ys[0, 2 * L : 2 * L + R] + factor * slope_now
            )

        return carry

    lax.fori_loop(0, SECTIONS, forward, 0)
    new_ref[...] = ys[0, 2 * L : 2 * L + R] + (step_size / 6.0) * acc[...]

    def norm_back(s, b, h, grad_act, slope, through):
        average = norms[s, b, 0:1]
        inverse = norms[s, b, 1:2]
        dz = grad_act * slope
        hat = (h - average) * inverse
        sums = jnp.concatenate(
            [
                jnp.sum(dz, axis=0, keepdims=True),
                jnp.sum(dz * hat, axis=0, keepdims=True),
            ],
            axis=0,
        )
        return sums, through + dz * (gains[b] * inverse)

    def norm_rest(s, b, h, weight_mask, direct, sums):
        average = norms[s, b, 0:1]
        inverse = norms[s, b, 1:2]
        hat = (h - average) * inverse
        norm_acc[b] += sums
        return direct - weight_mask * (
            gains[b] * inverse * inverse_count
        ) * (sums[0:1] + hat * sums[1:2])

    def backward(turn, carry):
        s = SECTIONS - 1 - turn
        hb = s * 6
        g = gk[s]
        g_h, g_l = split(g)
        grad3 = dot(lanes_cat(g_h, g_l, g_h), wht3[...])
        bias_acc[1:2] += jnp.sum(g, axis=0, keepdims=True)
        gw[head_base : head_base + ch] += rows_product(h3h[s], h3l[s], g_h, g_l)
        hi, lo = split(grad3)
        gw[out_base : out_base + ch] += rows_product(bh[s], bl[s], hi, lo)
        hi, lo = split(dot(lanes_cat(hi, lo, hi), wot3[...]))
        dbh[...] = hi
        dbl[...] = lo
        dkv[...] = jnp.zeros_like(dkv)

        def attend_back(gi, c):
            cols = [gi * group + k for k in range(group)]
            dps = []
            for col in cols:
                at = pl.multiple_of(col * L, L)
                d_h = per_head(dbh[pl.ds(at, L)])
                d_l = per_head(dbl[pl.ds(at, L)])
                v_h = vh[s, pl.ds(at, 4 * L)]
                v_l = vl[s, pl.ds(at, 4 * L)]
                dps.append(
                    dot(
                        lanes_cat(d_h, d_l, d_h),
                        lanes_cat(v_h, v_h, v_l),
                        ((1,), (1,)),
                    )
                )
            dss = []
            for col, dp in zip(cols, dps):
                p = probs[s, col]
                mean = jnp.sum(p * dp, axis=1, keepdims=True)
                dss.append(p * (dp - mean))
            for col, ds in zip(cols, dss):
                at = pl.multiple_of(col * L, L)
                ds_h, ds_l = split(ds)
                k_h = kh[s, pl.ds(at, 4 * L)]
                k_l = kl[s, pl.ds(at, 4 * L)]
                o = dot(
                    lanes_cat(ds_h, ds_l, ds_h),
                    jnp.concatenate([k_h, k_h, k_l], axis=0),
                )
                dq[pl.ds(at, L)] = heads_sum(o) * scale
                q_h = per_head(qh[s, pl.ds(at, L)])
                q_l = per_head(ql[s, pl.ds(at, L)])
                t_h, t_l = split(ds.T)
                dkv[pl.ds(at, 4 * L), :ch] += dot(
                    lanes_cat(t_h, t_l, t_h),
                    jnp.concatenate([q_h, q_h, q_l], axis=0),
                )
                t_h, t_l = split(probs[s, col].T)
                d_h = per_head(dbh[pl.ds(at, L)])
                d_l = per_head(dbl[pl.ds(at, L)])
                dkv[pl.ds(at, 4 * L), ch:] += dot(
                    lanes_cat(t_h, t_l, t_h),
                    jnp.concatenate([d_h, d_h, d_l], axis=0),
                )
            return c

        lax.fori_loop(0, W // group, attend_back, 0)
        zeros = jnp.zeros((L, ch), f32)
        d_all = lanes_cat(
            jnp.concatenate([zeros, dq[...], zeros], axis=0), dkv[:R1]
        )
        d_h, d_l = split(d_all)
        part = dot(lanes_cat(d_h, d_l, d_h), wqt3[...])
        dh2[...] = part + jnp.concatenate([zeros, grad3, zeros], axis=0)
        sb[s, 0, : 2 * L] = dh2[: 2 * L]
        sb[s, 0, 2 * L :] = gk[s, :L]
        sb[s, 1, : 2 * L] = dh2[R:]
        sb[s, 1, 2 * L :] = gk[s, R - L :]
        edges = [
            side_copy(hb + 3, side, sb.at[s, side], rb.at[s, side])
            for side in range(2)
        ]
        for e in edges:
            e.start()
        wide = rows_product(h2h[s], h2l[s], d_h, d_l)
        for k in range(3):
            at = qkv_base + k * ch
            gw[at : at + ch] += wide[:, k * ch : (k + 1) * ch]
        for e in edges:
            e.wait()
        dh2[: 2 * L] += rb[s, 1, : 2 * L]
        dh2[R:] += rb[s, 0, : 2 * L]

        t_h, t_l = lat_triple(dh2[...])
        grad_act = conv_back(t_h, t_l, R, w3t[2])
        sums, direct = norm_back(
            s, 1, h1[s, 2 * L : 2 * L + R], grad_act, dg2[s], dh2[L : L + R]
        )
        sum_start(s * 4 + 2, sums)
        de1[s, 2 * L : 2 * L + R] = direct
        halo_start(hb + 4, de1, s, 1)
        add_conv_grad(
            conv_base + 9 * ch,
            a2h[s, L : L + R1],
            a2l[s, L : L + R1],
            t_h[L : L + R],
            t_l[L : L + R],
        )
        sums = sum_wait(s * 4 + 2)
        halo_wait(hb + 4, de1, s, 1)
        grad1 = norm_rest(
            s, 1, h1[s, L : L + R1], mask[L : L + R1], de1[s, L : L + R1], sums
        )
        t_h, t_l = lat_triple(grad1)
        grad_act = conv_back(t_h, t_l, R, w3t[1])
        sums, direct = norm_back(
            s, 0, h0[s, 2 * L : 2 * L + R], grad_act, dg1[s], grad1[L : L + R]
        )
        sum_start(s * 4 + 3, sums)
        de0[s, 2 * L : 2 * L + R] = direct
        halo_start(hb + 5, de0, s, 2)
        add_conv_grad(
            conv_base, a1h[s], a1l[s], t_h[L : L + R], t_l[L : L + R]
        )
        sums = sum_wait(s * 4 + 3)
        halo_wait(hb + 5, de0, s, 2)
        grad0 = norm_rest(s, 0, h0[s], mask[...], de0[s], sums)
        bias_acc[0:1] += jnp.sum(grad0[2 * L : 2 * L + R], axis=0, keepdims=True)
        t_h, t_l = lat_triple(grad0)
        add_conv_grad(
            lift_base, xh[s], xl[s], t_h[2 * L : 2 * L + R], t_l[2 * L : 2 * L + R]
        )
        dx = conv_back(t_h, t_l, R1, w3t[0])
        lane = lane_of(R)
        own = dx[L : L + R]
        lon = 0.5 * (dx[2 * L :] - dx[:R])
        g = gk[s]
        g_lon = jnp.concatenate([g[L:], rb[s, 0, 2 * L :]], axis=0)
        g_lon = 0.5 * (
            g_lon - jnp.concatenate([rb[s, 1, 2 * L :], g[: R - L]], axis=0)
        )
        dflux = jnp.where(
            lane < VARS, lat_diff(g), jnp.where(lane < 2 * VARS, g_lon, 0.0)
        )
        y = ys[s, 2 * L : 2 * L + R]
        parts = jnp.where(
            lane < VARS,
            own,
            jnp.where(lane < 2 * VARS, -lat_diff(own), -lon),
        )
        parts = parts + dflux * lroll(y, -3 * VARS)
        parts = jnp.where(lane < 3 * VARS, parts, 0.0)
        fields_grad = (
            parts
            + lroll(parts, VARS)
            + lroll(parts, 2 * VARS)
            + lroll(parts, -VARS)
            + lroll(parts, -2 * VARS)
        )
        velocity_grad = own + lroll(dflux * y, 3 * VARS)
        gy = jnp.where(
            lane < 3 * VARS,
            fields_grad,
            jnp.where(lane < 5 * VARS, velocity_grad, 0.0),
        )
        grad_ref[...] += gy

        @pl.when(s > 0)
        def _():
            factor = jnp.where(s == SECTIONS - 1, 1.0, 0.5) * step_size
            gk[s - 1] = gk[s - 1] + factor * gy

        return carry

    lax.fori_loop(0, SECTIONS, backward, 0)

    gw[ch - 28 : ch - 27] = bias_acc[0:1]
    gw[ch - 27 : ch - 26] = bias_acc[1:2]
    norm_out[...] = norm_acc[...]

    stages = []
    step = 1
    for n in factors(nl):
        idx = lax.rem(me_l // step, n)

        def at(k, idx=idx, n=n, step=step):
            q = lax.rem(idx + k, n)
            return q, (me_l + (q - idx) * step, me_b)

        stages.append((n, idx, at))
        step *= n
    step = 1
    for n in factors(nb):
        idx = lax.rem(me_b // step, n)

        def at(k, idx=idx, n=n, step=step):
            q = lax.rem(idx + k, n)
            return q, (me_l, me_b + (q - idx) * step)

        stages.append((n, idx, at))
        step *= n
    size = gw.shape[0]
    off = 0
    slot = 0
    regions = []
    for t, (n, idx, at) in enumerate(stages):
        part = size // n
        for k in range(1, n):
            q, device = at(k)
            pltpu.make_async_remote_copy(
                gw.at[pl.ds(pl.multiple_of(off + q * part, 8), part)],
                rsb.at[pl.ds(slot + (n - 1 - k) * part, part)],
                rs_send.at[t],
                rs_recv.at[t],
                device_id=device,
                device_id_type=MESH,
            ).start()
        got = rsb.at[pl.ds(slot, (n - 1) * part)]
        pltpu.make_async_copy(got, got, rs_recv.at[t]).wait()
        pltpu.make_async_copy(got, got, rs_send.at[t]).wait()
        regions.append((off, size, part))
        off = off + idx * part
        chunk = math.gcd(part, 256)

        def add(i, c, off=off, slot=slot, n=n, part=part, chunk=chunk):
            at_row = pl.multiple_of(i * chunk, 8)
            total = gw[pl.ds(pl.multiple_of(off + at_row, 8), chunk)]
            for k in range(n - 1):
                total = total + rsb[
                    pl.ds(pl.multiple_of(slot + k * part + at_row, 8), chunk)
                ]
            gw[pl.ds(pl.multiple_of(off + at_row, 8), chunk)] = total
            return c

        lax.fori_loop(0, part // chunk, add, 0)
        slot += (n - 1) * part
        size = part
    weights_out[pl.ds(pl.multiple_of(off, 8), size)] = gw[
        pl.ds(pl.multiple_of(off, 8), size)
    ]
    for t in reversed(range(len(stages))):
        n, idx, at = stages[t]
        base, _, part = regions[t]
        mine = weights_out.at[pl.ds(pl.multiple_of(base + idx * part, 8), part)]
        for k in range(1, n):
            pltpu.make_async_remote_copy(
                mine,
                mine,
                ag_send.at[t],
                ag_recv.at[t],
                device_id=at(k)[1],
                device_id_type=MESH,
            ).start()
        got = rsb.at[pl.ds(0, (n - 1) * part)]
        pltpu.make_async_copy(got, got, ag_recv.at[t]).wait()
        pltpu.make_async_copy(got, got, ag_send.at[t]).wait()


def on_device(
    nl,
    nb,
    fields,
    velocity,
    context,
    masks,
    window,
    lift_weight,
    lift_bias,
    norm_gain,
    norm_shift,
    conv_weight,
    attn_qkv,
    attn_out,
    head_weight,
    head_bias,
    cot_fields,
    cot_velocity,
):
    _, L, W, _ = fields.shape
    R, R1, R2 = L * W, L * (W + 2), L * (W + 4)
    ch = LANES
    nd = nl * nb
    grid = (L, W)
    used = 3 * VARS + 2 * VARS + context.shape[-1]
    start = jnp.concatenate(
        [
            fields[0],
            fields[0],
            fields[0],
            velocity[0],
            context[0],
            jnp.zeros((*grid, MASK_LANE - used), f32),
            masks[0].astype(f32)[..., None],
            cot_fields[0],
            cot_fields[0],
            cot_fields[0],
            cot_velocity[0],
            jnp.zeros((*grid, ch - 5 * VARS), f32),
        ],
        axis=-1,
    )
    start = start.transpose(1, 0, 2).reshape(R, 2 * ch)
    keys = window.transpose(1, 0, 2).reshape(R, window.shape[-1])
    side = ((0, 0), (3 * VARS, ch - 5 * VARS))
    small = jnp.concatenate(
        [
            lift_bias[None],
            jnp.pad(head_bias[None], side),
            norm_gain,
            norm_shift,
            jnp.zeros((2, ch), f32),
        ],
        axis=0,
    )
    head = jnp.pad(head_weight, side)
    S = SECTIONS
    rows = 32 * ch
    rows = -(-rows // (8 * nd)) * 8 * nd
    stage_count = len(factors(nl)) + len(factors(nb))
    vm = pltpu.VMEM
    dma = pltpu.SemaphoreType.DMA
    scratch = [
        vm((S, R2, ch), f32),
        vm((S, R1, ch), bf16),
        vm((S, R1, ch), bf16),
        vm((S, R2, ch), f32),
        vm((S, R2, ch), f32),
        vm((S, R1, ch), bf16),
        vm((S, R1, ch), bf16),
        vm((S, R2, ch), bf16),
        vm((S, R2, ch), bf16),
        vm((S, R, ch), f32),
        vm((S, R, ch), f32),
        vm((S, R1, ch), bf16),
        vm((S, R1, ch), bf16),
        vm((S, R, ch), bf16),
        vm((S, R, ch), bf16),
        vm((S, R1 + L, ch), bf16),
        vm((S, R1 + L, ch), bf16),
        vm((S, R1 + L, ch), bf16),
        vm((S, R1 + L, ch), bf16),
        vm((S, W, HEADS * L, ch), f32),
        vm((S, R, ch), bf16),
        vm((S, R, ch), bf16),
        vm((S, R, ch), bf16),
        vm((S, R, ch), bf16),
        vm((S, 2, 8, ch), f32),
        vm((S, R, ch), f32),
        vm((R, ch), f32),
        vm((R, ch), f32),
        vm((R2, ch), f32),
        vm((W, L, ch), f32),
        vm((3, 9 * ch, 3 * ch), bf16),
        vm((3, 9 * ch, 3 * ch), bf16),
        vm((3 * ch, 3 * ch), bf16),
        vm((9 * ch, ch), bf16),
        vm((3 * ch, ch), bf16),
        vm((3 * ch, ch), bf16),
        vm((3 * ch, ch), bf16),
        vm((3 * ch, ch), bf16),
        vm((ch, ch), f32),
        vm((R, ch), f32),
        vm((R, ch), bf16),
        vm((R, ch), bf16),
        vm((R, ch), f32),
        vm((R1 + L, 2 * ch), f32),
        vm((R1, ch), f32),
        vm((S, R2, ch), f32),
        vm((S, R2, ch), f32),
        vm((S, 2, 3 * L, ch), f32),
        vm((S, 2, 3 * L, ch), f32),
        vm((rows, ch), f32),
        vm((rows, ch), f32),
        vm((2, 2, ch), f32),
        vm((2, ch), f32),
        vm((4 * S + 1, 2, ch), f32),
        vm((4 * S + 1, nd, 2, ch), f32),
        dma((4 * S + 1,)),
        dma((4 * S + 1,)),
        dma((6 * S, 2)),
        dma((6 * S, 2)),
        dma((stage_count,)),
        dma((stage_count,)),
        dma((stage_count,)),
        dma((stage_count,)),
    ]
    whole = pl.BlockSpec(memory_space=pltpu.VMEM)
    new, grad, weights, norm_grads = pl.pallas_call(
        partial(kernel, (nl, nb, L, W, HEADS)),
        out_shape=(
            jax.ShapeDtypeStruct((R, ch), f32),
            jax.ShapeDtypeStruct((R, ch), f32),
            jax.ShapeDtypeStruct((rows, ch), f32),
            jax.ShapeDtypeStruct((2, 2, ch), f32),
        ),
        in_specs=[whole] * 8,
        out_specs=(whole,) * 4,
        scratch_shapes=scratch,
        compiler_params=pltpu.CompilerParams(
            collective_id=0, has_side_effects=True, vmem_limit_bytes=60 * 2**20
        ),
    )(start, keys, small, lift_weight, conv_weight, attn_qkv, attn_out, head)

    def state(x):
        x = x.reshape(W, L, ch).transpose(1, 0, 2)[None]
        return x[..., :VARS], x[..., 3 * VARS : 5 * VARS]

    new_fields, new_velocity = state(new)
    grad_fields, grad_velocity = state(grad)
    cin = lift_weight.shape[2]
    vel = slice(3 * VARS, 5 * VARS)
    return (
        new_fields,
        new_velocity,
        grad_fields,
        grad_velocity,
        weights[: 9 * ch].reshape(3, 3, ch, ch)[:, :, :cin],
        weights[cin],
        norm_grads[:, 1],
        norm_grads[:, 0],
        weights[9 * ch : 27 * ch].reshape(2, 3, 3, ch, ch),
        weights[27 * ch : 30 * ch].reshape(3, ch, ch).transpose(1, 0, 2).reshape(ch, 3 * ch),
        weights[30 * ch : 31 * ch],
        weights[31 * ch : 32 * ch, vel],
        weights[cin + 1, vel],
    )


def solution(mesh):
    field = P("batch", None, "lon", None)
    return jax.shard_map(
        partial(on_device, mesh.shape["lon"], mesh.shape["batch"]),
        mesh=mesh,
        in_specs=(
            field,
            field,
            field,
            P("batch", None, "lon"),
            P(None, "lon", None),
            P(),
            P(),
            P(),
            P(),
            P(),
            P(),
            P(),
            P(),
            P(),
            field,
            field,
        ),
        out_specs=(field,) * 4 + (P(),) * 9,
        check_vma=False,
    )
```

```python
from functools import partial
import math

import jax
import jax.numpy as jnp
from jax import lax
from jax.experimental import pallas as pl
from jax.experimental.pallas import tpu as pltpu
from jax.sharding import PartitionSpec as P

HEADS = 4
SECTIONS = 4
LANES = 128
VARS = 5
MASK_LANE = 127
epsilon = 1e-05
step_size = 0.25
f32 = jnp.float32
bf16 = jnp.bfloat16
MESH = pl.DeviceIdType.MESH


def split(x):
    hi = x.astype(bf16)
    return hi, (x - hi.astype(f32)).astype(bf16)


def dot(a, b, dims=((1,), (0,))):
    return lax.dot_general(a, b, (dims, ((), ())), preferred_element_type=f32)


def lanes_cat(*parts):
    return jnp.concatenate(parts, axis=1)


def factors(n):
    out = []
    while n > 4 and n % 2 == 0:
        out.append(2)
        n //= 2
    if n > 1:
        out.append(n)
    return out


def kernel(
    sizes,
    fields_in,
    velocity_in,
    cot_fields_in,
    cot_velocity_in,
    masks_in,
    context_in,
    window_in,
    lift_in,
    conv_in,
    qkv_in,
    out_in,
    head_in,
    lift_bias_ref,
    head_bias_ref,
    gain_ref,
    shift_ref,
    all_out,
    ys,
    xh,
    xl,
    h0,
    h1,
    a1h,
    a1l,
    a2h,
    a2l,
    dg1,
    dg2,
    h2h,
    h2l,
    qh,
    ql,
    kh,
    kl,
    vh,
    vl,
    probs,
    bh,
    bl,
    h3h,
    h3l,
    norms,
    gk,
    acc,
    tend,
    mask,
    mult,
    w3f,
    w3t,
    wq3,
    wqt3,
    wo3,
    wot3,
    wh3,
    wht3,
    tap,
    blend,
    dbh,
    dbl,
    dqkv,
    dh2,
    h2,
    count,
    de1,
    de0,
    sb,
    rb,
    gw,
    rsb,
    norm_acc,
    bias_acc,
    planes,
    mask_plane,
    context_ref,
    window_ref,
    lift_ref,
    conv_ref,
    qkv_ref,
    out_ref,
    head_ref,
    head_bias_row,
    grad_ref,
    load_sems,
    ar_src,
    ar_buf,
    ar_send,
    ar_recv,
    halo_send,
    halo_recv,
    rs_send,
    rs_recv,
    ag_send,
    ag_recv,
):
    nl, nb, L, W, hid_heads = sizes
    nd = nl * nb
    R = L * W
    R1 = R + 2 * L
    R2 = R + 4 * L
    ch = LANES
    me_l = lax.axis_index("lon")
    me_b = lax.axis_index("batch")
    me = me_l * nb + me_b
    left = (lax.rem(me_l + nl - 1, nl), me_b)
    right = (lax.rem(me_l + 1, nl), me_b)

    def peer(k):
        t = lax.rem(me + k, nd)
        return (t // nb, lax.rem(t, nb))

    low_half = 1 - me_b // max(nb // 2, 1) if nb > 1 else 0
    lon_order = sorted(range(nl), key=lambda hop: -min(hop, nl - hop))
    barrier = pltpu.get_barrier_semaphore()

    def greet(k, c):
        pl.semaphore_signal(barrier, inc=1, device_id=peer(k), device_id_type=MESH)
        return c

    lax.fori_loop(1, nd, greet, 0)

    def sum_start(a, vals):
        ar_src[a] = vals
        ar_buf[a, me] = vals

        def send(k, c):
            to_b = k + low_half * (nb - 1 - 2 * k)
            for hop in lon_order:
                copy = pltpu.make_async_remote_copy(
                    ar_src.at[a],
                    ar_buf.at[a, me],
                    ar_send.at[a],
                    ar_recv.at[a],
                    device_id=(lax.rem(me_l + hop, nl), to_b),
                    device_id_type=MESH,
                )
                if hop == 0:
                    pl.when(to_b != me_b)(copy.start)
                else:
                    copy.start()
            return c

        lax.fori_loop(0, nb, send, 0)

    def sum_wait(a):
        got = ar_buf.at[a, pl.ds(0, nd - 1)]
        pltpu.make_async_copy(got, got, ar_recv.at[a]).wait()
        pltpu.make_async_copy(got, got, ar_send.at[a]).wait()
        return jnp.sum(ar_buf[a], axis=0)

    def side_copy(h, side, src, dst):
        return pltpu.make_async_remote_copy(
            src,
            dst,
            halo_send.at[h, side],
            halo_recv.at[h, side],
            device_id=left if side == 0 else right,
            device_id_type=MESH,
        )

    def halo_copies(h, buf, s, cols):
        n = cols * L
        lo = 2 * L - n
        to_left = side_copy(
            h, 0, buf.at[s, pl.ds(2 * L, n)], buf.at[s, pl.ds(R + 2 * L, n)]
        )
        to_right = side_copy(
            h, 1, buf.at[s, pl.ds(R + 2 * L - n, n)], buf.at[s, pl.ds(lo, n)]
        )
        return to_left, to_right

    def halo_start(h, buf, s, cols):
        for c in halo_copies(h, buf, s, cols):
            c.start()

    def halo_wait(h, buf, s, cols):
        for c in halo_copies(h, buf, s, cols):
            c.wait()

    def lat_of(n):
        return lax.broadcasted_iota(jnp.int32, (n, LANES), 0) % L

    def north(x):
        n = x.shape[0]
        return jnp.where(lat_of(n) == L - 1, 0.0, pltpu.roll(x, n - 1, 0))

    def south(x):
        n = x.shape[0]
        return jnp.where(lat_of(n) == 0, 0.0, pltpu.roll(x, 1, 0))

    def lat_diff(x):
        return 0.5 * (north(x) - south(x))

    def lane_of(n):
        return lax.broadcasted_iota(jnp.int32, (n, LANES), 1)

    def lroll(x, shift):
        return pltpu.roll(x, shift % LANES, 1)

    def conv(hi, lo, base, n, weights):
        cols_h = [hi[base + j * L : base + j * L + n] for j in range(3)]
        cols_l = [lo[base + j * L : base + j * L + n] for j in range(3)]
        wide = dot(lanes_cat(*cols_h, *cols_l, *cols_h), weights)
        return (
            wide[:, ch : 2 * ch]
            + south(wide[:, :ch])
            + north(wide[:, 2 * ch :])
        )

    def product(x, weights):
        hi, lo = split(x)
        return dot(lanes_cat(hi, lo, hi), weights)

    def rows_product(ah, al, gh, gl):
        t = ((0,), (0,))
        return dot(ah, gh, t) + dot(ah, gl, t) + dot(al, gh, t)

    def lat_triple(x):
        return split(lanes_cat(north(x), x, south(x)))

    def conv_back(gh, gl, n, weights):
        wide = dot(lanes_cat(gh, gl, gh), weights)
        return (
            wide[2 * L : 2 * L + n, :ch]
            + wide[L : L + n, ch : 2 * ch]
            + wide[:n, 2 * ch :]
        )

    def add_conv_grad(base, ah, al, gh, gl):
        for j in range(3):
            part = rows_product(
                ah[j * L : j * L + R], al[j * L : j * L + R], gh, gl
            )
            for i in range(3):
                at = base + (i * 3 + j) * ch
                gw[at : at + ch, :] += part[:, i * ch : (i + 1) * ch]

    lift_base, conv_base = 0, 9 * ch
    qkv_base = 27 * ch
    out_base, head_base = 30 * ch, 31 * ch

    at_f, at_v, at_cf, at_cv, at_m = (
        k * VARS for k in (0, 1, 3, 4, 6)
    )
    loads = [
        (fields_in, planes.at[at_f * W : at_v * W]),
        (velocity_in, planes.at[at_v * W : at_cf * W]),
        (cot_fields_in, planes.at[at_cf * W : at_cv * W]),
        (cot_velocity_in, planes.at[at_cv * W : at_m * W]),
        (masks_in, mask_plane),
        (context_in, context_ref),
        (lift_in, lift_ref),
        (conv_in, conv_ref),
        (qkv_in, qkv_ref),
        (out_in, out_ref),
        (head_in, head_ref),
        (window_in, window_ref),
    ]
    loads = [
        pltpu.make_async_copy(src, dst, load_sems.at[k])
        for k, (src, dst) in enumerate(loads)
    ]
    for load in loads:
        load.start()
    planes[(at_m + 1) * W :] = jnp.zeros((W, L), f32)
    for load in loads[:6]:
        load.wait()
    planes[at_m * W : (at_m + 1) * W] = mask_plane[...].astype(f32)
    cots = []
    masks_own = []
    for col in range(W):
        at = 2 * L + col * L
        x = planes[pl.ds(col, at_m + 2, stride=W), :].T
        ys[0, at : at + L] = jnp.zeros((L, ch), f32)
        for k in range(3):
            ys[0, at : at + L, k * VARS : (k + 1) * VARS] = x[:, at_f:at_v]
            gk[0, at - 2 * L : at - L, k * VARS : (k + 1) * VARS] = x[:, at_cf:at_cv]
        ys[0, at : at + L, 3 * VARS : 5 * VARS] = x[:, at_v:at_cf]
        gk[0, at - 2 * L : at - L, 3 * VARS : 5 * VARS] = x[:, at_cv:at_m]
        gk[0, at - 2 * L : at - L, 5 * VARS :] = jnp.zeros((L, ch - 5 * VARS), f32)
        ys[0, at : at + L, 5 * VARS : 5 * VARS + context_ref.shape[1]] = context_ref[
            pl.ds(col, L, stride=W), :
        ]
        ys[0, at : at + L, MASK_LANE:] = x[:, at_m : at_m + 1]
    cot = gk[0]
    mask_own = jnp.broadcast_to(
        ys[0, 2 * L : 2 * L + R, MASK_LANE : MASK_LANE + 1], (R, LANES)
    )
    count_part = jnp.sum(mask_own, axis=0, keepdims=True)
    for load in loads[6:8]:
        load.wait()

    tap[...] = jnp.zeros_like(tap)
    for b in range(3):
        for i in range(3):
            for j in range(3):
                if b == 0:
                    tap[: lift_ref.shape[2]] = lift_ref[i, j]
                    w = tap[...]
                else:
                    w = conv_ref[b - 1, i, j]
                hi, lo = split(w)
                for p, part in enumerate((hi, hi, lo)):
                    at = (p * 3 + j) * ch
                    w3f[b, at : at + ch, i * ch : (i + 1) * ch] = part
                hi, lo = split(w.T)
                for p, part in enumerate((hi, hi, lo)):
                    at = (p * 3 + i) * ch
                    w3t[b, at : at + ch, j * ch : (j + 1) * ch] = part

    pl.semaphore_wait(barrier, nd - 1)
    halo_start(0, ys, 0, 2)
    sum_start(4 * SECTIONS, jnp.concatenate([count_part, count_part], axis=0))

    def put_three(target, w):
        n = w.shape[0]
        hi, lo = split(w)
        target[:n] = hi
        target[n : 2 * n] = hi
        target[2 * n :] = lo

    for load in loads[8:]:
        load.wait()
    put_three(wq3, qkv_ref[...])
    put_three(wqt3, qkv_ref[...].T)
    put_three(wo3, out_ref[...])
    put_three(wot3, out_ref[...].T)
    tap[...] = jnp.zeros_like(tap)
    tap[3 * VARS : 5 * VARS] = head_ref[...]
    put_three(wht3, tap[...])
    put_three(wh3, tap[...].T)
    head_bias_row[...] = jnp.zeros_like(head_bias_row)
    head_bias_row[:, 3 * VARS : 5 * VARS] = head_bias_ref[...]
    for s, weight in enumerate((1.0, 2.0, 2.0, 1.0)):
        gk[s] = cot * (weight * step_size / 6.0)
    grad_ref[...] = cot
    acc[...] = jnp.zeros_like(acc)
    gw[...] = jnp.zeros_like(gw)
    norm_acc[...] = jnp.zeros_like(norm_acc)
    bias_acc[...] = jnp.zeros_like(bias_acc)

    pair = 2 * L
    shape = (2 * pair, HEADS * pair)
    key_of = lax.broadcasted_iota(jnp.int32, shape, 0)
    key_of = key_of - lax.broadcasted_iota(jnp.int32, shape, 1) // L % 2 * L
    for p in range(W // 2):
        entries = lanes_cat(*[window_ref[2 * p], window_ref[2 * p + 1]] * HEADS)
        counted = jnp.zeros(shape, f32)
        for k in range(entries.shape[0]):
            counted = counted + jnp.where(entries[k : k + 1] == key_of, 1.0, 0.0)
        mult[p] = jnp.where(
            counted > 0.0, jnp.log(jnp.maximum(counted, 1.0)), -1e30
        )

    head_rows = lax.broadcasted_iota(jnp.int32, (HEADS * pair, ch), 0) // pair
    head_lanes = lax.broadcasted_iota(jnp.int32, (HEADS * pair, ch), 1) // (ch // HEADS)
    head_mask = jnp.where(head_rows == head_lanes, 1.0, 0.0)
    head_mask_h = head_mask.astype(bf16)
    scale = (ch // HEADS) ** -0.5

    def per_head(x):
        return jnp.concatenate([x] * HEADS, axis=0) * head_mask_h

    def heads_sum(x):
        x = x * head_mask
        return sum(x[h * pair : (h + 1) * pair] for h in range(1, HEADS)) + x[:pair]

    lift_bias = lift_bias_ref[...]
    head_bias = head_bias_row[...]
    gains = [gain_ref[0:1], gain_ref[1:2]]
    shifts = [shift_ref[0:1], shift_ref[1:2]]

    def stats(h):
        weighted = h * mask[2 * L : 2 * L + R]
        return jnp.concatenate(
            [
                jnp.sum(weighted, axis=0, keepdims=True),
                jnp.sum(weighted * h, axis=0, keepdims=True),
            ],
            axis=0,
        )

    def normalise(s, b, sums):
        total_count = count[0:1]
        average = sums[0:1] / total_count
        spread = sums[1:2] / total_count - average * average
        inverse = lax.rsqrt(spread + epsilon)
        norms[s, b, 0:1] = average
        norms[s, b, 1:2] = inverse
        return average, inverse

    def activity(h, b, average, inverse):
        z = (h - average) * inverse * gains[b] + shifts[b]
        below = 0.5 * (1.0 + lax.erf(z * (0.5**0.5)))
        slope = below + z * (
            jnp.exp(-0.5 * z * z) * (1.0 / math.sqrt(2.0 * math.pi))
        )
        return z * below, slope

    group = 2

    def forward(s, carry):
        hb = s * 6

        halo_wait(hb, ys, s, 2)

        @pl.when(s == 0)
        def _():
            mask[...] = jnp.broadcast_to(
                ys[0, :, MASK_LANE : MASK_LANE + 1], (R2, LANES)
            )

        y1 = ys[s, L : L + R1]
        lane = lane_of(R1)
        lon = 0.5 * (ys[s, 2 * L : 2 * L + R1] - ys[s, 0:R1])
        x = jnp.where(
            (lane >= VARS) & (lane < 2 * VARS),
            lat_diff(y1),
            jnp.where((lane >= 2 * VARS) & (lane < 3 * VARS), lon, y1),
        )
        hi, lo = split(x)
        xh[s] = hi
        xl[s] = lo
        first = conv(xh.at[s], xl.at[s], 0, R, w3f[0]) + lift_bias
        h0[s, 2 * L : 2 * L + R] = first
        sum_start(s * 4, stats(first))
        halo_start(hb + 1, h0, s, 2)
        flux = y1 * lroll(y1, -3 * VARS)
        flux = jnp.where(lane < 2 * VARS, flux, 0.0)
        own_lane = lane_of(R)
        t_lat = jnp.where(own_lane < VARS, lat_diff(flux[L : L + R]), 0.0)
        t_lon = jnp.where(
            own_lane >= VARS, 0.5 * (flux[2 * L : 2 * L + R] - flux[:R]), 0.0
        )
        t = -(t_lat + lroll(t_lon, -VARS))
        tend[...] = t + lroll(t, VARS) + lroll(t, 2 * VARS)


        @pl.when(s == 0)
        def _():
            count[...] = sum_wait(4 * SECTIONS)

        average, inverse = normalise(s, 0, sum_wait(s * 4))
        halo_wait(hb + 1, h0, s, 2)
        act, slope = activity(h0[s, L : L + R1], 0, average, inverse)
        dg1[s] = slope[L : L + R]
        hi, lo = split(act)
        a1h[s] = hi
        a1l[s] = lo
        second = h0[s, 2 * L : 2 * L + R] + conv(a1h.at[s], a1l.at[s], 0, R, w3f[1])
        h1[s, 2 * L : 2 * L + R] = second
        sum_start(s * 4 + 1, stats(second))
        halo_start(hb + 2, h1, s, 2)
        average, inverse = normalise(s, 1, sum_wait(s * 4 + 1))
        halo_wait(hb + 2, h1, s, 2)
        act, slope = activity(h1[s], 1, average, inverse)
        dg2[s] = slope[2 * L : 2 * L + R]
        hi, lo = split(act)
        a2h[s] = hi
        a2l[s] = lo
        third = h1[s, L : L + R1] + conv(a2h.at[s], a2l.at[s], 0, R1, w3f[2])
        h2[...] = third
        hi, lo = split(third)
        h2h[s] = hi
        h2l[s] = lo
        mixing = dot(lanes_cat(hi, lo, hi), wq3[...])
        hi, lo = split(mixing[L : L + R, :ch] * scale)
        qh[s] = hi
        ql[s] = lo
        hi, lo = split(mixing[:, ch : 2 * ch])
        kh[s] = hi
        kl[s] = lo
        hi, lo = split(mixing[:, 2 * ch :])
        vh[s] = hi
        vl[s] = lo

        def attend(pairs):
            scores = []
            for p in pairs:
                at = pl.multiple_of(p * pair, pair)
                q_h = per_head(qh[s, pl.ds(at, pair)])
                q_l = per_head(ql[s, pl.ds(at, pair)])
                k_h = kh[s, pl.ds(at, 2 * pair)]
                k_l = kl[s, pl.ds(at, 2 * pair)]
                scores.append(
                    dot(
                        lanes_cat(k_h, k_l, k_h),
                        lanes_cat(q_h, q_h, q_l),
                        ((1,), (1,)),
                    )
                )
            weights = []
            for p, score in zip(pairs, scores):
                score = score + mult[p]
                e = jnp.exp(score - jnp.max(score, axis=0, keepdims=True))
                e = e * (1.0 / jnp.sum(e, axis=0, keepdims=True))
                probs[s, p] = e
                weights.append(e)
            for p, e in zip(pairs, weights):
                at = pl.multiple_of(p * pair, pair)
                p_h, p_l = split(e.T)
                v_h = vh[s, pl.ds(at, 2 * pair)]
                v_l = vl[s, pl.ds(at, 2 * pair)]
                o = dot(
                    lanes_cat(p_h, p_l, p_h),
                    jnp.concatenate([v_h, v_h, v_l], axis=0),
                )
                blend[pl.ds(at, pair)] = heads_sum(o)

        weight = jnp.where((s == 0) | (s == SECTIONS - 1), 1.0, 2.0)
        factor = jnp.where(s == SECTIONS - 2, 1.0, 0.5) * step_size

        def finish(ranges):
            def take(ref, base=0):
                return jnp.concatenate(
                    [ref[base + a : base + b] for a, b in ranges], axis=0
                )

            def give(ref, value, base=0):
                at = 0
                for a, b in ranges:
                    ref[base + a : base + b] = value[at : at + b - a]
                    at += b - a

            hi, lo = split(take(blend))
            give(bh.at[s], hi)
            give(bl.at[s], lo)
            fourth = take(h2, L) + dot(lanes_cat(hi, lo, hi), wo3[...])
            hi, lo = split(fourth)
            give(h3h.at[s], hi)
            give(h3l.at[s], lo)
            slope_now = (
                take(tend) + dot(lanes_cat(hi, lo, hi), wh3[...]) + head_bias
            )
            give(acc, take(acc) + weight * slope_now)

            @pl.when(s < SECTIONS - 1)
            def _():
                give(
                    ys.at[s + 1],
                    take(ys.at[0], 2 * L) + factor * slope_now,
                    2 * L,
                )

        last = W // 2 - 1
        attend([0, last])
        finish([(0, pair), (R - pair, R)])

        @pl.when(s < SECTIONS - 1)
        def _():
            halo_start(hb + 6, ys, s + 1, 2)

        def inner(k, c):
            attend([1 + group * k + m for m in range(group)])
            return c

        lax.fori_loop(0, (last - 1) // group, inner, 0)
        finish([(pair, R - pair)])
        return carry

    lax.fori_loop(0, SECTIONS, forward, 0)
    acc[...] = ys[0, 2 * L : 2 * L + R] + (step_size / 6.0) * acc[...]

    def norm_back(s, b, h, grad_act, slope, through):
        average = norms[s, b, 0:1]
        inverse = norms[s, b, 1:2]
        dz = grad_act * slope
        hat = (h - average) * inverse
        sums = jnp.concatenate(
            [
                jnp.sum(dz, axis=0, keepdims=True),
                jnp.sum(dz * hat, axis=0, keepdims=True),
            ],
            axis=0,
        )
        return sums, through + dz * (gains[b] * inverse)

    def norm_rest(s, b, h, weight_mask, direct, sums):
        average = norms[s, b, 0:1]
        inverse = norms[s, b, 1:2]
        hat = (h - average) * inverse
        norm_acc[b] += sums
        return direct - weight_mask * (
            gains[b] * inverse / count[0:1]
        ) * (sums[0:1] + hat * sums[1:2])

    def backward(turn, carry):
        s = SECTIONS - 1 - turn
        hb = s * 6
        g = gk[s]
        g_h, g_l = split(g)
        grad3 = dot(lanes_cat(g_h, g_l, g_h), wht3[...])
        grad3_h, grad3_l = split(grad3)
        hi, lo = split(dot(lanes_cat(grad3_h, grad3_l, grad3_h), wot3[...]))
        dbh[...] = hi
        dbl[...] = lo
        dqkv[...] = jnp.zeros_like(dqkv)

        def attend_back(pairs):
            dps = []
            for p in pairs:
                at = pl.multiple_of(p * pair, pair)
                d_h = per_head(dbh[pl.ds(at, pair)])
                d_l = per_head(dbl[pl.ds(at, pair)])
                v_h = vh[s, pl.ds(at, 2 * pair)]
                v_l = vl[s, pl.ds(at, 2 * pair)]
                dps.append(
                    dot(
                        lanes_cat(v_h, v_l, v_h),
                        lanes_cat(d_h, d_h, d_l),
                        ((1,), (1,)),
                    )
                )
            dss = []
            for p, dp in zip(pairs, dps):
                e = probs[s, p]
                dss.append(e * (dp - jnp.sum(e * dp, axis=0, keepdims=True)))
            for p, ds in zip(pairs, dss):
                at = pl.multiple_of(p * pair, pair)
                k_h = kh[s, pl.ds(at, 2 * pair)]
                k_l = kl[s, pl.ds(at, 2 * pair)]
                t_h, t_l = split(ds.T)
                o = dot(
                    lanes_cat(t_h, t_l, t_h),
                    jnp.concatenate([k_h, k_h, k_l], axis=0),
                )
                dqkv[pl.ds(at + L, pair), :ch] = heads_sum(o) * scale
                q_h = per_head(qh[s, pl.ds(at, pair)])
                q_l = per_head(ql[s, pl.ds(at, pair)])
                s_h, s_l = split(ds)
                o = dot(s_h, lanes_cat(q_h, q_l))
                o = o[:, :ch] + o[:, ch:] + dot(s_l, q_h)
                dqkv[pl.ds(at, 2 * pair), ch : 2 * ch] += o
                d_h = per_head(dbh[pl.ds(at, pair)])
                d_l = per_head(dbl[pl.ds(at, pair)])
                s_h, s_l = split(probs[s, p])
                o = dot(s_h, lanes_cat(d_h, d_l))
                o = o[:, :ch] + o[:, ch:] + dot(s_l, d_h)
                dqkv[pl.ds(at, 2 * pair), 2 * ch :] += o

        last = W // 2 - 1
        attend_back([0, last])
        edge_h, edge_l = split(
            jnp.concatenate([dqkv[:pair], dqkv[R1 - pair :]], axis=0)
        )
        part = dot(lanes_cat(edge_h, edge_l, edge_h), wqt3[...])
        zeros = jnp.zeros((L, ch), f32)
        part = part + jnp.concatenate(
            [zeros, grad3[:L], grad3[R - L :], zeros], axis=0
        )
        dh2[:pair] = part[:pair]
        dh2[R1 - pair :] = part[pair:]
        sb[s, 0, :pair] = part[:pair]
        sb[s, 0, pair:] = gk[s, :L]
        sb[s, 1, :pair] = part[pair:]
        sb[s, 1, pair:] = gk[s, R - L :]
        edges = [
            side_copy(hb + 3, side, sb.at[s, side], rb.at[s, side])
            for side in range(2)
        ]
        for e in edges:
            e.start()

        def inner(k, c):
            attend_back([1 + group * k + m for m in range(group)])
            return c

        lax.fori_loop(0, (last - 1) // group, inner, 0)
        d_h, d_l = split(dqkv[...])
        mid_h, mid_l = d_h[pair : R1 - pair], d_l[pair : R1 - pair]
        dh2[pair : R1 - pair] = grad3[L : R - L] + dot(
            lanes_cat(mid_h, mid_l, mid_h), wqt3[...]
        )
        for e in edges:
            e.wait()
        dh2[:pair] += rb[s, 1, :pair]
        dh2[R1 - pair :] += rb[s, 0, :pair]

        t_h, t_l = lat_triple(dh2[...])
        grad_act = conv_back(t_h, t_l, R, w3t[2])
        sums, direct = norm_back(
            s, 1, h1[s, 2 * L : 2 * L + R], grad_act, dg2[s], dh2[L : L + R]
        )
        sum_start(s * 4 + 2, sums)
        de1[s, 2 * L : 2 * L + R] = direct
        halo_start(hb + 4, de1, s, 1)
        bias_acc[1:2] += jnp.sum(g, axis=0, keepdims=True)
        gw[head_base : head_base + ch] += rows_product(h3h[s], h3l[s], g_h, g_l)
        gw[out_base : out_base + ch] += rows_product(bh[s], bl[s], grad3_h, grad3_l)
        wide = rows_product(h2h[s], h2l[s], d_h, d_l)
        for k in range(3):
            at = qkv_base + k * ch
            gw[at : at + ch] += wide[:, k * ch : (k + 1) * ch]
        add_conv_grad(
            conv_base + 9 * ch,
            a2h[s, L : L + R1],
            a2l[s, L : L + R1],
            t_h[L : L + R],
            t_l[L : L + R],
        )
        sums = sum_wait(s * 4 + 2)
        halo_wait(hb + 4, de1, s, 1)
        grad1 = norm_rest(
            s, 1, h1[s, L : L + R1], mask[L : L + R1], de1[s, L : L + R1], sums
        )
        t_h, t_l = lat_triple(grad1)
        grad_act = conv_back(t_h, t_l, R, w3t[1])
        sums, direct = norm_back(
            s, 0, h0[s, 2 * L : 2 * L + R], grad_act, dg1[s], grad1[L : L + R]
        )
        sum_start(s * 4 + 3, sums)
        de0[s, 2 * L : 2 * L + R] = direct
        halo_start(hb + 5, de0, s, 2)
        add_conv_grad(
            conv_base, a1h[s], a1l[s], t_h[L : L + R], t_l[L : L + R]
        )
        sums = sum_wait(s * 4 + 3)
        halo_wait(hb + 5, de0, s, 2)
        grad0 = norm_rest(s, 0, h0[s], mask[...], de0[s], sums)
        bias_acc[0:1] += jnp.sum(grad0[2 * L : 2 * L + R], axis=0, keepdims=True)
        t_h, t_l = lat_triple(grad0)
        add_conv_grad(
            lift_base, xh[s], xl[s], t_h[2 * L : 2 * L + R], t_l[2 * L : 2 * L + R]
        )
        dx = conv_back(t_h, t_l, R1, w3t[0])
        lane = lane_of(R)
        own = dx[L : L + R]
        lon = 0.5 * (dx[2 * L :] - dx[:R])
        g = gk[s]
        g_lon = jnp.concatenate([g[L:], rb[s, 0, 2 * L :]], axis=0)
        g_lon = 0.5 * (
            g_lon - jnp.concatenate([rb[s, 1, 2 * L :], g[: R - L]], axis=0)
        )
        dflux = jnp.where(
            lane < VARS, lat_diff(g), jnp.where(lane < 2 * VARS, g_lon, 0.0)
        )
        y = ys[s, 2 * L : 2 * L + R]
        parts = jnp.where(
            lane < VARS,
            own,
            jnp.where(lane < 2 * VARS, -lat_diff(own), -lon),
        )
        parts = parts + dflux * lroll(y, -3 * VARS)
        parts = jnp.where(lane < 3 * VARS, parts, 0.0)
        fields_grad = (
            parts
            + lroll(parts, VARS)
            + lroll(parts, 2 * VARS)
            + lroll(parts, -VARS)
            + lroll(parts, -2 * VARS)
        )
        velocity_grad = own + lroll(dflux * y, 3 * VARS)
        gy = jnp.where(
            lane < 3 * VARS,
            fields_grad,
            jnp.where(lane < 5 * VARS, velocity_grad, 0.0),
        )
        grad_ref[...] += gy

        @pl.when(s > 0)
        def _():
            factor = jnp.where(s == SECTIONS - 1, 1.0, 0.5) * step_size
            gk[s - 1] = gk[s - 1] + factor * gy

        return carry

    lax.fori_loop(0, SECTIONS, backward, 0)

    gw[ch - 28 : ch - 27] = bias_acc[0:1]
    gw[ch - 27 : ch - 26] = bias_acc[1:2]
    weights_out = all_out.at[: gw.shape[0]]
    all_out[gw.shape[0] : gw.shape[0] + 4] = norm_acc[...].reshape(4, ch)
    lane = lane_of(R)
    new, grad = acc[...], grad_ref[...]
    merged = jnp.where(
        lane < at_v,
        new,
        jnp.where(
            lane < at_cf,
            lroll(new, at_v - 3 * VARS),
            jnp.where(
                lane < at_cv, lroll(grad, at_cf), lroll(grad, at_cv - 3 * VARS)
            ),
        ),
    )
    for col in range(W):
        x = merged[col * L : (col + 1) * L].T
        all_out[pl.ds(gw.shape[0] + 8 + col, at_m, stride=W), :] = lanes_cat(
            x[:at_m], jnp.zeros((at_m, ch - L), f32)
        )

    stages = []
    step = 1
    for n in factors(nl):
        idx = lax.rem(me_l // step, n)

        def at(k, idx=idx, n=n, step=step):
            q = lax.rem(idx + k, n)
            return q, (me_l + (q - idx) * step, me_b)

        stages.append((n, idx, at))
        step *= n
    step = 1
    for n in factors(nb):
        idx = lax.rem(me_b // step, n)

        def at(k, idx=idx, n=n, step=step):
            q = lax.rem(idx + k, n)
            return q, (me_l, me_b + (q - idx) * step)

        stages.append((n, idx, at))
        step *= n
    size = gw.shape[0]
    off = 0
    slot = 0
    regions = []
    for t, (n, idx, at) in enumerate(stages):
        part = size // n
        for k in range(1, n):
            q, device = at(k)
            pltpu.make_async_remote_copy(
                gw.at[pl.ds(pl.multiple_of(off + q * part, 8), part)],
                rsb.at[pl.ds(slot + (n - 1 - k) * part, part)],
                rs_send.at[t],
                rs_recv.at[t],
                device_id=device,
                device_id_type=MESH,
            ).start()
        got = rsb.at[pl.ds(slot, (n - 1) * part)]
        pltpu.make_async_copy(got, got, rs_recv.at[t]).wait()
        pltpu.make_async_copy(got, got, rs_send.at[t]).wait()
        regions.append((off, size, part))
        off = off + idx * part
        chunk = math.gcd(part, 256)

        def add(i, c, off=off, slot=slot, n=n, part=part, chunk=chunk):
            at_row = pl.multiple_of(i * chunk, 8)
            total = gw[pl.ds(pl.multiple_of(off + at_row, 8), chunk)]
            for k in range(n - 1):
                total = total + rsb[
                    pl.ds(pl.multiple_of(slot + k * part + at_row, 8), chunk)
                ]
            gw[pl.ds(pl.multiple_of(off + at_row, 8), chunk)] = total
            return c

        lax.fori_loop(0, part // chunk, add, 0)
        slot += (n - 1) * part
        size = part
    weights_out[pl.ds(pl.multiple_of(off, 8), size)] = gw[
        pl.ds(pl.multiple_of(off, 8), size)
    ]
    for t in reversed(range(len(stages))):
        n, idx, at = stages[t]
        base, _, part = regions[t]
        mine = weights_out.at[pl.ds(pl.multiple_of(base + idx * part, 8), part)]
        for k in range(1, n):
            pltpu.make_async_remote_copy(
                mine,
                mine,
                ag_send.at[t],
                ag_recv.at[t],
                device_id=at(k)[1],
                device_id_type=MESH,
            ).start()
        got = rsb.at[pl.ds(0, (n - 1) * part)]
        pltpu.make_async_copy(got, got, ag_recv.at[t]).wait()
        pltpu.make_async_copy(got, got, ag_send.at[t]).wait()


def hand_out(rows, weights, *outs):
    fields = outs[:4]
    lift, lift_bias, gain, shift, conv, qkv, out, head, head_bias = outs[4:]
    ch = LANES
    at = rows + 8
    for ref in fields:
        ref[...] = weights[at : at + ref.shape[0], : ref.shape[1]]
        at += ref.shape[0]
    cin = lift.shape[2]
    vel = slice(3 * VARS, 5 * VARS)
    for i in range(3):
        for j in range(3):
            at = (i * 3 + j) * ch
            lift[i, j] = weights[at : at + cin]
            for b in range(2):
                at_conv = at + (b + 1) * 9 * ch
                conv[b, i, j] = weights[at_conv : at_conv + ch]
    lift_bias[...] = weights[cin : cin + 1]
    head_bias[...] = weights[cin + 1 : cin + 2, vel]
    for b in range(2):
        at = rows + 2 * b
        shift[b : b + 1] = weights[at : at + 1]
        gain[b : b + 1] = weights[at + 1 : at + 2]
    for k in range(3):
        at = (27 + k) * ch
        qkv[:, k * ch : (k + 1) * ch] = weights[at : at + ch]
    out[...] = weights[30 * ch : 31 * ch]
    head[...] = weights[31 * ch : 32 * ch].T[vel]


def on_device(
    nl,
    nb,
    fields,
    velocity,
    context,
    masks,
    window,
    lift_weight,
    lift_bias,
    norm_gain,
    norm_shift,
    conv_weight,
    attn_qkv,
    attn_out,
    head_weight,
    head_bias,
    cot_fields,
    cot_velocity,
):
    _, L, W, _ = fields.shape
    R, R1, R2 = L * W, L * (W + 2), L * (W + 4)
    ch = LANES
    nd = nl * nb

    def flat(x):
        return x[0].transpose(2, 1, 0).reshape(-1, L)

    S = SECTIONS
    rows = 32 * ch
    rows = -(-rows // (8 * nd)) * 8 * nd
    stage_count = len(factors(nl)) + len(factors(nb))
    vm = pltpu.VMEM
    dma = pltpu.SemaphoreType.DMA
    scratch = [
        vm((S, R2, ch), f32),
        vm((S, R1, ch), bf16),
        vm((S, R1, ch), bf16),
        vm((S, R2, ch), f32),
        vm((S, R2, ch), f32),
        vm((S, R1, ch), bf16),
        vm((S, R1, ch), bf16),
        vm((S, R2, ch), bf16),
        vm((S, R2, ch), bf16),
        vm((S, R, ch), f32),
        vm((S, R, ch), f32),
        vm((S, R1, ch), bf16),
        vm((S, R1, ch), bf16),
        vm((S, R, ch), bf16),
        vm((S, R, ch), bf16),
        vm((S, R1, ch), bf16),
        vm((S, R1, ch), bf16),
        vm((S, R1, ch), bf16),
        vm((S, R1, ch), bf16),
        vm((S, W // 2, 4 * L, 2 * HEADS * L), f32),
        vm((S, R, ch), bf16),
        vm((S, R, ch), bf16),
        vm((S, R, ch), bf16),
        vm((S, R, ch), bf16),
        vm((S, 2, 8, ch), f32),
        vm((S, R, ch), f32),
        vm((R, ch), f32),
        vm((R, ch), f32),
        vm((R2, ch), f32),
        vm((W // 2, 4 * L, 2 * HEADS * L), f32),
        vm((3, 9 * ch, 3 * ch), bf16),
        vm((3, 9 * ch, 3 * ch), bf16),
        vm((3 * ch, 3 * ch), bf16),
        vm((9 * ch, ch), bf16),
        vm((3 * ch, ch), bf16),
        vm((3 * ch, ch), bf16),
        vm((3 * ch, ch), bf16),
        vm((3 * ch, ch), bf16),
        vm((ch, ch), f32),
        vm((R, ch), f32),
        vm((R, ch), bf16),
        vm((R, ch), bf16),
        vm((R1, 3 * ch), f32),
        vm((R1, ch), f32),
        vm((R1, ch), f32),
        vm((2, ch), f32),
        vm((S, R2, ch), f32),
        vm((S, R2, ch), f32),
        vm((S, 2, 3 * L, ch), f32),
        vm((S, 2, 3 * L, ch), f32),
        vm((rows, ch), f32),
        vm((rows, ch), f32),
        vm((2, 2, ch), f32),
        vm((2, ch), f32),
        vm((32 * W, L), f32),
        vm((W, L), jnp.int32),
        vm((R, context.shape[-1]), f32),
        vm((W, window.shape[-1], L), jnp.int32),
        vm(lift_weight.shape, f32),
        vm(conv_weight.shape, f32),
        vm(attn_qkv.shape, f32),
        vm(attn_out.shape, f32),
        vm(head_weight.shape[::-1], f32),
        vm((1, ch), f32),
        vm((R, ch), f32),
        dma((12,)),
        vm((4 * S + 1, 2, ch), f32),
        vm((4 * S + 1, nd, 2, ch), f32),
        dma((4 * S + 1,)),
        dma((4 * S + 1,)),
        dma((6 * S, 2)),
        dma((6 * S, 2)),
        dma((stage_count,)),
        dma((stage_count,)),
        dma((stage_count,)),
        dma((stage_count,)),
    ]
    whole = pl.BlockSpec(memory_space=pltpu.VMEM)
    apart = pl.BlockSpec(memory_space=pl.ANY)
    results = pl.pallas_call(
        partial(kernel, (nl, nb, L, W, HEADS)),
        out_shape=jax.ShapeDtypeStruct((rows + 8 + 6 * VARS * W, ch), f32),
        in_specs=[apart] * 12 + [whole] * 4,
        out_specs=whole,
        scratch_shapes=scratch,
        compiler_params=pltpu.CompilerParams(
            collective_id=0, has_side_effects=True, vmem_limit_bytes=60 * 2**20
        ),
    )(
        flat(fields),
        flat(velocity),
        flat(cot_fields),
        flat(cot_velocity),
        masks[0].T,
        context.reshape(R, -1),
        window.transpose(1, 2, 0),
        lift_weight,
        conv_weight,
        attn_qkv,
        attn_out,
        head_weight.T,
        lift_bias[None],
        head_bias[None],
        norm_gain,
        norm_shift,
    )
    pixels = VARS * W
    shapes = (
        (pixels, L),
        (2 * pixels, L),
        (pixels, L),
        (2 * pixels, L),
        lift_weight.shape,
        (1, ch),
        norm_gain.shape,
        norm_shift.shape,
        conv_weight.shape,
        attn_qkv.shape,
        attn_out.shape,
        head_weight.shape[::-1],
        (1, head_bias.shape[0]),
    )
    outs = pl.pallas_call(
        partial(hand_out, rows),
        out_shape=tuple(jax.ShapeDtypeStruct(shape, f32) for shape in shapes),
        in_specs=[whole],
        out_specs=(whole,) * len(shapes),
        compiler_params=pltpu.CompilerParams(vmem_limit_bytes=32 * 2**20),
    )(results)

    def field(x):
        return x.reshape(-1, W, L).transpose(2, 1, 0)[None]

    return (
        *(field(x) for x in outs[:4]),
        outs[4],
        outs[5][0],
        *outs[6:11],
        outs[11].T,
        outs[12][0],
    )


def solution(mesh):
    field = P("batch", None, "lon", None)
    return jax.shard_map(
        partial(on_device, mesh.shape["lon"], mesh.shape["batch"]),
        mesh=mesh,
        in_specs=(
            field,
            field,
            field,
            P("batch", None, "lon"),
            P(None, "lon", None),
            P(),
            P(),
            P(),
            P(),
            P(),
            P(),
            P(),
            P(),
            P(),
            field,
            field,
        ),
        out_specs=(field,) * 4 + (P(),) * 9,
        check_vma=False,
    )
```

```python
from functools import partial
import math

import jax
import jax.numpy as jnp
from jax import lax
from jax.experimental import pallas as pl
from jax.experimental.pallas import tpu as pltpu
from jax.sharding import PartitionSpec as P

HEADS = 4
SECTIONS = 4
LANES = 128
VARS = 5
MASK_LANE = 127
epsilon = 1e-05
step_size = 0.25
f32 = jnp.float32
bf16 = jnp.bfloat16
MESH = pl.DeviceIdType.MESH


def split(x):
    hi = x.astype(bf16)
    return hi, (x - hi.astype(f32)).astype(bf16)


def dot(a, b, dims=((1,), (0,))):
    return lax.dot_general(a, b, (dims, ((), ())), preferred_element_type=f32)


def lanes_cat(*parts):
    return jnp.concatenate(parts, axis=1)


def factors(n, largest):
    out = []
    while n > largest and n % 2 == 0:
        out.append(2)
        n //= 2
    if n > 1:
        out.append(n)
    return out


def job_plan(rows, unit):
    late = -(-9 * LANES // unit)
    middle = -(-18 * LANES // unit) - late
    early = rows // unit - late - middle
    split_late, split_early = (late + 1) // 2, (early + 1) // 2
    sizes = (
        (split_late, "A", 0),
        (late - split_late, "B", 0),
        (middle, "C", 1),
        (split_early, "A", 2),
        (early - split_early, "B", 2),
    )
    plan, at = [], 0
    for units, order, kind in sizes:
        if units:
            plan.append((at * unit, units * unit, order, kind))
        at += units
    return plan


def kernel(
    sizes,
    fields_in,
    velocity_in,
    cot_fields_in,
    cot_velocity_in,
    masks_in,
    context_in,
    window_in,
    lift_in,
    conv_in,
    qkv_in,
    out_in,
    head_in,
    lift_bias_ref,
    head_bias_ref,
    gain_ref,
    shift_ref,
    all_out,
    ys,
    xh,
    xl,
    h0,
    h1,
    a1h,
    a1l,
    a2h,
    a2l,
    dg1,
    dg2,
    h2h,
    h2l,
    qh,
    ql,
    kh,
    kl,
    vh,
    vl,
    probs,
    bh,
    bl,
    h3h,
    h3l,
    norms,
    gk,
    acc,
    tend,
    mask,
    mult,
    w3f,
    w3t,
    wq3,
    wqt3,
    wo3,
    wot3,
    wh3,
    wht3,
    tap,
    blend,
    dbh,
    dbl,
    dqkv,
    dh2,
    h2,
    count,
    de1,
    de0,
    sb,
    rb,
    gw,
    rsb,
    norm_acc,
    bias_acc,
    planes,
    mask_plane,
    context_ref,
    window_ref,
    lift_ref,
    conv_ref,
    qkv_ref,
    out_ref,
    head_ref,
    head_bias_row,
    grad_ref,
    load_sems,
    ar_src,
    ar_buf,
    ar_send,
    ar_recv,
    halo_send,
    halo_recv,
    rs_send,
    rs_recv,
    ag_send,
    ag_recv,
):
    nl, nb, L, W, hid_heads = sizes
    nd = nl * nb
    R = L * W
    R1 = R + 2 * L
    R2 = R + 4 * L
    ch = LANES
    me_l = lax.axis_index("lon")
    me_b = lax.axis_index("batch")
    me = me_l * nb + me_b
    left = (lax.rem(me_l + nl - 1, nl), me_b)
    right = (lax.rem(me_l + 1, nl), me_b)

    def peer(k):
        t = lax.rem(me + k, nd)
        return (t // nb, lax.rem(t, nb))

    low_half = 1 - me_b // max(nb // 2, 1) if nb > 1 else 0
    lon_order = sorted(range(nl), key=lambda hop: -min(hop, nl - hop))
    barrier = pltpu.get_barrier_semaphore()

    def greet(k, c):
        pl.semaphore_signal(barrier, inc=1, device_id=peer(k), device_id_type=MESH)
        return c

    lax.fori_loop(1, nd, greet, 0)

    def sum_start(a, vals):
        ar_src[a] = vals
        ar_buf[a, me] = vals

        def send(k, c):
            to_b = k + low_half * (nb - 1 - 2 * k)
            for hop in lon_order:
                copy = pltpu.make_async_remote_copy(
                    ar_src.at[a],
                    ar_buf.at[a, me],
                    ar_send.at[a],
                    ar_recv.at[a],
                    device_id=(lax.rem(me_l + hop, nl), to_b),
                    device_id_type=MESH,
                )
                if hop == 0:
                    pl.when(to_b != me_b)(copy.start)
                else:
                    copy.start()
            return c

        lax.fori_loop(0, nb, send, 0)

    def sum_wait(a):
        got = ar_buf.at[a, pl.ds(0, nd - 1)]
        pltpu.make_async_copy(got, got, ar_recv.at[a]).wait()
        pltpu.make_async_copy(got, got, ar_send.at[a]).wait()
        return jnp.sum(ar_buf[a], axis=0)

    def side_copy(h, side, src, dst):
        return pltpu.make_async_remote_copy(
            src,
            dst,
            halo_send.at[h, side],
            halo_recv.at[h, side],
            device_id=left if side == 0 else right,
            device_id_type=MESH,
        )

    def halo_copies(h, buf, s, cols):
        n = cols * L
        lo = 2 * L - n
        to_left = side_copy(
            h, 0, buf.at[s, pl.ds(2 * L, n)], buf.at[s, pl.ds(R + 2 * L, n)]
        )
        to_right = side_copy(
            h, 1, buf.at[s, pl.ds(R + 2 * L - n, n)], buf.at[s, pl.ds(lo, n)]
        )
        return to_left, to_right

    def halo_start(h, buf, s, cols):
        for c in halo_copies(h, buf, s, cols):
            c.start()

    def halo_wait(h, buf, s, cols):
        for c in halo_copies(h, buf, s, cols):
            c.wait()

    def lat_of(n):
        return lax.broadcasted_iota(jnp.int32, (n, LANES), 0) % L

    def north(x):
        n = x.shape[0]
        return jnp.where(lat_of(n) == L - 1, 0.0, pltpu.roll(x, n - 1, 0))

    def south(x):
        n = x.shape[0]
        return jnp.where(lat_of(n) == 0, 0.0, pltpu.roll(x, 1, 0))

    def lat_diff(x):
        return 0.5 * (north(x) - south(x))

    def lane_of(n):
        return lax.broadcasted_iota(jnp.int32, (n, LANES), 1)

    def lroll(x, shift):
        return pltpu.roll(x, shift % LANES, 1)

    def conv(hi, lo, base, n, weights):
        cols_h = [hi[base + j * L : base + j * L + n] for j in range(3)]
        cols_l = [lo[base + j * L : base + j * L + n] for j in range(3)]
        wide = dot(lanes_cat(*cols_h, *cols_l, *cols_h), weights)
        return (
            wide[:, ch : 2 * ch]
            + south(wide[:, :ch])
            + north(wide[:, 2 * ch :])
        )

    def product(x, weights):
        hi, lo = split(x)
        return dot(lanes_cat(hi, lo, hi), weights)

    def rows_product(ah, al, gh, gl):
        t = ((0,), (0,))
        return dot(ah, gh, t) + dot(ah, gl, t) + dot(al, gh, t)

    def lat_triple(x):
        return split(lanes_cat(north(x), x, south(x)))

    def conv_back(gh, gl, n, weights):
        wide = dot(lanes_cat(gh, gl, gh), weights)
        return (
            wide[2 * L : 2 * L + n, :ch]
            + wide[L : L + n, ch : 2 * ch]
            + wide[:n, 2 * ch :]
        )

    def add_conv_grad(base, ah, al, gh, gl):
        for j in range(3):
            part = rows_product(
                ah[j * L : j * L + R], al[j * L : j * L + R], gh, gl
            )
            for i in range(3):
                at = base + (i * 3 + j) * ch
                gw[at : at + ch, :] += part[:, i * ch : (i + 1) * ch]

    lift_base, conv_base = 0, 9 * ch
    qkv_base = 27 * ch
    out_base, head_base = 30 * ch, 31 * ch

    all_rows = gw.shape[0]
    unit = 8 * nd
    minor, batch_parts = factors(nl, 2), factors(nb, 4)
    axes = [("lon", n) for n in minor] + [("batch", n) for n in batch_parts]
    steps = {"lon": 1, "batch": 1}
    members = []
    for axis, n in axes:
        mine = me_l if axis == "lon" else me_b
        members.append((axis, steps[axis], n, lax.rem(mine // steps[axis], n)))
        steps[axis] *= n
    def stage_of(member):
        axis, step, n, idx = member

        def device_of(q):
            shift = (q - idx) * step
            if axis == "lon":
                return (me_l + shift, me_b)
            return (me_l, me_b + shift)

        return n, idx, device_of

    first, rest = members[:1], members[1:]
    orders = {
        "A": first + rest,
        "B": first + rest[1::-1] + rest[2:],
        "C": first + rest[::-1],
    }

    def rows_at(at, n):
        return pl.ds(pl.multiple_of(at, 8), n)

    class Job:
        def __init__(self, number, base, size, order):
            self.number = number
            self.stages = stages = [stage_of(m) for m in orders[order]]
            self.regions = []
            off, slot = base, base
            for n, idx, _ in stages:
                part = size // n
                self.regions.append((off, part, slot))
                off = off + idx * part
                slot += (n - 1) * part
                size = part
            self.own, self.size = off, size
            self.done, self.todo = 0, list(self.moves())

        def scatter_start(self, t):
            n, idx, device_of = self.stages[t]
            off, part, slot = self.regions[t]
            for k in range(1, n):
                q = lax.rem(idx + k, n)
                pltpu.make_async_remote_copy(
                    gw.at[rows_at(off + q * part, part)],
                    rsb.at[pl.ds(slot + (n - 1 - k) * part, part)],
                    rs_send.at[self.number, t],
                    rs_recv.at[self.number, t],
                    device_id=device_of(q),
                    device_id_type=MESH,
                ).start()

        def scatter_finish(self, t):
            n, idx, _ = self.stages[t]
            off, part, slot = self.regions[t]
            got = rsb.at[pl.ds(slot, (n - 1) * part)]
            pltpu.make_async_copy(got, got, rs_recv.at[self.number, t]).wait()
            pltpu.make_async_copy(got, got, rs_send.at[self.number, t]).wait()
            mine = off + idx * part
            chunk = math.gcd(part, 128)

            def add(i, c):
                at = pl.multiple_of(i * chunk, 8)
                total = gw[rows_at(mine + at, chunk)]
                for k in range(n - 1):
                    total = total + rsb[rows_at(slot + k * part + at, chunk)]
                gw[rows_at(mine + at, chunk)] = total
                return c

            lax.fori_loop(0, part // chunk, add, 0)

        def gather_start(self, t):
            n, idx, device_of = self.stages[t]
            off, part, _ = self.regions[t]
            if t == len(self.stages) - 1:
                all_out[rows_at(self.own, self.size)] = gw[
                    rows_at(self.own, self.size)
                ]
            mine = all_out.at[rows_at(off + idx * part, part)]
            for k in range(1, n):
                pltpu.make_async_remote_copy(
                    mine,
                    mine,
                    ag_send.at[self.number, t],
                    ag_recv.at[self.number, t],
                    device_id=device_of(lax.rem(idx + k, n)),
                    device_id_type=MESH,
                ).start()

        def gather_finish(self, t):
            n, _, _ = self.stages[t]
            _, part, slot = self.regions[t]
            got = rsb.at[pl.ds(slot, (n - 1) * part)]
            pltpu.make_async_copy(got, got, ag_recv.at[self.number, t]).wait()
            pltpu.make_async_copy(got, got, ag_send.at[self.number, t]).wait()

        def moves(self):
            for t in range(len(self.stages)):
                yield partial(self.scatter_start, t)
                yield partial(self.scatter_finish, t)
            for t in reversed(range(len(self.stages))):
                yield partial(self.gather_start, t)
                yield partial(self.gather_finish, t)

    def take_steps(job, n):
        for _ in range(n):
            job.done += 1
            job.todo[job.done - 1]()

    def drain(jobs):
        while any(job.done < len(job.todo) for job in jobs):
            for job in jobs:
                left_over = len(job.todo) - job.done
                take_steps(job, min(left_over, 1 + (job.done % 2 and left_over > 1)))

    jobs, late, middle, early = [], [], [], []
    for k, (base, size, order, kind) in enumerate(job_plan(all_rows, unit)):
        jobs.append(Job(k, base, size, order))
        (late, middle, early)[kind].append(jobs[-1])
    points = (
        ((early, 1),),
        ((early, 2),),
        ((middle, 1),),
        ((early, 2), (middle, 2)),
        ((late, 1),),
        ((late, 2),),
    )

    def advance(k):
        for some, n in points[k]:
            for job in some:
                take_steps(job, n)

    at_f, at_v, at_cf, at_cv, at_m = (
        k * VARS for k in (0, 1, 3, 4, 6)
    )
    loads = [
        (fields_in, planes.at[at_f * W : at_v * W]),
        (velocity_in, planes.at[at_v * W : at_cf * W]),
        (cot_fields_in, planes.at[at_cf * W : at_cv * W]),
        (cot_velocity_in, planes.at[at_cv * W : at_m * W]),
        (masks_in, mask_plane),
        (context_in, context_ref),
        (lift_in, lift_ref),
        (conv_in, conv_ref),
        (qkv_in, qkv_ref),
        (out_in, out_ref),
        (head_in, head_ref),
        (window_in, window_ref),
    ]
    loads = [
        pltpu.make_async_copy(src, dst, load_sems.at[k])
        for k, (src, dst) in enumerate(loads)
    ]
    for load in loads:
        load.start()
    planes[(at_m + 1) * W :] = jnp.zeros((W, L), f32)
    for load in loads[:6]:
        load.wait()
    planes[at_m * W : (at_m + 1) * W] = mask_plane[...].astype(f32)
    cots = []
    masks_own = []
    for col in range(W):
        at = 2 * L + col * L
        x = planes[pl.ds(col, at_m + 2, stride=W), :].T
        ys[0, at : at + L] = jnp.zeros((L, ch), f32)
        for k in range(3):
            ys[0, at : at + L, k * VARS : (k + 1) * VARS] = x[:, at_f:at_v]
            gk[0, at - 2 * L : at - L, k * VARS : (k + 1) * VARS] = x[:, at_cf:at_cv]
        ys[0, at : at + L, 3 * VARS : 5 * VARS] = x[:, at_v:at_cf]
        gk[0, at - 2 * L : at - L, 3 * VARS : 5 * VARS] = x[:, at_cv:at_m]
        gk[0, at - 2 * L : at - L, 5 * VARS :] = jnp.zeros((L, ch - 5 * VARS), f32)
        ys[0, at : at + L, 5 * VARS : 5 * VARS + context_ref.shape[1]] = context_ref[
            pl.ds(col, L, stride=W), :
        ]
        ys[0, at : at + L, MASK_LANE:] = x[:, at_m : at_m + 1]
    cot = gk[0]
    mask_own = jnp.broadcast_to(
        ys[0, 2 * L : 2 * L + R, MASK_LANE : MASK_LANE + 1], (R, LANES)
    )
    count_part = jnp.sum(mask_own, axis=0, keepdims=True)
    for load in loads[6:8]:
        load.wait()

    tap[...] = jnp.zeros_like(tap)
    for b in range(3):
        for i in range(3):
            for j in range(3):
                if b == 0:
                    tap[: lift_ref.shape[2]] = lift_ref[i, j]
                    w = tap[...]
                else:
                    w = conv_ref[b - 1, i, j]
                hi, lo = split(w)
                for p, part in enumerate((hi, hi, lo)):
                    at = (p * 3 + j) * ch
                    w3f[b, at : at + ch, i * ch : (i + 1) * ch] = part
                hi, lo = split(w.T)
                for p, part in enumerate((hi, hi, lo)):
                    at = (p * 3 + i) * ch
                    w3t[b, at : at + ch, j * ch : (j + 1) * ch] = part

    pl.semaphore_wait(barrier, nd - 1)
    halo_start(0, ys, 0, 2)
    sum_start(4 * SECTIONS, jnp.concatenate([count_part, count_part], axis=0))

    def put_three(target, w):
        n = w.shape[0]
        hi, lo = split(w)
        target[:n] = hi
        target[n : 2 * n] = hi
        target[2 * n :] = lo

    for load in loads[8:]:
        load.wait()
    put_three(wq3, qkv_ref[...])
    put_three(wqt3, qkv_ref[...].T)
    put_three(wo3, out_ref[...])
    put_three(wot3, out_ref[...].T)
    tap[...] = jnp.zeros_like(tap)
    tap[3 * VARS : 5 * VARS] = head_ref[...]
    put_three(wht3, tap[...])
    put_three(wh3, tap[...].T)
    head_bias_row[...] = jnp.zeros_like(head_bias_row)
    head_bias_row[:, 3 * VARS : 5 * VARS] = head_bias_ref[...]
    for s, weight in enumerate((1.0, 2.0, 2.0, 1.0)):
        gk[s] = cot * (weight * step_size / 6.0)
    grad_ref[...] = cot
    acc[...] = jnp.zeros_like(acc)
    gw[...] = jnp.zeros_like(gw)
    norm_acc[...] = jnp.zeros_like(norm_acc)
    bias_acc[...] = jnp.zeros_like(bias_acc)

    pair = 2 * L
    shape = (2 * pair, HEADS * pair)
    key_of = lax.broadcasted_iota(jnp.int32, shape, 0)
    key_of = key_of - lax.broadcasted_iota(jnp.int32, shape, 1) // L % 2 * L
    for p in range(W // 2):
        entries = lanes_cat(*[window_ref[2 * p], window_ref[2 * p + 1]] * HEADS)
        counted = jnp.zeros(shape, f32)
        for k in range(entries.shape[0]):
            counted = counted + jnp.where(entries[k : k + 1] == key_of, 1.0, 0.0)
        mult[p] = jnp.where(
            counted > 0.0, jnp.log(jnp.maximum(counted, 1.0)), -1e30
        )

    head_rows = lax.broadcasted_iota(jnp.int32, (HEADS * pair, ch), 0) // pair
    head_lanes = lax.broadcasted_iota(jnp.int32, (HEADS * pair, ch), 1) // (ch // HEADS)
    head_mask = jnp.where(head_rows == head_lanes, 1.0, 0.0)
    head_mask_h = head_mask.astype(bf16)
    scale = (ch // HEADS) ** -0.5

    def per_head(x):
        return jnp.concatenate([x] * HEADS, axis=0) * head_mask_h

    def heads_sum(x):
        x = x * head_mask
        return sum(x[h * pair : (h + 1) * pair] for h in range(1, HEADS)) + x[:pair]

    lift_bias = lift_bias_ref[...]
    head_bias = head_bias_row[...]
    gains = [gain_ref[0:1], gain_ref[1:2]]
    shifts = [shift_ref[0:1], shift_ref[1:2]]

    def stats(h):
        weighted = h * mask[2 * L : 2 * L + R]
        return jnp.concatenate(
            [
                jnp.sum(weighted, axis=0, keepdims=True),
                jnp.sum(weighted * h, axis=0, keepdims=True),
            ],
            axis=0,
        )

    def normalise(s, b, sums):
        total_count = count[0:1]
        average = sums[0:1] / total_count
        spread = sums[1:2] / total_count - average * average
        inverse = lax.rsqrt(spread + epsilon)
        norms[s, b, 0:1] = average
        norms[s, b, 1:2] = inverse
        return average, inverse

    def activity(h, b, average, inverse):
        z = (h - average) * inverse * gains[b] + shifts[b]
        below = 0.5 * (1.0 + lax.erf(z * (0.5**0.5)))
        slope = below + z * (
            jnp.exp(-0.5 * z * z) * (1.0 / math.sqrt(2.0 * math.pi))
        )
        return z * below, slope

    group = 2

    def forward(s, carry):
        hb = s * 6

        halo_wait(hb, ys, s, 2)

        @pl.when(s == 0)
        def _():
            mask[...] = jnp.broadcast_to(
                ys[0, :, MASK_LANE : MASK_LANE + 1], (R2, LANES)
            )

        y1 = ys[s, L : L + R1]
        lane = lane_of(R1)
        lon = 0.5 * (ys[s, 2 * L : 2 * L + R1] - ys[s, 0:R1])
        x = jnp.where(
            (lane >= VARS) & (lane < 2 * VARS),
            lat_diff(y1),
            jnp.where((lane >= 2 * VARS) & (lane < 3 * VARS), lon, y1),
        )
        hi, lo = split(x)
        xh[s] = hi
        xl[s] = lo
        first = conv(xh.at[s], xl.at[s], 0, R, w3f[0]) + lift_bias
        h0[s, 2 * L : 2 * L + R] = first
        sum_start(s * 4, stats(first))
        halo_start(hb + 1, h0, s, 2)
        flux = y1 * lroll(y1, -3 * VARS)
        flux = jnp.where(lane < 2 * VARS, flux, 0.0)
        own_lane = lane_of(R)
        t_lat = jnp.where(own_lane < VARS, lat_diff(flux[L : L + R]), 0.0)
        t_lon = jnp.where(
            own_lane >= VARS, 0.5 * (flux[2 * L : 2 * L + R] - flux[:R]), 0.0
        )
        t = -(t_lat + lroll(t_lon, -VARS))
        tend[...] = t + lroll(t, VARS) + lroll(t, 2 * VARS)


        @pl.when(s == 0)
        def _():
            count[...] = sum_wait(4 * SECTIONS)

        average, inverse = normalise(s, 0, sum_wait(s * 4))
        halo_wait(hb + 1, h0, s, 2)
        act, slope = activity(h0[s, L : L + R1], 0, average, inverse)
        dg1[s] = slope[L : L + R]
        hi, lo = split(act)
        a1h[s] = hi
        a1l[s] = lo
        second = h0[s, 2 * L : 2 * L + R] + conv(a1h.at[s], a1l.at[s], 0, R, w3f[1])
        h1[s, 2 * L : 2 * L + R] = second
        sum_start(s * 4 + 1, stats(second))
        halo_start(hb + 2, h1, s, 2)
        average, inverse = normalise(s, 1, sum_wait(s * 4 + 1))
        halo_wait(hb + 2, h1, s, 2)
        act, slope = activity(h1[s], 1, average, inverse)
        dg2[s] = slope[2 * L : 2 * L + R]
        hi, lo = split(act)
        a2h[s] = hi
        a2l[s] = lo
        third = h1[s, L : L + R1] + conv(a2h.at[s], a2l.at[s], 0, R1, w3f[2])
        h2[...] = third
        hi, lo = split(third)
        h2h[s] = hi
        h2l[s] = lo
        mixing = dot(lanes_cat(hi, lo, hi), wq3[...])
        hi, lo = split(mixing[L : L + R, :ch] * scale)
        qh[s] = hi
        ql[s] = lo
        hi, lo = split(mixing[:, ch : 2 * ch])
        kh[s] = hi
        kl[s] = lo
        hi, lo = split(mixing[:, 2 * ch :])
        vh[s] = hi
        vl[s] = lo

        def attend(pairs):
            scores = []
            for p in pairs:
                at = pl.multiple_of(p * pair, pair)
                q_h = per_head(qh[s, pl.ds(at, pair)])
                q_l = per_head(ql[s, pl.ds(at, pair)])
                k_h = kh[s, pl.ds(at, 2 * pair)]
                k_l = kl[s, pl.ds(at, 2 * pair)]
                scores.append(
                    dot(
                        lanes_cat(k_h, k_l, k_h),
                        lanes_cat(q_h, q_h, q_l),
                        ((1,), (1,)),
                    )
                )
            weights = []
            for p, score in zip(pairs, scores):
                score = score + mult[p]
                e = jnp.exp(score - jnp.max(score, axis=0, keepdims=True))
                e = e * (1.0 / jnp.sum(e, axis=0, keepdims=True))
                probs[s, p] = e
                weights.append(e)
            for p, e in zip(pairs, weights):
                at = pl.multiple_of(p * pair, pair)
                p_h, p_l = split(e.T)
                v_h = vh[s, pl.ds(at, 2 * pair)]
                v_l = vl[s, pl.ds(at, 2 * pair)]
                o = dot(
                    lanes_cat(p_h, p_l, p_h),
                    jnp.concatenate([v_h, v_h, v_l], axis=0),
                )
                blend[pl.ds(at, pair)] = heads_sum(o)

        weight = jnp.where((s == 0) | (s == SECTIONS - 1), 1.0, 2.0)
        factor = jnp.where(s == SECTIONS - 2, 1.0, 0.5) * step_size

        def finish(ranges):
            def take(ref, base=0):
                return jnp.concatenate(
                    [ref[base + a : base + b] for a, b in ranges], axis=0
                )

            def give(ref, value, base=0):
                at = 0
                for a, b in ranges:
                    ref[base + a : base + b] = value[at : at + b - a]
                    at += b - a

            hi, lo = split(take(blend))
            give(bh.at[s], hi)
            give(bl.at[s], lo)
            fourth = take(h2, L) + dot(lanes_cat(hi, lo, hi), wo3[...])
            hi, lo = split(fourth)
            give(h3h.at[s], hi)
            give(h3l.at[s], lo)
            slope_now = (
                take(tend) + dot(lanes_cat(hi, lo, hi), wh3[...]) + head_bias
            )
            give(acc, take(acc) + weight * slope_now)

            @pl.when(s < SECTIONS - 1)
            def _():
                give(
                    ys.at[s + 1],
                    take(ys.at[0], 2 * L) + factor * slope_now,
                    2 * L,
                )

        last = W // 2 - 1
        attend([0, last])
        finish([(0, pair), (R - pair, R)])

        @pl.when(s < SECTIONS - 1)
        def _():
            halo_start(hb + 6, ys, s + 1, 2)

        def inner(k, c):
            attend([1 + group * k + m for m in range(group)])
            return c

        lax.fori_loop(0, (last - 1) // group, inner, 0)
        finish([(pair, R - pair)])
        return carry

    lax.fori_loop(0, SECTIONS, forward, 0)
    acc[...] = ys[0, 2 * L : 2 * L + R] + (step_size / 6.0) * acc[...]

    def norm_back(s, b, h, grad_act, slope, through):
        average = norms[s, b, 0:1]
        inverse = norms[s, b, 1:2]
        dz = grad_act * slope
        hat = (h - average) * inverse
        sums = jnp.concatenate(
            [
                jnp.sum(dz, axis=0, keepdims=True),
                jnp.sum(dz * hat, axis=0, keepdims=True),
            ],
            axis=0,
        )
        return sums, through + dz * (gains[b] * inverse)

    def norm_rest(s, b, h, weight_mask, direct, sums):
        average = norms[s, b, 0:1]
        inverse = norms[s, b, 1:2]
        hat = (h - average) * inverse
        norm_acc[b] += sums
        return direct - weight_mask * (
            gains[b] * inverse / count[0:1]
        ) * (sums[0:1] + hat * sums[1:2])

    def backward(turn, carry):
        s = SECTIONS - 1 - turn
        hb = s * 6
        g = gk[s]
        g_h, g_l = split(g)
        grad3 = dot(lanes_cat(g_h, g_l, g_h), wht3[...])
        grad3_h, grad3_l = split(grad3)
        hi, lo = split(dot(lanes_cat(grad3_h, grad3_l, grad3_h), wot3[...]))
        dbh[...] = hi
        dbl[...] = lo
        dqkv[...] = jnp.zeros_like(dqkv)

        def attend_back(pairs):
            dps = []
            for p in pairs:
                at = pl.multiple_of(p * pair, pair)
                d_h = per_head(dbh[pl.ds(at, pair)])
                d_l = per_head(dbl[pl.ds(at, pair)])
                v_h = vh[s, pl.ds(at, 2 * pair)]
                v_l = vl[s, pl.ds(at, 2 * pair)]
                dps.append(
                    dot(
                        lanes_cat(v_h, v_l, v_h),
                        lanes_cat(d_h, d_h, d_l),
                        ((1,), (1,)),
                    )
                )
            dss = []
            for p, dp in zip(pairs, dps):
                e = probs[s, p]
                dss.append(e * (dp - jnp.sum(e * dp, axis=0, keepdims=True)))
            for p, ds in zip(pairs, dss):
                at = pl.multiple_of(p * pair, pair)
                k_h = kh[s, pl.ds(at, 2 * pair)]
                k_l = kl[s, pl.ds(at, 2 * pair)]
                t_h, t_l = split(ds.T)
                o = dot(
                    lanes_cat(t_h, t_l, t_h),
                    jnp.concatenate([k_h, k_h, k_l], axis=0),
                )
                dqkv[pl.ds(at + L, pair), :ch] = heads_sum(o) * scale
                q_h = per_head(qh[s, pl.ds(at, pair)])
                q_l = per_head(ql[s, pl.ds(at, pair)])
                s_h, s_l = split(ds)
                o = dot(s_h, lanes_cat(q_h, q_l))
                o = o[:, :ch] + o[:, ch:] + dot(s_l, q_h)
                dqkv[pl.ds(at, 2 * pair), ch : 2 * ch] += o
                d_h = per_head(dbh[pl.ds(at, pair)])
                d_l = per_head(dbl[pl.ds(at, pair)])
                s_h, s_l = split(probs[s, p])
                o = dot(s_h, lanes_cat(d_h, d_l))
                o = o[:, :ch] + o[:, ch:] + dot(s_l, d_h)
                dqkv[pl.ds(at, 2 * pair), 2 * ch :] += o

        last = W // 2 - 1
        attend_back([0, last])
        edge_h, edge_l = split(
            jnp.concatenate([dqkv[:pair], dqkv[R1 - pair :]], axis=0)
        )
        part = dot(lanes_cat(edge_h, edge_l, edge_h), wqt3[...])
        zeros = jnp.zeros((L, ch), f32)
        part = part + jnp.concatenate(
            [zeros, grad3[:L], grad3[R - L :], zeros], axis=0
        )
        dh2[:pair] = part[:pair]
        dh2[R1 - pair :] = part[pair:]
        sb[s, 0, :pair] = part[:pair]
        sb[s, 0, pair:] = gk[s, :L]
        sb[s, 1, :pair] = part[pair:]
        sb[s, 1, pair:] = gk[s, R - L :]
        edges = [
            side_copy(hb + 3, side, sb.at[s, side], rb.at[s, side])
            for side in range(2)
        ]
        for e in edges:
            e.start()

        def inner(k, c):
            attend_back([1 + group * k + m for m in range(group)])
            return c

        lax.fori_loop(0, (last - 1) // group, inner, 0)
        d_h, d_l = split(dqkv[...])
        mid_h, mid_l = d_h[pair : R1 - pair], d_l[pair : R1 - pair]
        dh2[pair : R1 - pair] = grad3[L : R - L] + dot(
            lanes_cat(mid_h, mid_l, mid_h), wqt3[...]
        )
        for e in edges:
            e.wait()
        dh2[:pair] += rb[s, 1, :pair]
        dh2[R1 - pair :] += rb[s, 0, :pair]

        t_h, t_l = lat_triple(dh2[...])
        grad_act = conv_back(t_h, t_l, R, w3t[2])
        sums, direct = norm_back(
            s, 1, h1[s, 2 * L : 2 * L + R], grad_act, dg2[s], dh2[L : L + R]
        )
        sum_start(s * 4 + 2, sums)
        de1[s, 2 * L : 2 * L + R] = direct
        halo_start(hb + 4, de1, s, 1)
        bias_acc[1:2] += jnp.sum(g, axis=0, keepdims=True)
        gw[head_base : head_base + ch] += rows_product(h3h[s], h3l[s], g_h, g_l)
        gw[out_base : out_base + ch] += rows_product(bh[s], bl[s], grad3_h, grad3_l)
        wide = rows_product(h2h[s], h2l[s], d_h, d_l)
        for k in range(3):
            at = qkv_base + k * ch
            gw[at : at + ch] += wide[:, k * ch : (k + 1) * ch]
        add_conv_grad(
            conv_base + 9 * ch,
            a2h[s, L : L + R1],
            a2l[s, L : L + R1],
            t_h[L : L + R],
            t_l[L : L + R],
        )
        pl.when(s == 0)(lambda: advance(0))
        sums = sum_wait(s * 4 + 2)
        halo_wait(hb + 4, de1, s, 1)
        pl.when(s == 0)(lambda: advance(1))
        grad1 = norm_rest(
            s, 1, h1[s, L : L + R1], mask[L : L + R1], de1[s, L : L + R1], sums
        )
        t_h, t_l = lat_triple(grad1)
        grad_act = conv_back(t_h, t_l, R, w3t[1])
        sums, direct = norm_back(
            s, 0, h0[s, 2 * L : 2 * L + R], grad_act, dg1[s], grad1[L : L + R]
        )
        sum_start(s * 4 + 3, sums)
        de0[s, 2 * L : 2 * L + R] = direct
        halo_start(hb + 5, de0, s, 2)
        add_conv_grad(
            conv_base, a1h[s], a1l[s], t_h[L : L + R], t_l[L : L + R]
        )
        pl.when(s == 0)(lambda: advance(2))
        sums = sum_wait(s * 4 + 3)
        halo_wait(hb + 5, de0, s, 2)

        @pl.when(s == 0)
        def _():
            advance(3)

        grad0 = norm_rest(s, 0, h0[s], mask[...], de0[s], sums)
        bias_acc[0:1] += jnp.sum(grad0[2 * L : 2 * L + R], axis=0, keepdims=True)
        t_h, t_l = lat_triple(grad0)
        add_conv_grad(
            lift_base, xh[s], xl[s], t_h[2 * L : 2 * L + R], t_l[2 * L : 2 * L + R]
        )

        @pl.when(s == 0)
        def _():
            gw[ch - 28 : ch - 26] = bias_acc[...]
            advance(4)

        dx = conv_back(t_h, t_l, R1, w3t[0])
        lane = lane_of(R)
        own = dx[L : L + R]
        lon = 0.5 * (dx[2 * L :] - dx[:R])
        g = gk[s]
        g_lon = jnp.concatenate([g[L:], rb[s, 0, 2 * L :]], axis=0)
        g_lon = 0.5 * (
            g_lon - jnp.concatenate([rb[s, 1, 2 * L :], g[: R - L]], axis=0)
        )
        dflux = jnp.where(
            lane < VARS, lat_diff(g), jnp.where(lane < 2 * VARS, g_lon, 0.0)
        )
        y = ys[s, 2 * L : 2 * L + R]
        parts = jnp.where(
            lane < VARS,
            own,
            jnp.where(lane < 2 * VARS, -lat_diff(own), -lon),
        )
        parts = parts + dflux * lroll(y, -3 * VARS)
        parts = jnp.where(lane < 3 * VARS, parts, 0.0)
        fields_grad = (
            parts
            + lroll(parts, VARS)
            + lroll(parts, 2 * VARS)
            + lroll(parts, -VARS)
            + lroll(parts, -2 * VARS)
        )
        velocity_grad = own + lroll(dflux * y, 3 * VARS)
        gy = jnp.where(
            lane < 3 * VARS,
            fields_grad,
            jnp.where(lane < 5 * VARS, velocity_grad, 0.0),
        )
        grad_ref[...] += gy

        @pl.when(s > 0)
        def _():
            factor = jnp.where(s == SECTIONS - 1, 1.0, 0.5) * step_size
            gk[s - 1] = gk[s - 1] + factor * gy

        return carry

    lax.fori_loop(0, SECTIONS, backward, 0)

    advance(5)
    all_out[gw.shape[0] : gw.shape[0] + 4] = norm_acc[...].reshape(4, ch)
    lane = lane_of(R)
    new, grad = acc[...], grad_ref[...]
    merged = jnp.where(
        lane < at_v,
        new,
        jnp.where(
            lane < at_cf,
            lroll(new, at_v - 3 * VARS),
            jnp.where(
                lane < at_cv, lroll(grad, at_cf), lroll(grad, at_cv - 3 * VARS)
            ),
        ),
    )
    for col in range(W):
        x = merged[col * L : (col + 1) * L].T
        all_out[pl.ds(gw.shape[0] + 8 + col, at_m, stride=W), :] = lanes_cat(
            x[:at_m], jnp.zeros((at_m, ch - L), f32)
        )

    drain(jobs)


def hand_out(rows, weights, *outs):
    fields = outs[:4]
    lift, lift_bias, gain, shift, conv, qkv, out, head, head_bias = outs[4:]
    ch = LANES
    at = rows + 8
    for ref in fields:
        ref[...] = weights[at : at + ref.shape[0], : ref.shape[1]]
        at += ref.shape[0]
    cin = lift.shape[2]
    vel = slice(3 * VARS, 5 * VARS)
    for i in range(3):
        for j in range(3):
            at = (i * 3 + j) * ch
            lift[i, j] = weights[at : at + cin]
            for b in range(2):
                at_conv = at + (b + 1) * 9 * ch
                conv[b, i, j] = weights[at_conv : at_conv + ch]
    lift_bias[...] = weights[cin : cin + 1]
    head_bias[...] = weights[cin + 1 : cin + 2, vel]
    for b in range(2):
        at = rows + 2 * b
        shift[b : b + 1] = weights[at : at + 1]
        gain[b : b + 1] = weights[at + 1 : at + 2]
    for k in range(3):
        at = (27 + k) * ch
        qkv[:, k * ch : (k + 1) * ch] = weights[at : at + ch]
    out[...] = weights[30 * ch : 31 * ch]
    head[...] = weights[31 * ch : 32 * ch].T[vel]


def on_device(
    nl,
    nb,
    fields,
    velocity,
    context,
    masks,
    window,
    lift_weight,
    lift_bias,
    norm_gain,
    norm_shift,
    conv_weight,
    attn_qkv,
    attn_out,
    head_weight,
    head_bias,
    cot_fields,
    cot_velocity,
):
    _, L, W, _ = fields.shape
    R, R1, R2 = L * W, L * (W + 2), L * (W + 4)
    ch = LANES
    nd = nl * nb

    def flat(x):
        return x[0].transpose(2, 1, 0).reshape(-1, L)

    S = SECTIONS
    rows = 32 * ch
    rows = -(-rows // (8 * nd)) * 8 * nd
    stage_count = len(factors(nl, 2)) + len(factors(nb, 4))
    job_count = len(job_plan(rows, 8 * nd))
    vm = pltpu.VMEM
    dma = pltpu.SemaphoreType.DMA
    scratch = [
        vm((S, R2, ch), f32),
        vm((S, R1, ch), bf16),
        vm((S, R1, ch), bf16),
        vm((S, R2, ch), f32),
        vm((S, R2, ch), f32),
        vm((S, R1, ch), bf16),
        vm((S, R1, ch), bf16),
        vm((S, R2, ch), bf16),
        vm((S, R2, ch), bf16),
        vm((S, R, ch), f32),
        vm((S, R, ch), f32),
        vm((S, R1, ch), bf16),
        vm((S, R1, ch), bf16),
        vm((S, R, ch), bf16),
        vm((S, R, ch), bf16),
        vm((S, R1, ch), bf16),
        vm((S, R1, ch), bf16),
        vm((S, R1, ch), bf16),
        vm((S, R1, ch), bf16),
        vm((S, W // 2, 4 * L, 2 * HEADS * L), f32),
        vm((S, R, ch), bf16),
        vm((S, R, ch), bf16),
        vm((S, R, ch), bf16),
        vm((S, R, ch), bf16),
        vm((S, 2, 8, ch), f32),
        vm((S, R, ch), f32),
        vm((R, ch), f32),
        vm((R, ch), f32),
        vm((R2, ch), f32),
        vm((W // 2, 4 * L, 2 * HEADS * L), f32),
        vm((3, 9 * ch, 3 * ch), bf16),
        vm((3, 9 * ch, 3 * ch), bf16),
        vm((3 * ch, 3 * ch), bf16),
        vm((9 * ch, ch), bf16),
        vm((3 * ch, ch), bf16),
        vm((3 * ch, ch), bf16),
        vm((3 * ch, ch), bf16),
        vm((3 * ch, ch), bf16),
        vm((ch, ch), f32),
        vm((R, ch), f32),
        vm((R, ch), bf16),
        vm((R, ch), bf16),
        vm((R1, 3 * ch), f32),
        vm((R1, ch), f32),
        vm((R1, ch), f32),
        vm((2, ch), f32),
        vm((S, R2, ch), f32),
        vm((S, R2, ch), f32),
        vm((S, 2, 3 * L, ch), f32),
        vm((S, 2, 3 * L, ch), f32),
        vm((rows, ch), f32),
        vm((rows, ch), f32),
        vm((2, 2, ch), f32),
        vm((2, ch), f32),
        vm((32 * W, L), f32),
        vm((W, L), jnp.int32),
        vm((R, context.shape[-1]), f32),
        vm((W, window.shape[-1], L), jnp.int32),
        vm(lift_weight.shape, f32),
        vm(conv_weight.shape, f32),
        vm(attn_qkv.shape, f32),
        vm(attn_out.shape, f32),
        vm(head_weight.shape[::-1], f32),
        vm((1, ch), f32),
        vm((R, ch), f32),
        dma((12,)),
        vm((4 * S + 1, 2, ch), f32),
        vm((4 * S + 1, nd, 2, ch), f32),
        dma((4 * S + 1,)),
        dma((4 * S + 1,)),
        dma((6 * S, 2)),
        dma((6 * S, 2)),
        dma((job_count, stage_count)),
        dma((job_count, stage_count)),
        dma((job_count, stage_count)),
        dma((job_count, stage_count)),
    ]
    whole = pl.BlockSpec(memory_space=pltpu.VMEM)
    apart = pl.BlockSpec(memory_space=pl.ANY)
    results = pl.pallas_call(
        partial(kernel, (nl, nb, L, W, HEADS)),
        out_shape=jax.ShapeDtypeStruct((rows + 8 + 6 * VARS * W, ch), f32),
        in_specs=[apart] * 12 + [whole] * 4,
        out_specs=whole,
        scratch_shapes=scratch,
        compiler_params=pltpu.CompilerParams(
            collective_id=0, has_side_effects=True, vmem_limit_bytes=60 * 2**20
        ),
    )(
        flat(fields),
        flat(velocity),
        flat(cot_fields),
        flat(cot_velocity),
        masks[0].T,
        context.reshape(R, -1),
        window.transpose(1, 2, 0),
        lift_weight,
        conv_weight,
        attn_qkv,
        attn_out,
        head_weight.T,
        lift_bias[None],
        head_bias[None],
        norm_gain,
        norm_shift,
    )
    pixels = VARS * W
    shapes = (
        (pixels, L),
        (2 * pixels, L),
        (pixels, L),
        (2 * pixels, L),
        lift_weight.shape,
        (1, ch),
        norm_gain.shape,
        norm_shift.shape,
        conv_weight.shape,
        attn_qkv.shape,
        attn_out.shape,
        head_weight.shape[::-1],
        (1, head_bias.shape[0]),
    )
    outs = pl.pallas_call(
        partial(hand_out, rows),
        out_shape=tuple(jax.ShapeDtypeStruct(shape, f32) for shape in shapes),
        in_specs=[whole],
        out_specs=(whole,) * len(shapes),
        compiler_params=pltpu.CompilerParams(vmem_limit_bytes=32 * 2**20),
    )(results)

    def field(x):
        return x.reshape(-1, W, L).transpose(2, 1, 0)[None]

    return (
        *(field(x) for x in outs[:4]),
        outs[4],
        outs[5][0],
        *outs[6:11],
        outs[11].T,
        outs[12][0],
    )


def solution(mesh):
    field = P("batch", None, "lon", None)
    return jax.shard_map(
        partial(on_device, mesh.shape["lon"], mesh.shape["batch"]),
        mesh=mesh,
        in_specs=(
            field,
            field,
            field,
            P("batch", None, "lon"),
            P(None, "lon", None),
            P(),
            P(),
            P(),
            P(),
            P(),
            P(),
            P(),
            P(),
            P(),
            field,
            field,
        ),
        out_specs=(field,) * 4 + (P(),) * 9,
        check_vma=False,
    )
```

```python
from functools import partial
import math

import jax
import jax.numpy as jnp
from jax import lax
from jax.experimental import pallas as pl
from jax.experimental.pallas import tpu as pltpu
from jax.sharding import PartitionSpec as P

HEADS = 4
SECTIONS = 4
LANES = 128
VARS = 5
MASK_LANE = 127
epsilon = 1e-05
step_size = 0.25
f32 = jnp.float32
bf16 = jnp.bfloat16
MESH = pl.DeviceIdType.MESH


def split(x):
    hi = x.astype(bf16)
    return hi, (x - hi.astype(f32)).astype(bf16)


def dot(a, b, dims=((1,), (0,))):
    return lax.dot_general(a, b, (dims, ((), ())), preferred_element_type=f32)


def lanes_cat(*parts):
    return jnp.concatenate(parts, axis=1)


def factors(n, largest):
    out = []
    while n > largest and n % 2 == 0:
        out.append(2)
        n //= 2
    if n > 1:
        out.append(n)
    return out


def job_plan(rows, unit):
    late = -(-9 * LANES // unit)
    middle = -(-18 * LANES // unit) - late
    early = rows // unit - late - middle
    split_late, split_early = (late + 1) // 2, (early + 1) // 2
    sizes = (
        (split_late, "A", 0),
        (late - split_late, "B", 0),
        (middle, "C", 1),
        (split_early, "A", 2),
        (early - split_early, "B", 2),
    )
    plan, at = [], 0
    for units, order, kind in sizes:
        if units:
            plan.append((at * unit, units * unit, order, kind))
        at += units
    return plan


def kernel(
    sizes,
    fields_in,
    velocity_in,
    cot_fields_in,
    cot_velocity_in,
    masks_in,
    context_in,
    window_in,
    lift_in,
    conv_in,
    qkv_in,
    out_in,
    head_in,
    lift_bias_ref,
    head_bias_ref,
    gain_ref,
    shift_ref,
    all_out,
    ys,
    xh,
    xl,
    h0,
    h1,
    a1h,
    a1l,
    a2h,
    a2l,
    dg1,
    dg2,
    h2h,
    h2l,
    qh,
    ql,
    kh,
    kl,
    vh,
    vl,
    probs,
    bh,
    bl,
    h3h,
    h3l,
    norms,
    gk,
    acc,
    tend,
    mask,
    mult,
    w3f,
    w3t,
    wq3,
    wqt3,
    wo3,
    wot3,
    wh3,
    wht3,
    tap,
    blend,
    dbh,
    dbl,
    gh,
    gl,
    dh3h,
    dh3l,
    th,
    tl,
    lift_th,
    lift_tl,
    dqkv,
    dh2,
    h2,
    count,
    de1,
    de0,
    sb,
    rb,
    gw,
    rsb,
    norm_acc,
    bias_acc,
    planes,
    mask_plane,
    context_ref,
    window_ref,
    lift_ref,
    conv_ref,
    qkv_ref,
    out_ref,
    head_ref,
    head_bias_row,
    grad_ref,
    load_sems,
    ar_src,
    ar_buf,
    ar_send,
    ar_recv,
    halo_send,
    halo_recv,
    rs_send,
    rs_recv,
    ag_send,
    ag_recv,
):
    nl, nb, L, W, hid_heads = sizes
    nd = nl * nb
    R = L * W
    R1 = R + 2 * L
    R2 = R + 4 * L
    ch = LANES
    me_l = lax.axis_index("lon")
    me_b = lax.axis_index("batch")
    me = me_l * nb + me_b
    left = (lax.rem(me_l + nl - 1, nl), me_b)
    right = (lax.rem(me_l + 1, nl), me_b)

    def peer(k):
        t = lax.rem(me + k, nd)
        return (t // nb, lax.rem(t, nb))

    low_half = 1 - me_b // max(nb // 2, 1) if nb > 1 else 0
    lon_order = sorted(range(nl), key=lambda hop: -min(hop, nl - hop))
    barrier = pltpu.get_barrier_semaphore()

    def greet(k, c):
        pl.semaphore_signal(barrier, inc=1, device_id=peer(k), device_id_type=MESH)
        return c

    lax.fori_loop(1, nd, greet, 0)

    def sum_start(a, vals):
        ar_src[a] = vals
        ar_buf[a, me] = vals

        def send(k, c):
            to_b = k + low_half * (nb - 1 - 2 * k)
            for hop in lon_order:
                copy = pltpu.make_async_remote_copy(
                    ar_src.at[a],
                    ar_buf.at[a, me],
                    ar_send.at[a],
                    ar_recv.at[a],
                    device_id=(lax.rem(me_l + hop, nl), to_b),
                    device_id_type=MESH,
                )
                if hop == 0:
                    pl.when(to_b != me_b)(copy.start)
                else:
                    copy.start()
            return c

        lax.fori_loop(0, nb, send, 0)

    def sum_wait(a):
        got = ar_buf.at[a, pl.ds(0, nd - 1)]
        pltpu.make_async_copy(got, got, ar_recv.at[a]).wait()
        pltpu.make_async_copy(got, got, ar_send.at[a]).wait()
        return jnp.sum(ar_buf[a], axis=0)

    def side_copy(h, side, src, dst):
        return pltpu.make_async_remote_copy(
            src,
            dst,
            halo_send.at[h, side],
            halo_recv.at[h, side],
            device_id=left if side == 0 else right,
            device_id_type=MESH,
        )

    def halo_copies(h, buf, s, cols):
        n = cols * L
        lo = 2 * L - n
        to_left = side_copy(
            h, 0, buf.at[s, pl.ds(2 * L, n)], buf.at[s, pl.ds(R + 2 * L, n)]
        )
        to_right = side_copy(
            h, 1, buf.at[s, pl.ds(R + 2 * L - n, n)], buf.at[s, pl.ds(lo, n)]
        )
        return to_left, to_right

    def halo_start(h, buf, s, cols):
        for c in halo_copies(h, buf, s, cols):
            c.start()

    def halo_wait(h, buf, s, cols):
        for c in halo_copies(h, buf, s, cols):
            c.wait()

    def lat_of(n):
        return lax.broadcasted_iota(jnp.int32, (n, LANES), 0) % L

    def north(x):
        n = x.shape[0]
        return jnp.where(lat_of(n) == L - 1, 0.0, pltpu.roll(x, n - 1, 0))

    def south(x):
        n = x.shape[0]
        return jnp.where(lat_of(n) == 0, 0.0, pltpu.roll(x, 1, 0))

    def lat_diff(x):
        return 0.5 * (north(x) - south(x))

    def lane_of(n):
        return lax.broadcasted_iota(jnp.int32, (n, LANES), 1)

    def lroll(x, shift):
        return pltpu.roll(x, shift % LANES, 1)

    def rows_of(ref, ranges, base=0):
        parts = [ref[base + a : base + b] for a, b in ranges]
        return parts[0] if len(parts) == 1 else jnp.concatenate(parts, axis=0)

    def put_rows(ref, value, ranges, base=0):
        at = 0
        for a, b in ranges:
            ref[base + a : base + b] = value[at : at + b - a]
            at += b - a

    def conv(hi, lo, ranges, weights):
        cols_h = [rows_of(hi, ranges, j * L) for j in range(3)]
        cols_l = [rows_of(lo, ranges, j * L) for j in range(3)]
        wide = dot(lanes_cat(*cols_h, *cols_l, *cols_h), weights)
        return (
            wide[:, ch : 2 * ch]
            + south(wide[:, :ch])
            + north(wide[:, 2 * ch :])
        )

    def product(hi, lo, weights):
        wide = dot(lanes_cat(hi, lo), weights)
        n = wide.shape[1] // 2
        return wide[:, :n] + wide[:, n:]

    def rows_product(ah, al, gh, gl):
        t = ((0,), (0,))
        return dot(ah, gh, t) + dot(ah, gl, t) + dot(al, gh, t)

    def lat_triple(x):
        return split(lanes_cat(north(x), x, south(x)))

    def conv_back(hi, lo, ranges, weights):
        wider = [(a, b + 2 * L) for a, b in ranges]
        gh, gl = rows_of(hi, wider), rows_of(lo, wider)
        wide = dot(lanes_cat(gh, gl, gh), weights)
        outs, at = [], 0
        for a, b in ranges:
            n = b - a
            outs.append(
                wide[at + 2 * L : at + 2 * L + n, :ch]
                + wide[at + L : at + L + n, ch : 2 * ch]
                + wide[at : at + n, 2 * ch :]
            )
            at += n + 2 * L
        return outs

    def add_conv_grad(base, ah, al, gh, gl):
        for j in range(3):
            part = rows_product(
                ah[j * L : j * L + R], al[j * L : j * L + R], gh, gl
            )
            for i in range(3):
                at = base + (i * 3 + j) * ch
                gw[at : at + ch, :] += part[:, i * ch : (i + 1) * ch]

    lift_base, conv_base = 0, 9 * ch
    qkv_base = 27 * ch
    out_base, head_base = 30 * ch, 31 * ch

    all_rows = gw.shape[0]
    unit = 8 * nd
    minor, batch_parts = factors(nl, 2), factors(nb, 4)
    axes = [("lon", n) for n in minor] + [("batch", n) for n in batch_parts]
    steps = {"lon": 1, "batch": 1}
    members = []
    for axis, n in axes:
        mine = me_l if axis == "lon" else me_b
        members.append((axis, steps[axis], n, lax.rem(mine // steps[axis], n)))
        steps[axis] *= n
    def stage_of(member):
        axis, step, n, idx = member

        def device_of(q):
            shift = (q - idx) * step
            if axis == "lon":
                return (me_l + shift, me_b)
            return (me_l, me_b + shift)

        return n, idx, device_of

    first, rest = members[:1], members[1:]
    orders = {
        "A": first + rest,
        "B": first + rest[1::-1] + rest[2:],
        "C": first + rest[::-1],
    }

    def rows_at(at, n):
        return pl.ds(pl.multiple_of(at, 8), n)

    class Job:
        def __init__(self, number, base, size, order):
            self.number = number
            self.stages = stages = [stage_of(m) for m in orders[order]]
            self.regions = []
            off, slot = base, base
            for n, idx, _ in stages:
                part = size // n
                self.regions.append((off, part, slot))
                off = off + idx * part
                slot += (n - 1) * part
                size = part
            self.own, self.size = off, size
            self.done, self.todo = 0, list(self.moves())

        def scatter_start(self, t):
            n, idx, device_of = self.stages[t]
            off, part, slot = self.regions[t]
            for k in range(1, n):
                q = lax.rem(idx + k, n)
                pltpu.make_async_remote_copy(
                    gw.at[rows_at(off + q * part, part)],
                    rsb.at[pl.ds(slot + (n - 1 - k) * part, part)],
                    rs_send.at[self.number, t],
                    rs_recv.at[self.number, t],
                    device_id=device_of(q),
                    device_id_type=MESH,
                ).start()

        def scatter_finish(self, t):
            n, idx, _ = self.stages[t]
            off, part, slot = self.regions[t]
            got = rsb.at[pl.ds(slot, (n - 1) * part)]
            pltpu.make_async_copy(got, got, rs_recv.at[self.number, t]).wait()
            pltpu.make_async_copy(got, got, rs_send.at[self.number, t]).wait()
            mine = off + idx * part
            chunk = math.gcd(part, 128)

            def add(i, c):
                at = pl.multiple_of(i * chunk, 8)
                total = gw[rows_at(mine + at, chunk)]
                for k in range(n - 1):
                    total = total + rsb[rows_at(slot + k * part + at, chunk)]
                gw[rows_at(mine + at, chunk)] = total
                return c

            lax.fori_loop(0, part // chunk, add, 0)

        def gather_start(self, t):
            n, idx, device_of = self.stages[t]
            off, part, _ = self.regions[t]
            if t == len(self.stages) - 1:
                all_out[rows_at(self.own, self.size)] = gw[
                    rows_at(self.own, self.size)
                ]
            mine = all_out.at[rows_at(off + idx * part, part)]
            for k in range(1, n):
                pltpu.make_async_remote_copy(
                    mine,
                    mine,
                    ag_send.at[self.number, t],
                    ag_recv.at[self.number, t],
                    device_id=device_of(lax.rem(idx + k, n)),
                    device_id_type=MESH,
                ).start()

        def gather_finish(self, t):
            n, _, _ = self.stages[t]
            _, part, slot = self.regions[t]
            got = rsb.at[pl.ds(slot, (n - 1) * part)]
            pltpu.make_async_copy(got, got, ag_recv.at[self.number, t]).wait()
            pltpu.make_async_copy(got, got, ag_send.at[self.number, t]).wait()

        def moves(self):
            for t in range(len(self.stages)):
                yield partial(self.scatter_start, t)
                yield partial(self.scatter_finish, t)
            for t in reversed(range(len(self.stages))):
                yield partial(self.gather_start, t)
                yield partial(self.gather_finish, t)

    def take_steps(job, n):
        for _ in range(n):
            job.done += 1
            job.todo[job.done - 1]()

    def drain(jobs):
        while any(job.done < len(job.todo) for job in jobs):
            for job in jobs:
                left_over = len(job.todo) - job.done
                take_steps(job, min(left_over, 1 + (job.done % 2 and left_over > 1)))

    jobs, late, middle, early = [], [], [], []
    for k, (base, size, order, kind) in enumerate(job_plan(all_rows, unit)):
        jobs.append(Job(k, base, size, order))
        (late, middle, early)[kind].append(jobs[-1])
    points = (
        ((early, 1),),
        ((early, 2),),
        ((middle, 1),),
        ((early, 2), (middle, 2)),
        ((late, 1),),
        ((late, 2),),
    )

    def advance(k):
        for some, n in points[k]:
            for job in some:
                take_steps(job, n)

    at_f, at_v, at_cf, at_cv, at_m = (
        k * VARS for k in (0, 1, 3, 4, 6)
    )
    loads = [
        (fields_in, planes.at[at_f * W : at_v * W]),
        (velocity_in, planes.at[at_v * W : at_cf * W]),
        (cot_fields_in, planes.at[at_cf * W : at_cv * W]),
        (cot_velocity_in, planes.at[at_cv * W : at_m * W]),
        (masks_in, mask_plane),
        (context_in, context_ref),
        (lift_in, lift_ref),
        (conv_in, conv_ref),
        (qkv_in, qkv_ref),
        (out_in, out_ref),
        (head_in, head_ref),
        (window_in, window_ref),
    ]
    loads = [
        pltpu.make_async_copy(src, dst, load_sems.at[k])
        for k, (src, dst) in enumerate(loads)
    ]
    for load in loads:
        load.start()
    planes[(at_m + 1) * W :] = jnp.zeros((W, L), f32)
    for load in loads[:6]:
        load.wait()
    planes[at_m * W : (at_m + 1) * W] = mask_plane[...].astype(f32)
    cots = []
    masks_own = []
    for col in range(W):
        at = 2 * L + col * L
        x = planes[pl.ds(col, at_m + 2, stride=W), :].T
        ys[0, at : at + L] = jnp.zeros((L, ch), f32)
        for k in range(3):
            ys[0, at : at + L, k * VARS : (k + 1) * VARS] = x[:, at_f:at_v]
            gk[0, at - 2 * L : at - L, k * VARS : (k + 1) * VARS] = x[:, at_cf:at_cv]
        ys[0, at : at + L, 3 * VARS : 5 * VARS] = x[:, at_v:at_cf]
        gk[0, at - 2 * L : at - L, 3 * VARS : 5 * VARS] = x[:, at_cv:at_m]
        gk[0, at - 2 * L : at - L, 5 * VARS :] = jnp.zeros((L, ch - 5 * VARS), f32)
        ys[0, at : at + L, 5 * VARS : 5 * VARS + context_ref.shape[1]] = context_ref[
            pl.ds(col, L, stride=W), :
        ]
        ys[0, at : at + L, MASK_LANE:] = x[:, at_m : at_m + 1]
    cot = gk[0]
    mask_own = jnp.broadcast_to(
        ys[0, 2 * L : 2 * L + R, MASK_LANE : MASK_LANE + 1], (R, LANES)
    )
    count_part = jnp.sum(mask_own, axis=0, keepdims=True)
    for load in loads[6:8]:
        load.wait()

    tap[...] = jnp.zeros_like(tap)
    for b in range(3):
        for i in range(3):
            for j in range(3):
                if b == 0:
                    tap[: lift_ref.shape[2]] = lift_ref[i, j]
                    w = tap[...]
                else:
                    w = conv_ref[b - 1, i, j]
                hi, lo = split(w)
                for p, part in enumerate((hi, hi, lo)):
                    at = (p * 3 + j) * ch
                    w3f[b, at : at + ch, i * ch : (i + 1) * ch] = part
                hi, lo = split(w.T)
                for p, part in enumerate((hi, hi, lo)):
                    at = (p * 3 + i) * ch
                    w3t[b, at : at + ch, j * ch : (j + 1) * ch] = part

    pl.semaphore_wait(barrier, nd - 1)
    halo_start(0, ys, 0, 2)
    sum_start(4 * SECTIONS, jnp.concatenate([count_part, count_part], axis=0))

    def square(hi, lo):
        return jnp.concatenate(
            [lanes_cat(hi, lo), lanes_cat(hi, jnp.zeros_like(hi))], axis=0
        )

    def put_square(target, w):
        n, m = w.shape
        hi, lo = split(w)
        target[:n, :m] = hi
        target[:n, m:] = lo
        target[n:, :m] = hi
        target[n:, m:] = jnp.zeros_like(hi)

    for load in loads[8:]:
        load.wait()
    put_square(wq3, qkv_ref[...])
    put_square(wqt3, qkv_ref[...].T)
    put_square(wo3, out_ref[...])
    put_square(wot3, out_ref[...].T)
    tap[...] = jnp.zeros_like(tap)
    tap[3 * VARS : 5 * VARS] = head_ref[...]
    put_square(wht3, tap[...])
    put_square(wh3, tap[...].T)
    head_bias_row[...] = jnp.zeros_like(head_bias_row)
    head_bias_row[:, 3 * VARS : 5 * VARS] = head_bias_ref[...]
    for s, weight in enumerate((1.0, 2.0, 2.0, 1.0)):
        gk[s] = cot * (weight * step_size / 6.0)
    grad_ref[...] = cot
    acc[...] = jnp.zeros_like(acc)
    gw[...] = jnp.zeros_like(gw)
    norm_acc[...] = jnp.zeros_like(norm_acc)
    bias_acc[...] = jnp.zeros_like(bias_acc)

    pair = 2 * L
    shape = (2 * pair, HEADS * pair)
    key_of = lax.broadcasted_iota(jnp.int32, shape, 0)
    key_of = key_of - lax.broadcasted_iota(jnp.int32, shape, 1) // L % 2 * L
    for p in range(W // 2):
        entries = lanes_cat(*[window_ref[2 * p], window_ref[2 * p + 1]] * HEADS)
        counted = jnp.zeros(shape, f32)
        for k in range(entries.shape[0]):
            counted = counted + jnp.where(entries[k : k + 1] == key_of, 1.0, 0.0)
        mult[p] = jnp.where(
            counted > 0.0, jnp.log(jnp.maximum(counted, 1.0)), -1e30
        )

    head_rows = lax.broadcasted_iota(jnp.int32, (HEADS * pair, ch), 0) // pair
    head_lanes = lax.broadcasted_iota(jnp.int32, (HEADS * pair, ch), 1) // (ch // HEADS)
    head_mask = jnp.where(head_rows == head_lanes, 1.0, 0.0)
    head_mask_h = head_mask.astype(bf16)
    scale = (ch // HEADS) ** -0.5

    def per_head(x):
        return jnp.concatenate([x] * HEADS, axis=0) * head_mask_h

    def heads_sum(x):
        x = x * head_mask
        return sum(x[h * pair : (h + 1) * pair] for h in range(1, HEADS)) + x[:pair]

    lift_bias = lift_bias_ref[...]
    head_bias = head_bias_row[...]
    gains = [gain_ref[0:1], gain_ref[1:2]]
    shifts = [shift_ref[0:1], shift_ref[1:2]]

    def stats(h, ranges):
        weighted = h * rows_of(mask, ranges, 2 * L)
        return jnp.concatenate(
            [
                jnp.sum(weighted, axis=0, keepdims=True),
                jnp.sum(weighted * h, axis=0, keepdims=True),
            ],
            axis=0,
        )

    def normalise(s, b, sums):
        total_count = count[0:1]
        average = sums[0:1] / total_count
        spread = sums[1:2] / total_count - average * average
        inverse = lax.rsqrt(spread + epsilon)
        norms[s, b, 0:1] = average
        norms[s, b, 1:2] = inverse
        return average, inverse

    def activity(h, b, average, inverse):
        z = (h - average) * inverse * gains[b] + shifts[b]
        below = 0.5 * (1.0 + lax.erf(z * (0.5**0.5)))
        slope = below + z * (
            jnp.exp(-0.5 * z * z) * (1.0 / math.sqrt(2.0 * math.pi))
        )
        return z * below, slope

    last = W // 2 - 1
    all_own = [(0, R)]
    own_edges, own_inner = [(0, pair), (R - pair, R)], [(pair, R - pair)]

    def forward(s, carry):
        hb = s * 6
        ext = 2 * pair

        def lift(ranges):
            value = conv(xh.at[s], xl.at[s], ranges, w3f[0]) + lift_bias
            put_rows(h0.at[s], value, ranges, 2 * L)
            return stats(value, ranges)

        def lay(a, b):
            y = ys[s, L + a : L + b]
            lane = lane_of(b - a)
            lon = 0.5 * (ys[s, 2 * L + a : 2 * L + b] - ys[s, a:b])
            x = jnp.where(
                (lane >= VARS) & (lane < 2 * VARS),
                lat_diff(y),
                jnp.where((lane >= 2 * VARS) & (lane < 3 * VARS), lon, y),
            )
            hi, lo = split(x)
            xh[s, a:b] = hi
            xl[s, a:b] = lo

        @pl.when(s == 0)
        def _():
            halo_wait(hb, ys, s, 2)
            mask[...] = jnp.broadcast_to(
                ys[0, :, MASK_LANE : MASK_LANE + 1], (R2, LANES)
            )

        lay(pair, R1 - pair)
        sums = lift(own_inner)
        pl.when(s > 0)(lambda: halo_wait(hb, ys, s, 2))
        lay(0, pair)
        lay(R1 - pair, R1)
        sum_start(s * 4, sums + lift(own_edges))
        halo_start(hb + 1, h0, s, 2)
        y1 = ys[s, L : L + R1]
        lane = lane_of(R1)
        flux = y1 * lroll(y1, -3 * VARS)
        flux = jnp.where(lane < 2 * VARS, flux, 0.0)
        own_lane = lane_of(R)
        t_lat = jnp.where(own_lane < VARS, lat_diff(flux[L : L + R]), 0.0)
        t_lon = jnp.where(
            own_lane >= VARS, 0.5 * (flux[2 * L : 2 * L + R] - flux[:R]), 0.0
        )
        t = -(t_lat + lroll(t_lon, -VARS))
        tend[...] = t + lroll(t, VARS) + lroll(t, 2 * VARS)

        @pl.when(s == 0)
        def _():
            count[...] = sum_wait(4 * SECTIONS)

        average, inverse = normalise(s, 0, sum_wait(s * 4))
        halo_wait(hb + 1, h0, s, 2)
        act, slope = activity(h0[s, L : L + R1], 0, average, inverse)
        dg1[s] = slope[L : L + R]
        hi, lo = split(act)
        a1h[s] = hi
        a1l[s] = lo
        second = h0[s, 2 * L : 2 * L + R] + conv(
            a1h.at[s], a1l.at[s], all_own, w3f[1]
        )
        h1[s, 2 * L : 2 * L + R] = second
        sum_start(s * 4 + 1, stats(second, all_own))
        halo_start(hb + 2, h1, s, 2)
        average, inverse = normalise(s, 1, sum_wait(s * 4 + 1))
        halo_wait(hb + 2, h1, s, 2)
        act, slope = activity(h1[s], 1, average, inverse)
        dg2[s] = slope[2 * L : 2 * L + R]
        hi, lo = split(act)
        a2h[s] = hi
        a2l[s] = lo

        def second_block(ranges):
            third = rows_of(h1.at[s], ranges, L) + conv(
                a2h.at[s], a2l.at[s], ranges, w3f[2]
            )
            put_rows(h2, third, ranges)
            hi, lo = split(third)
            put_rows(h2h.at[s], hi, ranges)
            put_rows(h2l.at[s], lo, ranges)
            mixing = product(hi, lo, wq3[...])
            hi, lo = split(mixing[:, :ch] * scale)
            put_rows(qh.at[s], hi, ranges)
            put_rows(ql.at[s], lo, ranges)
            hi, lo = split(mixing[:, ch : 2 * ch])
            put_rows(kh.at[s], hi, ranges)
            put_rows(kl.at[s], lo, ranges)
            hi, lo = split(mixing[:, 2 * ch :])
            put_rows(vh.at[s], hi, ranges)
            put_rows(vl.at[s], lo, ranges)

        def attend(pairs):
            scores = []
            for p in pairs:
                at = p * pair
                q_h = per_head(qh[s, at + L : at + L + pair])
                q_l = per_head(ql[s, at + L : at + L + pair])
                k_h = kh[s, at : at + ext]
                k_l = kl[s, at : at + ext]
                scores.append(
                    dot(
                        lanes_cat(k_h, k_l, k_h),
                        lanes_cat(q_h, q_h, q_l),
                        ((1,), (1,)),
                    )
                )
            weights = []
            for p, score in zip(pairs, scores):
                score = score + mult[p]
                e = jnp.exp(score - jnp.max(score, axis=0, keepdims=True))
                e = e * (1.0 / jnp.sum(e, axis=0, keepdims=True))
                probs[s, p] = e
                weights.append(e)
            for p, e in zip(pairs, weights):
                at = p * pair
                p_h, p_l = split(e.T)
                v_h = vh[s, at : at + ext]
                v_l = vl[s, at : at + ext]
                o = product(p_h, p_l, square(v_h, v_l))
                blend[at : at + pair] = heads_sum(o)

        weight = jnp.where((s == 0) | (s == SECTIONS - 1), 1.0, 2.0)
        factor = jnp.where(s == SECTIONS - 2, 1.0, 0.5) * step_size

        def finish(ranges):
            hi, lo = split(rows_of(blend, ranges))
            put_rows(bh.at[s], hi, ranges)
            put_rows(bl.at[s], lo, ranges)
            fourth = rows_of(h2, ranges, L) + product(hi, lo, wo3[...])
            hi, lo = split(fourth)
            put_rows(h3h.at[s], hi, ranges)
            put_rows(h3l.at[s], lo, ranges)
            slope_now = (
                rows_of(tend, ranges)
                + product(hi, lo, wh3[...])
                + head_bias
            )
            put_rows(acc, rows_of(acc, ranges) + weight * slope_now, ranges)
            put_rows(
                ys.at[s + 1],
                rows_of(ys.at[0], ranges, 2 * L) + factor * slope_now,
                ranges,
                2 * L,
            )

        second_block([(0, ext), (R1 - ext, R1)])
        attend([0, last])
        finish(own_edges)

        @pl.when(s < SECTIONS - 1)
        def _():
            halo_start(hb + 6, ys, s + 1, 2)

        second_block([(ext, R1 - ext)])
        attend(range(1, last))
        finish(own_inner)
        return carry

    lax.fori_loop(0, SECTIONS, forward, 0)
    acc[...] = ys[0, 2 * L : 2 * L + R] + (step_size / 6.0) * acc[...]

    def norm_back(s, b, h, grad_act, slope, through):
        average = norms[s, b, 0:1]
        inverse = norms[s, b, 1:2]
        dz = grad_act * slope
        hat = (h - average) * inverse
        sums = jnp.concatenate(
            [
                jnp.sum(dz, axis=0, keepdims=True),
                jnp.sum(dz * hat, axis=0, keepdims=True),
            ],
            axis=0,
        )
        return sums, through + dz * (gains[b] * inverse)

    def norm_rest(s, b, h, weight_mask, direct, sums):
        average = norms[s, b, 0:1]
        inverse = norms[s, b, 1:2]
        hat = (h - average) * inverse
        norm_acc[b] += sums
        return direct - weight_mask * (
            gains[b] * inverse / count[0:1]
        ) * (sums[0:1] + hat * sums[1:2])

    def backward(turn, carry):
        s = SECTIONS - 1 - turn
        hb = s * 6
        g_h, g_l = split(gk[s])
        gh[...] = g_h
        gl[...] = g_l
        dqkv[...] = jnp.zeros_like(dqkv)

        def head_back(ranges):
            hi, lo = rows_of(gh, ranges), rows_of(gl, ranges)
            grad3 = product(hi, lo, wht3[...])
            hi, lo = split(grad3)
            put_rows(dh2, grad3, ranges, L)
            put_rows(dh3h, hi, ranges)
            put_rows(dh3l, lo, ranges)
            hi, lo = split(product(hi, lo, wot3[...]))
            put_rows(dbh, hi, ranges)
            put_rows(dbl, lo, ranges)

        def attend_back(pairs):
            dps = []
            for p in pairs:
                at = p * pair
                d_h = per_head(dbh[pl.ds(at, pair)])
                d_l = per_head(dbl[pl.ds(at, pair)])
                v_h = vh[s, pl.ds(at, 2 * pair)]
                v_l = vl[s, pl.ds(at, 2 * pair)]
                dps.append(
                    dot(
                        lanes_cat(v_h, v_l, v_h),
                        lanes_cat(d_h, d_h, d_l),
                        ((1,), (1,)),
                    )
                )
            dss = []
            for p, dp in zip(pairs, dps):
                e = probs[s, p]
                dss.append(e * (dp - jnp.sum(e * dp, axis=0, keepdims=True)))
            for p, ds in zip(pairs, dss):
                at = p * pair
                k_h = kh[s, pl.ds(at, 2 * pair)]
                k_l = kl[s, pl.ds(at, 2 * pair)]
                t_h, t_l = split(ds.T)
                o = product(t_h, t_l, square(k_h, k_l))
                dqkv[pl.ds(at + L, pair), :ch] = heads_sum(o) * scale
                q_h = per_head(qh[s, at + L : at + L + pair])
                q_l = per_head(ql[s, at + L : at + L + pair])
                s_h, s_l = split(ds)
                o = dot(s_h, lanes_cat(q_h, q_l))
                o = o[:, :ch] + o[:, ch:] + dot(s_l, q_h)
                dqkv[pl.ds(at, 2 * pair), ch : 2 * ch] += o
                d_h = per_head(dbh[pl.ds(at, pair)])
                d_l = per_head(dbl[pl.ds(at, pair)])
                s_h, s_l = split(probs[s, p])
                o = dot(s_h, lanes_cat(d_h, d_l))
                o = o[:, :ch] + o[:, ch:] + dot(s_l, d_h)
                dqkv[pl.ds(at, 2 * pair), 2 * ch :] += o

        def to_hidden(ranges):
            hi, lo = split(rows_of(dqkv, ranges))
            part = product(hi, lo, wqt3[...])
            put_rows(dh2, rows_of(dh2, ranges) + part, ranges)

        def triple(ranges):
            hi, lo = lat_triple(rows_of(dh2, ranges))
            put_rows(th, hi, ranges)
            put_rows(tl, lo, ranges)

        dh2[:L] = jnp.zeros((L, ch), f32)
        dh2[R1 - L :] = jnp.zeros((L, ch), f32)
        head_back(own_edges)
        attend_back([0, last])
        border = [(0, pair), (R1 - pair, R1)]
        to_hidden(border)
        for side, (a, b) in enumerate(border):
            sb[s, side, :pair] = dh2[a:b]
        sb[s, 0, pair:] = gk[s, :L]
        sb[s, 1, pair:] = gk[s, R - L :]
        edges = [
            side_copy(hb + 3, side, sb.at[s, side], rb.at[s, side])
            for side in range(2)
        ]
        for e in edges:
            e.start()
        head_back(own_inner)
        attend_back(range(1, last))
        to_hidden([(pair, R1 - pair)])
        triple([(pair, R1 - pair)])
        (inner_act,) = conv_back(th, tl, own_inner, w3t[2])
        bias_acc[1:2] += jnp.sum(gk[s], axis=0, keepdims=True)
        gw[head_base : head_base + ch] += rows_product(
            h3h[s], h3l[s], gh[...], gl[...]
        )
        for e in edges:
            e.wait()
        dh2[:pair] += rb[s, 1, :pair]
        dh2[R1 - pair :] += rb[s, 0, :pair]
        triple(border)
        low_act, high_act = conv_back(th, tl, own_edges, w3t[2])

        grad_act = jnp.concatenate([low_act, inner_act, high_act], axis=0)
        sums, direct = norm_back(
            s, 1, h1[s, 2 * L : 2 * L + R], grad_act, dg2[s], dh2[L : L + R]
        )
        sum_start(s * 4 + 2, sums)
        de1[s, 2 * L : 2 * L + R] = direct
        halo_start(hb + 4, de1, s, 1)
        gw[out_base : out_base + ch] += rows_product(
            bh[s], bl[s], dh3h[...], dh3l[...]
        )
        d_h, d_l = split(dqkv[...])
        wide = rows_product(h2h[s], h2l[s], d_h, d_l)
        for k in range(3):
            at = qkv_base + k * ch
            gw[at : at + ch] += wide[:, k * ch : (k + 1) * ch]
        add_conv_grad(
            conv_base + 9 * ch,
            a2h[s, L : L + R1],
            a2l[s, L : L + R1],
            th[L : L + R],
            tl[L : L + R],
        )
        pl.when(s == 0)(lambda: advance(0))
        sums = sum_wait(s * 4 + 2)
        halo_wait(hb + 4, de1, s, 1)
        pl.when(s == 0)(lambda: advance(1))
        grad1 = norm_rest(
            s, 1, h1[s, L : L + R1], mask[L : L + R1], de1[s, L : L + R1], sums
        )
        t_h, t_l = lat_triple(grad1)
        (grad_act,) = conv_back(t_h, t_l, all_own, w3t[1])
        sums, direct = norm_back(
            s, 0, h0[s, 2 * L : 2 * L + R], grad_act, dg1[s], grad1[L : L + R]
        )
        sum_start(s * 4 + 3, sums)
        de0[s, 2 * L : 2 * L + R] = direct
        halo_start(hb + 5, de0, s, 2)
        add_conv_grad(
            conv_base, a1h[s], a1l[s], t_h[L : L + R], t_l[L : L + R]
        )

        def lift_grad(s):
            add_conv_grad(lift_base, xh[s], xl[s], lift_th[...], lift_tl[...])

        pl.when(s < SECTIONS - 1)(lambda: lift_grad(s + 1))
        pl.when(s == 0)(lambda: advance(2))
        sums = sum_wait(s * 4 + 3)
        halo_wait(hb + 5, de0, s, 2)

        @pl.when(s == 0)
        def _():
            advance(3)

        grad0 = norm_rest(s, 0, h0[s], mask[...], de0[s], sums)
        bias_acc[0:1] += jnp.sum(grad0[2 * L : 2 * L + R], axis=0, keepdims=True)
        t_h, t_l = lat_triple(grad0)
        lift_th[...] = t_h[2 * L : 2 * L + R]
        lift_tl[...] = t_l[2 * L : 2 * L + R]

        @pl.when(s == 0)
        def _():
            lift_grad(s)
            gw[ch - 28 : ch - 26] = bias_acc[...]
            advance(4)

        (dx,) = conv_back(t_h, t_l, [(0, R1)], w3t[0])
        lane = lane_of(R)
        own = dx[L : L + R]
        lon = 0.5 * (dx[2 * L :] - dx[:R])
        g = gk[s]
        g_lon = jnp.concatenate([g[L:], rb[s, 0, 2 * L :]], axis=0)
        g_lon = 0.5 * (
            g_lon - jnp.concatenate([rb[s, 1, 2 * L :], g[: R - L]], axis=0)
        )
        dflux = jnp.where(
            lane < VARS, lat_diff(g), jnp.where(lane < 2 * VARS, g_lon, 0.0)
        )
        y = ys[s, 2 * L : 2 * L + R]
        parts = jnp.where(
            lane < VARS,
            own,
            jnp.where(lane < 2 * VARS, -lat_diff(own), -lon),
        )
        parts = parts + dflux * lroll(y, -3 * VARS)
        parts = jnp.where(lane < 3 * VARS, parts, 0.0)
        fields_grad = (
            parts
            + lroll(parts, VARS)
            + lroll(parts, 2 * VARS)
            + lroll(parts, -VARS)
            + lroll(parts, -2 * VARS)
        )
        velocity_grad = own + lroll(dflux * y, 3 * VARS)
        gy = jnp.where(
            lane < 3 * VARS,
            fields_grad,
            jnp.where(lane < 5 * VARS, velocity_grad, 0.0),
        )
        grad_ref[...] += gy

        @pl.when(s > 0)
        def _():
            factor = jnp.where(s == SECTIONS - 1, 1.0, 0.5) * step_size
            gk[s - 1] = gk[s - 1] + factor * gy

        return carry

    lax.fori_loop(0, SECTIONS, backward, 0)

    advance(5)
    all_out[gw.shape[0] : gw.shape[0] + 4] = norm_acc[...].reshape(4, ch)
    lane = lane_of(R)
    new, grad = acc[...], grad_ref[...]
    merged = jnp.where(
        lane < at_v,
        new,
        jnp.where(
            lane < at_cf,
            lroll(new, at_v - 3 * VARS),
            jnp.where(
                lane < at_cv, lroll(grad, at_cf), lroll(grad, at_cv - 3 * VARS)
            ),
        ),
    )
    for col in range(W):
        x = merged[col * L : (col + 1) * L].T
        all_out[pl.ds(gw.shape[0] + 8 + col, at_m, stride=W), :] = lanes_cat(
            x[:at_m], jnp.zeros((at_m, ch - L), f32)
        )

    drain(jobs)


def hand_out(rows, weights, *outs):
    fields = outs[:4]
    lift, lift_bias, gain, shift, conv, qkv, out, head, head_bias = outs[4:]
    ch = LANES
    at = rows + 8
    for ref in fields:
        ref[...] = weights[at : at + ref.shape[0], : ref.shape[1]]
        at += ref.shape[0]
    cin = lift.shape[2]
    vel = slice(3 * VARS, 5 * VARS)
    for i in range(3):
        for j in range(3):
            at = (i * 3 + j) * ch
            lift[i, j] = weights[at : at + cin]
            for b in range(2):
                at_conv = at + (b + 1) * 9 * ch
                conv[b, i, j] = weights[at_conv : at_conv + ch]
    lift_bias[...] = weights[cin : cin + 1]
    head_bias[...] = weights[cin + 1 : cin + 2, vel]
    for b in range(2):
        at = rows + 2 * b
        shift[b : b + 1] = weights[at : at + 1]
        gain[b : b + 1] = weights[at + 1 : at + 2]
    for k in range(3):
        at = (27 + k) * ch
        qkv[:, k * ch : (k + 1) * ch] = weights[at : at + ch]
    out[...] = weights[30 * ch : 31 * ch]
    head[...] = weights[31 * ch : 32 * ch].T[vel]


def on_device(
    nl,
    nb,
    fields,
    velocity,
    context,
    masks,
    window,
    lift_weight,
    lift_bias,
    norm_gain,
    norm_shift,
    conv_weight,
    attn_qkv,
    attn_out,
    head_weight,
    head_bias,
    cot_fields,
    cot_velocity,
):
    _, L, W, _ = fields.shape
    R, R1, R2 = L * W, L * (W + 2), L * (W + 4)
    ch = LANES
    nd = nl * nb

    def flat(x):
        return x[0].transpose(2, 1, 0).reshape(-1, L)

    S = SECTIONS
    rows = 32 * ch
    rows = -(-rows // (8 * nd)) * 8 * nd
    stage_count = len(factors(nl, 2)) + len(factors(nb, 4))
    job_count = len(job_plan(rows, 8 * nd))
    vm = pltpu.VMEM
    dma = pltpu.SemaphoreType.DMA
    scratch = [
        vm((S + 1, R2, ch), f32),
        vm((S, R1, ch), bf16),
        vm((S, R1, ch), bf16),
        vm((S, R2, ch), f32),
        vm((S, R2, ch), f32),
        vm((S, R1, ch), bf16),
        vm((S, R1, ch), bf16),
        vm((S, R2, ch), bf16),
        vm((S, R2, ch), bf16),
        vm((S, R, ch), f32),
        vm((S, R, ch), f32),
        vm((S, R1, ch), bf16),
        vm((S, R1, ch), bf16),
        vm((S, R1, ch), bf16),
        vm((S, R1, ch), bf16),
        vm((S, R1, ch), bf16),
        vm((S, R1, ch), bf16),
        vm((S, R1, ch), bf16),
        vm((S, R1, ch), bf16),
        vm((S, W // 2, 4 * L, 2 * HEADS * L), f32),
        vm((S, R, ch), bf16),
        vm((S, R, ch), bf16),
        vm((S, R, ch), bf16),
        vm((S, R, ch), bf16),
        vm((S, 2, 8, ch), f32),
        vm((S, R, ch), f32),
        vm((R, ch), f32),
        vm((R, ch), f32),
        vm((R2, ch), f32),
        vm((W // 2, 4 * L, 2 * HEADS * L), f32),
        vm((3, 9 * ch, 3 * ch), bf16),
        vm((3, 9 * ch, 3 * ch), bf16),
        vm((2 * ch, 6 * ch), bf16),
        vm((6 * ch, 2 * ch), bf16),
        vm((2 * ch, 2 * ch), bf16),
        vm((2 * ch, 2 * ch), bf16),
        vm((2 * ch, 2 * ch), bf16),
        vm((2 * ch, 2 * ch), bf16),
        vm((ch, ch), f32),
        vm((R, ch), f32),
        vm((R, ch), bf16),
        vm((R, ch), bf16),
        vm((R, ch), bf16),
        vm((R, ch), bf16),
        vm((R, ch), bf16),
        vm((R, ch), bf16),
        vm((R1, 3 * ch), bf16),
        vm((R1, 3 * ch), bf16),
        vm((R, 3 * ch), bf16),
        vm((R, 3 * ch), bf16),
        vm((R1, 3 * ch), f32),
        vm((R1, ch), f32),
        vm((R1, ch), f32),
        vm((2, ch), f32),
        vm((S, R2, ch), f32),
        vm((S, R2, ch), f32),
        vm((S, 2, 3 * L, ch), f32),
        vm((S, 2, 3 * L, ch), f32),
        vm((rows, ch), f32),
        vm((rows, ch), f32),
        vm((2, 2, ch), f32),
        vm((2, ch), f32),
        vm((32 * W, L), f32),
        vm((W, L), jnp.int32),
        vm((R, context.shape[-1]), f32),
        vm((W, window.shape[-1], L), jnp.int32),
        vm(lift_weight.shape, f32),
        vm(conv_weight.shape, f32),
        vm(attn_qkv.shape, f32),
        vm(attn_out.shape, f32),
        vm(head_weight.shape[::-1], f32),
        vm((1, ch), f32),
        vm((R, ch), f32),
        dma((12,)),
        vm((4 * S + 1, 2, ch), f32),
        vm((4 * S + 1, nd, 2, ch), f32),
        dma((4 * S + 1,)),
        dma((4 * S + 1,)),
        dma((6 * S, 2)),
        dma((6 * S, 2)),
        dma((job_count, stage_count)),
        dma((job_count, stage_count)),
        dma((job_count, stage_count)),
        dma((job_count, stage_count)),
    ]
    whole = pl.BlockSpec(memory_space=pltpu.VMEM)
    apart = pl.BlockSpec(memory_space=pl.ANY)
    results = pl.pallas_call(
        partial(kernel, (nl, nb, L, W, HEADS)),
        out_shape=jax.ShapeDtypeStruct((rows + 8 + 6 * VARS * W, ch), f32),
        in_specs=[apart] * 12 + [whole] * 4,
        out_specs=whole,
        scratch_shapes=scratch,
        compiler_params=pltpu.CompilerParams(
            collective_id=0, has_side_effects=True, vmem_limit_bytes=60 * 2**20
        ),
    )(
        flat(fields),
        flat(velocity),
        flat(cot_fields),
        flat(cot_velocity),
        masks[0].T,
        context.reshape(R, -1),
        window.transpose(1, 2, 0),
        lift_weight,
        conv_weight,
        attn_qkv,
        attn_out,
        head_weight.T,
        lift_bias[None],
        head_bias[None],
        norm_gain,
        norm_shift,
    )
    pixels = VARS * W
    shapes = (
        (pixels, L),
        (2 * pixels, L),
        (pixels, L),
        (2 * pixels, L),
        lift_weight.shape,
        (1, ch),
        norm_gain.shape,
        norm_shift.shape,
        conv_weight.shape,
        attn_qkv.shape,
        attn_out.shape,
        head_weight.shape[::-1],
        (1, head_bias.shape[0]),
    )
    outs = pl.pallas_call(
        partial(hand_out, rows),
        out_shape=tuple(jax.ShapeDtypeStruct(shape, f32) for shape in shapes),
        in_specs=[whole],
        out_specs=(whole,) * len(shapes),
        compiler_params=pltpu.CompilerParams(vmem_limit_bytes=32 * 2**20),
    )(results)

    def field(x):
        return x.reshape(-1, W, L).transpose(2, 1, 0)[None]

    return (
        *(field(x) for x in outs[:4]),
        outs[4],
        outs[5][0],
        *outs[6:11],
        outs[11].T,
        outs[12][0],
    )


def solution(mesh):
    field = P("batch", None, "lon", None)
    return jax.shard_map(
        partial(on_device, mesh.shape["lon"], mesh.shape["batch"]),
        mesh=mesh,
        in_specs=(
            field,
            field,
            field,
            P("batch", None, "lon"),
            P(None, "lon", None),
            P(),
            P(),
            P(),
            P(),
            P(),
            P(),
            P(),
            P(),
            P(),
            field,
            field,
        ),
        out_specs=(field,) * 4 + (P(),) * 9,
        check_vma=False,
    )
```

```python
from functools import partial
import math

import jax
import jax.numpy as jnp
from jax import lax
from jax.experimental import pallas as pl
from jax.experimental.pallas import tpu as pltpu
from jax.sharding import PartitionSpec as P

HEADS = 4
SECTIONS = 4
LANES = 128
VARS = 5
MASK_LANE = 127
HEAD_ROWS = 32
LIFT_BACK = 32
epsilon = 1e-05
step_size = 0.25
f32 = jnp.float32
bf16 = jnp.bfloat16
MESH = pl.DeviceIdType.MESH


def split(x):
    hi = x.astype(bf16)
    return hi, (x - hi.astype(f32)).astype(bf16)


def dot(a, b, dims=((1,), (0,))):
    return lax.dot_general(a, b, (dims, ((), ())), preferred_element_type=f32)


def lanes_cat(*parts):
    return jnp.concatenate(parts, axis=1)


def factors(n, largest):
    out = []
    while n > largest and n % 2 == 0:
        out.append(2)
        n //= 2
    if n > 1:
        out.append(n)
    return out


def tap_rows(cin):
    return -(-(cin + 2) // 8) * 8


def bases(cin):
    conv = 9 * tap_rows(cin)
    qkv = conv + 18 * LANES
    out = qkv + 3 * LANES
    return conv, qkv, out, out + LANES


def job_plan(rows, unit, cin):
    conv = bases(cin)[0]
    late = -(-conv // unit)
    middle = -(-(conv + 9 * LANES) // unit) - late
    early = rows // unit - late - middle
    sizes = []
    for kind, units in enumerate((late, middle, early)):
        half = (units + 1) // 2
        sizes += [(half, "A", kind), (units - half, "B", kind)]
    plan, at = [], 0
    for units, order, kind in sizes:
        if units:
            plan.append((at * unit, units * unit, order, kind))
        at += units
    return plan


def kernel(
    sizes,
    fields_in,
    velocity_in,
    cot_fields_in,
    cot_velocity_in,
    masks_in,
    context_in,
    window_in,
    lift_in,
    conv_in,
    qkv_in,
    out_in,
    head_in,
    lift_bias_ref,
    head_bias_ref,
    gain_ref,
    shift_ref,
    final_out,
    ys,
    xh,
    xl,
    h0,
    h1,
    a1h,
    a1l,
    a2h,
    a2l,
    dg1,
    dg2,
    h2h,
    h2l,
    qh,
    ql,
    kh,
    kl,
    vh,
    vl,
    probs,
    bh,
    bl,
    h3h,
    h3l,
    norms,
    gk,
    acc,
    tend,
    mask,
    mult,
    w3f,
    w3t,
    lift_t,
    wq3,
    wqt3,
    wo3,
    wot3,
    wh3,
    wht3,
    tap,
    blend,
    dbh,
    dbl,
    gh,
    gl,
    dh3h,
    dh3l,
    th,
    tl,
    lift_th,
    lift_tl,
    dqkv,
    dh2,
    h2,
    count,
    de1,
    de0,
    sb,
    rb,
    gw,
    rsb,
    norm_acc,
    bias_acc,
    all_out,
    out_sems,
    planes,
    mask_plane,
    context_ref,
    window_ref,
    lift_ref,
    conv_ref,
    qkv_ref,
    out_ref,
    head_ref,
    head_bias_row,
    grad_ref,
    load_sems,
    ar_src,
    ar_buf,
    ar_send,
    ar_recv,
    halo_send,
    halo_recv,
    rs_send,
    rs_recv,
    ag_send,
    ag_recv,
):
    nl, nb, L, W, hid_heads = sizes
    nd = nl * nb
    R = L * W
    R1 = R + 2 * L
    R2 = R + 4 * L
    ch = LANES
    me_l = lax.axis_index("lon")
    me_b = lax.axis_index("batch")
    me = me_l * nb + me_b
    left = (lax.rem(me_l + nl - 1, nl), me_b)
    right = (lax.rem(me_l + 1, nl), me_b)

    def peer(k):
        t = lax.rem(me + k, nd)
        return (t // nb, lax.rem(t, nb))

    low_half = 1 - me_b // max(nb // 2, 1) if nb > 1 else 0
    lon_order = sorted(range(nl), key=lambda hop: -min(hop, nl - hop))
    barrier = pltpu.get_barrier_semaphore()

    def greet(k, c):
        pl.semaphore_signal(barrier, inc=1, device_id=peer(k), device_id_type=MESH)
        return c

    lax.fori_loop(1, nd, greet, 0)

    def sum_start(a, vals):
        ar_src[a] = vals
        ar_buf[a, me] = vals

        def send(k, c):
            to_b = k + low_half * (nb - 1 - 2 * k)
            for hop in lon_order:
                copy = pltpu.make_async_remote_copy(
                    ar_src.at[a],
                    ar_buf.at[a, me],
                    ar_send.at[a],
                    ar_recv.at[a],
                    device_id=(lax.rem(me_l + hop, nl), to_b),
                    device_id_type=MESH,
                )
                if hop == 0:
                    pl.when(to_b != me_b)(copy.start)
                else:
                    copy.start()
            return c

        lax.fori_loop(0, nb, send, 0)

    def sum_wait(a):
        got = ar_buf.at[a, pl.ds(0, nd - 1)]
        pltpu.make_async_copy(got, got, ar_recv.at[a]).wait()
        pltpu.make_async_copy(got, got, ar_send.at[a]).wait()
        return jnp.sum(ar_buf[a], axis=0)

    def side_copy(h, side, src, dst):
        return pltpu.make_async_remote_copy(
            src,
            dst,
            halo_send.at[h, side],
            halo_recv.at[h, side],
            device_id=left if side == 0 else right,
            device_id_type=MESH,
        )

    def halo_copies(h, buf, s, cols):
        n = cols * L
        lo = 2 * L - n
        to_left = side_copy(
            h, 0, buf.at[s, pl.ds(2 * L, n)], buf.at[s, pl.ds(R + 2 * L, n)]
        )
        to_right = side_copy(
            h, 1, buf.at[s, pl.ds(R + 2 * L - n, n)], buf.at[s, pl.ds(lo, n)]
        )
        return to_left, to_right

    def halo_start(h, buf, s, cols):
        for c in halo_copies(h, buf, s, cols):
            c.start()

    def halo_wait(h, buf, s, cols):
        for c in halo_copies(h, buf, s, cols):
            c.wait()

    def lat_of(n):
        return lax.broadcasted_iota(jnp.int32, (n, LANES), 0) % L

    def north(x):
        n = x.shape[0]
        return jnp.where(lat_of(n) == L - 1, 0.0, pltpu.roll(x, n - 1, 0))

    def south(x):
        n = x.shape[0]
        return jnp.where(lat_of(n) == 0, 0.0, pltpu.roll(x, 1, 0))

    def lat_diff(x):
        return 0.5 * (north(x) - south(x))

    def lane_of(n):
        return lax.broadcasted_iota(jnp.int32, (n, LANES), 1)

    def lroll(x, shift):
        return pltpu.roll(x, shift % LANES, 1)

    def rows_of(ref, ranges, base=0):
        parts = [ref[base + a : base + b] for a, b in ranges]
        return parts[0] if len(parts) == 1 else jnp.concatenate(parts, axis=0)

    def put_rows(ref, value, ranges, base=0):
        at = 0
        for a, b in ranges:
            ref[base + a : base + b] = value[at : at + b - a]
            at += b - a

    def conv(hi, lo, ranges, weights):
        cols_h = [rows_of(hi, ranges, j * L) for j in range(3)]
        cols_l = [rows_of(lo, ranges, j * L) for j in range(3)]
        wide = dot(lanes_cat(*cols_h, *cols_l, *cols_h), weights)
        return (
            wide[:, ch : 2 * ch]
            + south(wide[:, :ch])
            + north(wide[:, 2 * ch :])
        )

    def product(hi, lo, weights):
        wide = dot(lanes_cat(hi, lo), weights)
        n = wide.shape[1] // 2
        return wide[:, :n] + wide[:, n:]

    def rows_product(ah, al, gh, gl):
        t = ((0,), (0,))
        return dot(ah, gh, t) + dot(ah, gl, t) + dot(al, gh, t)

    def lat_triple(x):
        return split(lanes_cat(north(x), x, south(x)))

    def conv_back(hi, lo, ranges, weights):
        wider = [(a, b + 2 * L) for a, b in ranges]
        gh, gl = rows_of(hi, wider), rows_of(lo, wider)
        wide = dot(lanes_cat(gh, gl, gh), weights)
        outs, at = [], 0
        for a, b in ranges:
            n = b - a
            outs.append(
                wide[at + 2 * L : at + 2 * L + n, :ch]
                + wide[at + L : at + L + n, ch : 2 * ch]
                + wide[at : at + n, 2 * ch :]
            )
            at += n + 2 * L
        return outs

    def add_conv_grad(base, ah, al, gh, gl, taken=ch):
        for j in range(3):
            part = rows_product(
                ah[j * L : j * L + R], al[j * L : j * L + R], gh, gl
            )
            for i in range(3):
                at = base + (i * 3 + j) * taken
                gw[at : at + taken, :] += part[:taken, i * ch : (i + 1) * ch]

    cin = lift_in.shape[2]
    conv_base, qkv_base, out_base, head_base = bases(cin)

    all_rows = gw.shape[0]
    unit = 8 * nd
    minor, batch_parts = factors(nl, 2), factors(nb, 4)
    axes = [("lon", n) for n in minor] + [("batch", n) for n in batch_parts]
    steps = {"lon": 1, "batch": 1}
    members = []
    for axis, n in axes:
        mine = me_l if axis == "lon" else me_b
        members.append((axis, steps[axis], n, lax.rem(mine // steps[axis], n)))
        steps[axis] *= n
    def stage_of(member):
        axis, step, n, idx = member

        def device_of(q):
            shift = (q - idx) * step
            if axis == "lon":
                return (me_l + shift, me_b)
            return (me_l, me_b + shift)

        return n, idx, device_of

    first, rest = members[:1], members[1:]
    orders = {
        "A": first + rest,
        "B": first + rest[1::-1] + rest[2:],
    }

    def rows_at(at, n):
        return pl.ds(pl.multiple_of(at, 8), n)

    class Job:
        def __init__(self, number, base, size, order):
            self.number = number
            self.result = pltpu.make_async_copy(
                all_out.at[base : base + size],
                final_out.at[base : base + size],
                out_sems.at[number],
            )
            self.stages = stages = [stage_of(m) for m in orders[order]]
            self.regions = []
            off, slot = base, base
            for n, idx, _ in stages:
                part = size // n
                self.regions.append((off, part, slot))
                off = off + idx * part
                slot += (n - 1) * part
                size = part
            self.own, self.size = off, size
            self.done, self.todo = 0, list(self.moves())

        def scatter_start(self, t):
            n, idx, device_of = self.stages[t]
            off, part, slot = self.regions[t]
            for k in range(1, n):
                q = lax.rem(idx + k, n)
                pltpu.make_async_remote_copy(
                    gw.at[rows_at(off + q * part, part)],
                    rsb.at[pl.ds(slot + (n - 1 - k) * part, part)],
                    rs_send.at[self.number, t],
                    rs_recv.at[self.number, t],
                    device_id=device_of(q),
                    device_id_type=MESH,
                ).start()

        def scatter_finish(self, t):
            n, idx, _ = self.stages[t]
            off, part, slot = self.regions[t]
            got = rsb.at[pl.ds(slot, (n - 1) * part)]
            pltpu.make_async_copy(got, got, rs_recv.at[self.number, t]).wait()
            pltpu.make_async_copy(got, got, rs_send.at[self.number, t]).wait()
            mine = off + idx * part
            chunk = math.gcd(part, 128)

            def add(i, c):
                at = pl.multiple_of(i * chunk, 8)
                total = gw[rows_at(mine + at, chunk)]
                for k in range(n - 1):
                    total = total + rsb[rows_at(slot + k * part + at, chunk)]
                gw[rows_at(mine + at, chunk)] = total
                return c

            lax.fori_loop(0, part // chunk, add, 0)

        def gather_start(self, t):
            n, idx, device_of = self.stages[t]
            off, part, _ = self.regions[t]
            if t == len(self.stages) - 1:
                all_out[rows_at(self.own, self.size)] = gw[
                    rows_at(self.own, self.size)
                ]
            mine = all_out.at[rows_at(off + idx * part, part)]
            for k in range(1, n):
                pltpu.make_async_remote_copy(
                    mine,
                    mine,
                    ag_send.at[self.number, t],
                    ag_recv.at[self.number, t],
                    device_id=device_of(lax.rem(idx + k, n)),
                    device_id_type=MESH,
                ).start()

        def gather_finish(self, t):
            n, _, _ = self.stages[t]
            _, part, slot = self.regions[t]
            got = rsb.at[pl.ds(slot, (n - 1) * part)]
            pltpu.make_async_copy(got, got, ag_recv.at[self.number, t]).wait()
            pltpu.make_async_copy(got, got, ag_send.at[self.number, t]).wait()

        def finished(self):
            self.gather_finish(0)
            self.result.start()

        def moves(self):
            for t in range(len(self.stages)):
                yield partial(self.scatter_start, t)
                yield partial(self.scatter_finish, t)
            for t in reversed(range(len(self.stages))):
                yield partial(self.gather_start, t)
                yield partial(self.gather_finish, t) if t else self.finished

    def take_steps(job, n):
        for _ in range(n):
            job.done += 1
            job.todo[job.done - 1]()

    def drain(jobs):
        while any(job.done < len(job.todo) for job in jobs):
            for job in jobs:
                left_over = len(job.todo) - job.done
                take_steps(job, min(left_over, 1 + (job.done % 2 and left_over > 1)))

    jobs, late, middle, early = [], [], [], []
    for k, (base, size, order, kind) in enumerate(job_plan(all_rows, unit, lift_in.shape[2])):
        jobs.append(Job(k, base, size, order))
        (late, middle, early)[kind].append(jobs[-1])
    points = (
        ((early, 1),),
        ((early, 2),),
        ((middle, 1),),
        ((early, 2), (middle, 2)),
        ((late, 1),),
        ((late, 2),),
    )

    def advance(k):
        for some, n in points[k]:
            for job in some:
                take_steps(job, n)

    at_f, at_v, at_cf, at_cv, at_m = (
        k * VARS for k in (0, 1, 3, 4, 6)
    )
    loads = [
        (fields_in, planes.at[at_f * W : at_v * W]),
        (velocity_in, planes.at[at_v * W : at_cf * W]),
        (cot_fields_in, planes.at[at_cf * W : at_cv * W]),
        (cot_velocity_in, planes.at[at_cv * W : at_m * W]),
        (masks_in, mask_plane),
        (context_in, context_ref),
        (lift_in, lift_ref),
        (conv_in, conv_ref),
        (qkv_in, qkv_ref),
        (out_in, out_ref),
        (head_in, head_ref),
        (window_in, window_ref),
    ]
    loads = [
        pltpu.make_async_copy(src, dst, load_sems.at[k])
        for k, (src, dst) in enumerate(loads)
    ]
    for load in loads:
        load.start()
    planes[(at_m + 1) * W :] = jnp.zeros((W, L), f32)
    for load in loads[:6]:
        load.wait()
    planes[at_m * W : (at_m + 1) * W] = mask_plane[...].astype(f32)
    cots = []
    masks_own = []
    for col in range(W):
        at = 2 * L + col * L
        x = planes[pl.ds(col, at_m + 2, stride=W), :].T
        ys[0, at : at + L] = jnp.zeros((L, ch), f32)
        for k in range(3):
            ys[0, at : at + L, k * VARS : (k + 1) * VARS] = x[:, at_f:at_v]
            gk[0, at - 2 * L : at - L, k * VARS : (k + 1) * VARS] = x[:, at_cf:at_cv]
        ys[0, at : at + L, 3 * VARS : 5 * VARS] = x[:, at_v:at_cf]
        gk[0, at - 2 * L : at - L, 3 * VARS : 5 * VARS] = x[:, at_cv:at_m]
        gk[0, at - 2 * L : at - L, 5 * VARS :] = jnp.zeros((L, ch - 5 * VARS), f32)
        ys[0, at : at + L, 5 * VARS : 5 * VARS + context_ref.shape[1]] = context_ref[
            pl.ds(col, L, stride=W), :
        ]
        ys[0, at : at + L, MASK_LANE:] = x[:, at_m : at_m + 1]
    cot = gk[0]
    mask_own = jnp.broadcast_to(
        ys[0, 2 * L : 2 * L + R, MASK_LANE : MASK_LANE + 1], (R, LANES)
    )
    mask[2 * L : 2 * L + R] = mask_own
    count_part = jnp.sum(mask_own, axis=0, keepdims=True)
    for load in loads[6:8]:
        load.wait()

    tap[...] = jnp.zeros_like(tap)
    lift_t[...] = jnp.zeros_like(lift_t)
    for b in range(3):
        for i in range(3):
            for j in range(3):
                if b == 0:
                    tap[: lift_ref.shape[2]] = lift_ref[i, j]
                    w = tap[...]
                else:
                    w = conv_ref[b - 1, i, j]
                hi, lo = split(w)
                for p, part in enumerate((hi, hi, lo)):
                    at = (p * 3 + j) * ch
                    w3f[b, at : at + ch, i * ch : (i + 1) * ch] = part
                hi, lo = split(w.T)
                if b == 0:
                    cols = slice(j * LIFT_BACK, (j + 1) * LIFT_BACK)
                    hi, lo = hi[:, :LIFT_BACK], lo[:, :LIFT_BACK]
                    at, below = i * ch, (3 + i) * ch
                    lift_t[at : at + ch, cols] = hi
                    lift_t[below : below + ch, cols] = hi
                    cols = slice(ch + cols.start, ch + cols.stop)
                    lift_t[at : at + ch, cols] = lo
                    continue
                for p, part in enumerate((hi, hi, lo)):
                    at = (p * 3 + i) * ch
                    w3t[b - 1, at : at + ch, j * ch : (j + 1) * ch] = part

    pl.semaphore_wait(barrier, nd - 1)
    halo_start(0, ys, 0, 2)
    sum_start(4 * SECTIONS, jnp.concatenate([count_part, count_part], axis=0))

    def square(hi, lo):
        return jnp.concatenate(
            [lanes_cat(hi, lo), lanes_cat(hi, jnp.zeros_like(hi))], axis=0
        )

    def put_square(target, w):
        n, m = w.shape
        hi, lo = split(w)
        target[:n, :m] = hi
        target[:n, m:] = lo
        target[n:, :m] = hi
        target[n:, m:] = jnp.zeros_like(hi)

    for load in loads[8:]:
        load.wait()
    put_square(wq3, qkv_ref[...])
    put_square(wqt3, qkv_ref[...].T)
    put_square(wo3, out_ref[...])
    put_square(wot3, out_ref[...].T)
    tap[...] = jnp.zeros_like(tap)
    tap[3 * VARS : 5 * VARS] = head_ref[...]
    put_square(wht3, tap[...])
    put_square(wh3, tap[...].T)
    head_bias_row[...] = jnp.zeros_like(head_bias_row)
    head_bias_row[:, 3 * VARS : 5 * VARS] = head_bias_ref[...]
    for s, weight in enumerate((1.0, 2.0, 2.0, 1.0)):
        gk[s] = cot * (weight * step_size / 6.0)
    grad_ref[...] = cot
    acc[...] = jnp.zeros_like(acc)
    gw[...] = jnp.zeros_like(gw)
    norm_acc[...] = jnp.zeros_like(norm_acc)
    bias_acc[...] = jnp.zeros_like(bias_acc)

    pair = 2 * L
    shape = (2 * pair, HEADS * pair)
    key_of = lax.broadcasted_iota(jnp.int32, shape, 0)
    key_of = key_of - lax.broadcasted_iota(jnp.int32, shape, 1) // L % 2 * L
    for p in range(W // 2):
        entries = lanes_cat(*[window_ref[2 * p], window_ref[2 * p + 1]] * HEADS)
        counted = jnp.zeros(shape, f32)
        for k in range(entries.shape[0]):
            counted = counted + jnp.where(entries[k : k + 1] == key_of, 1.0, 0.0)
        mult[p] = jnp.where(
            counted > 0.0, jnp.log(jnp.maximum(counted, 1.0)), -1e30
        )

    head_rows = lax.broadcasted_iota(jnp.int32, (HEADS * pair, ch), 0) // pair
    head_lanes = lax.broadcasted_iota(jnp.int32, (HEADS * pair, ch), 1) // (ch // HEADS)
    head_mask = jnp.where(head_rows == head_lanes, 1.0, 0.0)
    head_mask_h = head_mask.astype(bf16)
    scale = (ch // HEADS) ** -0.5

    def per_head(x):
        return jnp.concatenate([x] * HEADS, axis=0) * head_mask_h

    def heads_sum(x):
        x = x * head_mask
        return sum(x[h * pair : (h + 1) * pair] for h in range(1, HEADS)) + x[:pair]

    lift_bias = lift_bias_ref[...]
    head_bias = head_bias_row[...]
    gains = [gain_ref[0:1], gain_ref[1:2]]
    shifts = [shift_ref[0:1], shift_ref[1:2]]

    def stats(h, ranges):
        weighted = h * rows_of(mask, ranges, 2 * L)
        return jnp.concatenate(
            [
                jnp.sum(weighted, axis=0, keepdims=True),
                jnp.sum(weighted * h, axis=0, keepdims=True),
            ],
            axis=0,
        )

    def normalise(s, b, sums):
        total_count = count[0:1]
        average = sums[0:1] / total_count
        spread = sums[1:2] / total_count - average * average
        inverse = lax.rsqrt(spread + epsilon)
        norms[s, b, 0:1] = average
        norms[s, b, 1:2] = inverse
        return average, inverse

    def activity(h, b, average, inverse):
        z = (h - average) * inverse * gains[b] + shifts[b]
        below = 0.5 * (1.0 + lax.erf(z * (0.5**0.5)))
        slope = below + z * (
            jnp.exp(-0.5 * z * z) * (1.0 / math.sqrt(2.0 * math.pi))
        )
        return z * below, slope

    last = W // 2 - 1
    all_own = [(0, R)]
    own_edges, own_inner = [(0, pair), (R - pair, R)], [(pair, R - pair)]

    def forward(s, carry):
        hb = s * 6
        ext = 2 * pair

        def lift(ranges):
            value = conv(xh.at[s], xl.at[s], ranges, w3f[0]) + lift_bias
            put_rows(h0.at[s], value, ranges, 2 * L)
            return stats(value, ranges)

        def lay(a, b):
            y = ys[s, L + a : L + b]
            lane = lane_of(b - a)
            lon = 0.5 * (ys[s, 2 * L + a : 2 * L + b] - ys[s, a:b])
            x = jnp.where(
                (lane >= VARS) & (lane < 2 * VARS),
                lat_diff(y),
                jnp.where((lane >= 2 * VARS) & (lane < 3 * VARS), lon, y),
            )
            hi, lo = split(x)
            xh[s, a:b] = hi
            xl[s, a:b] = lo

        lay(pair, R1 - pair)
        sums = lift(own_inner)
        halo_wait(hb, ys, s, 2)
        lay(0, pair)
        lay(R1 - pair, R1)
        sum_start(s * 4, sums + lift(own_edges))
        halo_start(hb + 1, h0, s, 2)
        y1 = ys[s, L : L + R1]
        lane = lane_of(R1)
        flux = y1 * lroll(y1, -3 * VARS)
        flux = jnp.where(lane < 2 * VARS, flux, 0.0)
        own_lane = lane_of(R)
        t_lat = jnp.where(own_lane < VARS, lat_diff(flux[L : L + R]), 0.0)
        t_lon = jnp.where(
            own_lane >= VARS, 0.5 * (flux[2 * L : 2 * L + R] - flux[:R]), 0.0
        )
        t = -(t_lat + lroll(t_lon, -VARS))
        tend[...] = t + lroll(t, VARS) + lroll(t, 2 * VARS)

        @pl.when(s == 0)
        def _():
            count[...] = sum_wait(4 * SECTIONS)
            for at in (0, R + pair):
                mask[at : at + pair] = jnp.broadcast_to(
                    ys[0, at : at + pair, MASK_LANE : MASK_LANE + 1], (pair, LANES)
                )

        average, inverse = normalise(s, 0, sum_wait(s * 4))
        halo_wait(hb + 1, h0, s, 2)
        act, slope = activity(h0[s, L : L + R1], 0, average, inverse)
        dg1[s] = slope[L : L + R]
        hi, lo = split(act)
        a1h[s] = hi
        a1l[s] = lo
        second = h0[s, 2 * L : 2 * L + R] + conv(
            a1h.at[s], a1l.at[s], all_own, w3f[1]
        )
        h1[s, 2 * L : 2 * L + R] = second
        sum_start(s * 4 + 1, stats(second, all_own))
        halo_start(hb + 2, h1, s, 2)
        average, inverse = normalise(s, 1, sum_wait(s * 4 + 1))
        halo_wait(hb + 2, h1, s, 2)
        act, slope = activity(h1[s], 1, average, inverse)
        dg2[s] = slope[2 * L : 2 * L + R]
        hi, lo = split(act)
        a2h[s] = hi
        a2l[s] = lo

        def second_block(ranges):
            third = rows_of(h1.at[s], ranges, L) + conv(
                a2h.at[s], a2l.at[s], ranges, w3f[2]
            )
            put_rows(h2, third, ranges)
            hi, lo = split(third)
            put_rows(h2h.at[s], hi, ranges)
            put_rows(h2l.at[s], lo, ranges)
            mixing = product(hi, lo, wq3[...])
            hi, lo = split(mixing[:, :ch] * scale)
            put_rows(qh.at[s], hi, ranges)
            put_rows(ql.at[s], lo, ranges)
            hi, lo = split(mixing[:, ch : 2 * ch])
            put_rows(kh.at[s], hi, ranges)
            put_rows(kl.at[s], lo, ranges)
            hi, lo = split(mixing[:, 2 * ch :])
            put_rows(vh.at[s], hi, ranges)
            put_rows(vl.at[s], lo, ranges)

        def attend(pairs):
            scores = []
            for p in pairs:
                at = p * pair
                q_h = per_head(qh[s, at + L : at + L + pair])
                q_l = per_head(ql[s, at + L : at + L + pair])
                k_h = kh[s, at : at + ext]
                k_l = kl[s, at : at + ext]
                scores.append(
                    dot(
                        lanes_cat(k_h, k_l, k_h),
                        lanes_cat(q_h, q_h, q_l),
                        ((1,), (1,)),
                    )
                )
            weights = []
            for p, score in zip(pairs, scores):
                score = score + mult[p]
                e = jnp.exp(score - jnp.max(score, axis=0, keepdims=True))
                e = e * (1.0 / jnp.sum(e, axis=0, keepdims=True))
                probs[s, p] = e
                weights.append(e)
            for p, e in zip(pairs, weights):
                at = p * pair
                p_h, p_l = split(e.T)
                v_h = vh[s, at : at + ext]
                v_l = vl[s, at : at + ext]
                o = product(p_h, p_l, square(v_h, v_l))
                blend[at : at + pair] = heads_sum(o)

        weight = jnp.where((s == 0) | (s == SECTIONS - 1), 1.0, 2.0)
        factor = jnp.where(s == SECTIONS - 2, 1.0, 0.5) * step_size

        def finish(ranges):
            hi, lo = split(rows_of(blend, ranges))
            put_rows(bh.at[s], hi, ranges)
            put_rows(bl.at[s], lo, ranges)
            fourth = rows_of(h2, ranges, L) + product(hi, lo, wo3[...])
            hi, lo = split(fourth)
            put_rows(h3h.at[s], hi, ranges)
            put_rows(h3l.at[s], lo, ranges)
            slope_now = (
                rows_of(tend, ranges)
                + product(hi, lo, wh3[...])
                + head_bias
            )
            put_rows(acc, rows_of(acc, ranges) + weight * slope_now, ranges)
            put_rows(
                ys.at[s + 1],
                rows_of(ys.at[0], ranges, 2 * L) + factor * slope_now,
                ranges,
                2 * L,
            )

        second_block([(0, ext), (R1 - ext, R1)])
        attend([0, last])
        finish(own_edges)

        @pl.when(s < SECTIONS - 1)
        def _():
            halo_start(hb + 6, ys, s + 1, 2)

        second_block([(ext, R1 - ext)])
        attend(range(1, last))
        finish(own_inner)
        return carry

    lax.fori_loop(0, SECTIONS, forward, 0)
    acc[...] = ys[0, 2 * L : 2 * L + R] + (step_size / 6.0) * acc[...]

    def norm_back(s, b, h, grad_act, slope, through):
        average = norms[s, b, 0:1]
        inverse = norms[s, b, 1:2]
        dz = grad_act * slope
        hat = (h - average) * inverse
        sums = jnp.concatenate(
            [
                jnp.sum(dz, axis=0, keepdims=True),
                jnp.sum(dz * hat, axis=0, keepdims=True),
            ],
            axis=0,
        )
        return sums, through + dz * (gains[b] * inverse)

    def norm_rest(s, b, h, weight_mask, direct, sums):
        average = norms[s, b, 0:1]
        inverse = norms[s, b, 1:2]
        hat = (h - average) * inverse
        norm_acc[b] += sums
        return direct - weight_mask * (
            gains[b] * inverse / count[0:1]
        ) * (sums[0:1] + hat * sums[1:2])

    def backward(turn, carry):
        s = SECTIONS - 1 - turn
        hb = s * 6
        g_h, g_l = split(gk[s])
        gh[...] = g_h
        gl[...] = g_l
        dqkv[...] = jnp.zeros_like(dqkv)

        def head_back(ranges):
            hi, lo = rows_of(gh, ranges), rows_of(gl, ranges)
            grad3 = product(hi, lo, wht3[...])
            hi, lo = split(grad3)
            put_rows(dh2, grad3, ranges, L)
            put_rows(dh3h, hi, ranges)
            put_rows(dh3l, lo, ranges)
            hi, lo = split(product(hi, lo, wot3[...]))
            put_rows(dbh, hi, ranges)
            put_rows(dbl, lo, ranges)

        def attend_back(pairs):
            dps = []
            for p in pairs:
                at = p * pair
                d_h = per_head(dbh[pl.ds(at, pair)])
                d_l = per_head(dbl[pl.ds(at, pair)])
                v_h = vh[s, pl.ds(at, 2 * pair)]
                v_l = vl[s, pl.ds(at, 2 * pair)]
                dps.append(
                    dot(
                        lanes_cat(v_h, v_l, v_h),
                        lanes_cat(d_h, d_h, d_l),
                        ((1,), (1,)),
                    )
                )
            dss = []
            for p, dp in zip(pairs, dps):
                e = probs[s, p]
                dss.append(e * (dp - jnp.sum(e * dp, axis=0, keepdims=True)))
            for p, ds in zip(pairs, dss):
                at = p * pair
                k_h = kh[s, pl.ds(at, 2 * pair)]
                k_l = kl[s, pl.ds(at, 2 * pair)]
                t_h, t_l = split(ds.T)
                o = product(t_h, t_l, square(k_h, k_l))
                dqkv[pl.ds(at + L, pair), :ch] = heads_sum(o) * scale
                q_h = per_head(qh[s, at + L : at + L + pair])
                q_l = per_head(ql[s, at + L : at + L + pair])
                s_h, s_l = split(ds)
                o = dot(s_h, lanes_cat(q_h, q_l))
                o = o[:, :ch] + o[:, ch:] + dot(s_l, q_h)
                dqkv[pl.ds(at, 2 * pair), ch : 2 * ch] += o
                d_h = per_head(dbh[pl.ds(at, pair)])
                d_l = per_head(dbl[pl.ds(at, pair)])
                s_h, s_l = split(probs[s, p])
                o = dot(s_h, lanes_cat(d_h, d_l))
                o = o[:, :ch] + o[:, ch:] + dot(s_l, d_h)
                dqkv[pl.ds(at, 2 * pair), 2 * ch :] += o

        def to_hidden(ranges):
            hi, lo = split(rows_of(dqkv, ranges))
            part = product(hi, lo, wqt3[...])
            put_rows(dh2, rows_of(dh2, ranges) + part, ranges)

        def triple(ranges):
            hi, lo = lat_triple(rows_of(dh2, ranges))
            put_rows(th, hi, ranges)
            put_rows(tl, lo, ranges)

        dh2[:L] = jnp.zeros((L, ch), f32)
        dh2[R1 - L :] = jnp.zeros((L, ch), f32)
        head_back(own_edges)
        attend_back([0, last])
        border = [(0, pair), (R1 - pair, R1)]
        to_hidden(border)
        for side, (a, b) in enumerate(border):
            sb[s, side, :pair] = dh2[a:b]
        sb[s, 0, pair:] = gk[s, :L]
        sb[s, 1, pair:] = gk[s, R - L :]
        edges = [
            side_copy(hb + 3, side, sb.at[s, side], rb.at[s, side])
            for side in range(2)
        ]
        for e in edges:
            e.start()
        head_back(own_inner)
        attend_back(range(1, last))
        to_hidden([(pair, R1 - pair)])
        triple([(pair, R1 - pair)])
        (inner_act,) = conv_back(th, tl, own_inner, w3t[1])
        bias_acc[1:2] += jnp.sum(gk[s], axis=0, keepdims=True)
        part = rows_product(gh[...], gl[...], h3h[s], h3l[s])
        gw[head_base : head_base + HEAD_ROWS] += part[:HEAD_ROWS]
        for e in edges:
            e.wait()
        dh2[:pair] += rb[s, 1, :pair]
        dh2[R1 - pair :] += rb[s, 0, :pair]
        triple(border)
        low_act, high_act = conv_back(th, tl, own_edges, w3t[1])

        grad_act = jnp.concatenate([low_act, inner_act, high_act], axis=0)
        sums, direct = norm_back(
            s, 1, h1[s, 2 * L : 2 * L + R], grad_act, dg2[s], dh2[L : L + R]
        )
        sum_start(s * 4 + 2, sums)
        de1[s, 2 * L : 2 * L + R] = direct
        halo_start(hb + 4, de1, s, 1)
        gw[out_base : out_base + ch] += rows_product(
            bh[s], bl[s], dh3h[...], dh3l[...]
        )
        d_h, d_l = split(dqkv[...])
        wide = rows_product(h2h[s], h2l[s], d_h, d_l)
        for k in range(3):
            at = qkv_base + k * ch
            gw[at : at + ch] += wide[:, k * ch : (k + 1) * ch]
        add_conv_grad(
            conv_base + 9 * ch,
            a2h[s, L : L + R1],
            a2l[s, L : L + R1],
            th[L : L + R],
            tl[L : L + R],
        )
        pl.when(s == 0)(lambda: advance(0))
        sums = sum_wait(s * 4 + 2)
        halo_wait(hb + 4, de1, s, 1)
        pl.when(s == 0)(lambda: advance(1))
        grad1 = norm_rest(
            s, 1, h1[s, L : L + R1], mask[L : L + R1], de1[s, L : L + R1], sums
        )
        t_h, t_l = lat_triple(grad1)
        (grad_act,) = conv_back(t_h, t_l, all_own, w3t[0])
        sums, direct = norm_back(
            s, 0, h0[s, 2 * L : 2 * L + R], grad_act, dg1[s], grad1[L : L + R]
        )
        sum_start(s * 4 + 3, sums)
        de0[s, 2 * L : 2 * L + R] = direct
        halo_start(hb + 5, de0, s, 2)
        add_conv_grad(
            conv_base, a1h[s], a1l[s], t_h[L : L + R], t_l[L : L + R]
        )

        def lift_grad(s):
            add_conv_grad(
                0, xh[s], xl[s], lift_th[...], lift_tl[...], tap_rows(cin)
            )

        pl.when(s < SECTIONS - 1)(lambda: lift_grad(s + 1))
        pl.when(s == 0)(lambda: advance(2))
        sums = sum_wait(s * 4 + 3)
        halo_wait(hb + 5, de0, s, 2)

        @pl.when(s == 0)
        def _():
            advance(3)

        grad0 = norm_rest(s, 0, h0[s], mask[...], de0[s], sums)
        bias_acc[0:1] += jnp.sum(grad0[2 * L : 2 * L + R], axis=0, keepdims=True)
        t_h, t_l = lat_triple(grad0)
        lift_th[...] = t_h[2 * L : 2 * L + R]
        lift_tl[...] = t_l[2 * L : 2 * L + R]

        @pl.when(s == 0)
        def _():
            lift_grad(s)
            gw[cin : cin + 2] = bias_acc[...]
            advance(4)

        wide = product(t_h, t_l, lift_t[...])
        dx = (
            wide[2 * L :]
            + lroll(wide[L : L + R1], -LIFT_BACK)
            + lroll(wide[:R1], -2 * LIFT_BACK)
        )
        lane = lane_of(R)
        own = dx[L : L + R]
        lon = 0.5 * (dx[2 * L :] - dx[:R])
        g = gk[s]
        g_lon = jnp.concatenate([g[L:], rb[s, 0, 2 * L :]], axis=0)
        g_lon = 0.5 * (
            g_lon - jnp.concatenate([rb[s, 1, 2 * L :], g[: R - L]], axis=0)
        )
        dflux = jnp.where(
            lane < VARS, lat_diff(g), jnp.where(lane < 2 * VARS, g_lon, 0.0)
        )
        y = ys[s, 2 * L : 2 * L + R]
        parts = jnp.where(
            lane < VARS,
            own,
            jnp.where(lane < 2 * VARS, -lat_diff(own), -lon),
        )
        parts = parts + dflux * lroll(y, -3 * VARS)
        parts = jnp.where(lane < 3 * VARS, parts, 0.0)
        fields_grad = (
            parts
            + lroll(parts, VARS)
            + lroll(parts, 2 * VARS)
            + lroll(parts, -VARS)
            + lroll(parts, -2 * VARS)
        )
        velocity_grad = own + lroll(dflux * y, 3 * VARS)
        gy = jnp.where(
            lane < 3 * VARS,
            fields_grad,
            jnp.where(lane < 5 * VARS, velocity_grad, 0.0),
        )
        grad_ref[...] += gy

        @pl.when(s > 0)
        def _():
            factor = jnp.where(s == SECTIONS - 1, 1.0, 0.5) * step_size
            gk[s - 1] = gk[s - 1] + factor * gy

        return carry

    lax.fori_loop(0, SECTIONS, backward, 0)

    advance(5)
    all_out[gw.shape[0] : gw.shape[0] + 4] = norm_acc[...].reshape(4, ch)
    lane = lane_of(R)
    new, grad = acc[...], grad_ref[...]
    merged = jnp.where(
        lane < at_v,
        new,
        jnp.where(
            lane < at_cf,
            lroll(new, at_v - 3 * VARS),
            jnp.where(
                lane < at_cv, lroll(grad, at_cf), lroll(grad, at_cv - 3 * VARS)
            ),
        ),
    )
    for col in range(W):
        x = merged[col * L : (col + 1) * L].T
        all_out[pl.ds(gw.shape[0] + 8 + col, at_m, stride=W), :] = lanes_cat(
            x[:at_m], jnp.zeros((at_m, ch - L), f32)
        )

    state_result = pltpu.make_async_copy(
        all_out.at[all_rows:], final_out.at[all_rows:], out_sems.at[len(jobs)]
    )
    state_result.start()
    drain(jobs[::-1])
    state_result.wait()
    for job in jobs:
        job.result.wait()


def hand_out(rows, weights, *outs):
    fields = outs[:4]
    lift, lift_bias, gain, shift, conv, qkv, out, head, head_bias = outs[4:]
    ch = LANES
    at = rows + 8
    for ref in fields:
        ref[...] = weights[at : at + ref.shape[0], : ref.shape[1]]
        at += ref.shape[0]
    cin = lift.shape[2]
    vel = slice(3 * VARS, 5 * VARS)
    conv_base, qkv_base, out_base, head_base = bases(cin)
    for k in range(9):
        at = k * tap_rows(cin)
        lift[k // 3, k % 3] = weights[at : at + cin]
        for b in range(2):
            at = conv_base + (b * 9 + k) * ch
            conv[b, k // 3, k % 3] = weights[at : at + ch]
    lift_bias[...] = weights[cin : cin + 1]
    head_bias[...] = weights[cin + 1 : cin + 2, vel]
    for b in range(2):
        at = rows + 2 * b
        shift[b : b + 1] = weights[at : at + 1]
        gain[b : b + 1] = weights[at + 1 : at + 2]
    for k in range(3):
        at = qkv_base + k * ch
        qkv[:, k * ch : (k + 1) * ch] = weights[at : at + ch]
    out[...] = weights[out_base : out_base + ch]
    head[...] = weights[head_base + vel.start : head_base + vel.stop]


def on_device(
    nl,
    nb,
    fields,
    velocity,
    context,
    masks,
    window,
    lift_weight,
    lift_bias,
    norm_gain,
    norm_shift,
    conv_weight,
    attn_qkv,
    attn_out,
    head_weight,
    head_bias,
    cot_fields,
    cot_velocity,
):
    _, L, W, _ = fields.shape
    R, R1, R2 = L * W, L * (W + 2), L * (W + 4)
    ch = LANES
    nd = nl * nb

    def flat(x):
        return x[0].transpose(2, 1, 0).reshape(-1, L)

    S = SECTIONS
    cin = lift_weight.shape[2]
    rows = bases(cin)[-1] + HEAD_ROWS
    rows = -(-rows // (8 * nd)) * 8 * nd
    stage_count = len(factors(nl, 2)) + len(factors(nb, 4))
    job_count = len(job_plan(rows, 8 * nd, lift_weight.shape[2]))
    vm = pltpu.VMEM
    dma = pltpu.SemaphoreType.DMA
    scratch = [
        vm((S + 1, R2, ch), f32),
        vm((S, R1, ch), bf16),
        vm((S, R1, ch), bf16),
        vm((S, R2, ch), f32),
        vm((S, R2, ch), f32),
        vm((S, R1, ch), bf16),
        vm((S, R1, ch), bf16),
        vm((S, R2, ch), bf16),
        vm((S, R2, ch), bf16),
        vm((S, R, ch), f32),
        vm((S, R, ch), f32),
        vm((S, R1, ch), bf16),
        vm((S, R1, ch), bf16),
        vm((S, R1, ch), bf16),
        vm((S, R1, ch), bf16),
        vm((S, R1, ch), bf16),
        vm((S, R1, ch), bf16),
        vm((S, R1, ch), bf16),
        vm((S, R1, ch), bf16),
        vm((S, W // 2, 4 * L, 2 * HEADS * L), f32),
        vm((S, R, ch), bf16),
        vm((S, R, ch), bf16),
        vm((S, R, ch), bf16),
        vm((S, R, ch), bf16),
        vm((S, 2, 8, ch), f32),
        vm((S, R, ch), f32),
        vm((R, ch), f32),
        vm((R, ch), f32),
        vm((R2, ch), f32),
        vm((W // 2, 4 * L, 2 * HEADS * L), f32),
        vm((3, 9 * ch, 3 * ch), bf16),
        vm((2, 9 * ch, 3 * ch), bf16),
        vm((6 * ch, 2 * ch), bf16),
        vm((2 * ch, 6 * ch), bf16),
        vm((6 * ch, 2 * ch), bf16),
        vm((2 * ch, 2 * ch), bf16),
        vm((2 * ch, 2 * ch), bf16),
        vm((2 * ch, 2 * ch), bf16),
        vm((2 * ch, 2 * ch), bf16),
        vm((ch, ch), f32),
        vm((R, ch), f32),
        vm((R, ch), bf16),
        vm((R, ch), bf16),
        vm((R, ch), bf16),
        vm((R, ch), bf16),
        vm((R, ch), bf16),
        vm((R, ch), bf16),
        vm((R1, 3 * ch), bf16),
        vm((R1, 3 * ch), bf16),
        vm((R, 3 * ch), bf16),
        vm((R, 3 * ch), bf16),
        vm((R1, 3 * ch), f32),
        vm((R1, ch), f32),
        vm((R1, ch), f32),
        vm((2, ch), f32),
        vm((S, R2, ch), f32),
        vm((S, R2, ch), f32),
        vm((S, 2, 3 * L, ch), f32),
        vm((S, 2, 3 * L, ch), f32),
        vm((rows, ch), f32),
        vm((rows, ch), f32),
        vm((2, 2, ch), f32),
        vm((2, ch), f32),
        vm((rows + 8 + 6 * VARS * W, ch), f32),
        dma((job_count + 1,)),
        vm((32 * W, L), f32),
        vm((W, L), jnp.int32),
        vm((R, context.shape[-1]), f32),
        vm((W, window.shape[-1], L), jnp.int32),
        vm(lift_weight.shape, f32),
        vm(conv_weight.shape, f32),
        vm(attn_qkv.shape, f32),
        vm(attn_out.shape, f32),
        vm(head_weight.shape[::-1], f32),
        vm((1, ch), f32),
        vm((R, ch), f32),
        dma((12,)),
        vm((4 * S + 1, 2, ch), f32),
        vm((4 * S + 1, nd, 2, ch), f32),
        dma((4 * S + 1,)),
        dma((4 * S + 1,)),
        dma((6 * S, 2)),
        dma((6 * S, 2)),
        dma((job_count, stage_count)),
        dma((job_count, stage_count)),
        dma((job_count, stage_count)),
        dma((job_count, stage_count)),
    ]
    whole = pl.BlockSpec(memory_space=pltpu.VMEM)
    apart = pl.BlockSpec(memory_space=pl.ANY)
    results = pl.pallas_call(
        partial(kernel, (nl, nb, L, W, HEADS)),
        out_shape=jax.ShapeDtypeStruct((rows + 8 + 6 * VARS * W, ch), f32),
        in_specs=[apart] * 12 + [whole] * 4,
        out_specs=apart,
        scratch_shapes=scratch,
        compiler_params=pltpu.CompilerParams(
            collective_id=0, has_side_effects=True, vmem_limit_bytes=60 * 2**20
        ),
    )(
        flat(fields),
        flat(velocity),
        flat(cot_fields),
        flat(cot_velocity),
        masks[0].T,
        context.reshape(R, -1),
        window.transpose(1, 2, 0),
        lift_weight,
        conv_weight,
        attn_qkv,
        attn_out,
        head_weight.T,
        lift_bias[None],
        head_bias[None],
        norm_gain,
        norm_shift,
    )
    pixels = VARS * W
    shapes = (
        (pixels, L),
        (2 * pixels, L),
        (pixels, L),
        (2 * pixels, L),
        lift_weight.shape,
        (1, ch),
        norm_gain.shape,
        norm_shift.shape,
        conv_weight.shape,
        attn_qkv.shape,
        attn_out.shape,
        head_weight.shape[::-1],
        (1, head_bias.shape[0]),
    )
    outs = pl.pallas_call(
        partial(hand_out, rows),
        out_shape=tuple(jax.ShapeDtypeStruct(shape, f32) for shape in shapes),
        in_specs=[whole],
        out_specs=(whole,) * len(shapes),
        compiler_params=pltpu.CompilerParams(vmem_limit_bytes=32 * 2**20),
    )(results)

    def field(x):
        return x.reshape(-1, W, L).transpose(2, 1, 0)[None]

    return (
        *(field(x) for x in outs[:4]),
        outs[4],
        outs[5][0],
        *outs[6:11],
        outs[11].T,
        outs[12][0],
    )


def solution(mesh):
    field = P("batch", None, "lon", None)
    return jax.shard_map(
        partial(on_device, mesh.shape["lon"], mesh.shape["batch"]),
        mesh=mesh,
        in_specs=(
            field,
            field,
            field,
            P("batch", None, "lon"),
            P(None, "lon", None),
            P(),
            P(),
            P(),
            P(),
            P(),
            P(),
            P(),
            P(),
            P(),
            field,
            field,
        ),
        out_specs=(field,) * 4 + (P(),) * 9,
        check_vma=False,
    )
```

```python
from functools import partial
import math

import jax
import jax.numpy as jnp
from jax import lax
from jax.experimental import pallas as pl
from jax.experimental.pallas import tpu as pltpu
from jax.sharding import PartitionSpec as P

HEADS = 4
SECTIONS = 4
LANES = 128
VARS = 5
MASK_LANE = 127
HEAD_ROWS = 32
LIFT_BACK = 32
epsilon = 1e-05
step_size = 0.25
f32 = jnp.float32
bf16 = jnp.bfloat16
MESH = pl.DeviceIdType.MESH


def split(x):
    hi = x.astype(bf16)
    return hi, (x - hi.astype(f32)).astype(bf16)


def dot(a, b, dims=((1,), (0,))):
    return lax.dot_general(a, b, (dims, ((), ())), preferred_element_type=f32)


def lanes_cat(*parts):
    return jnp.concatenate(parts, axis=1)


def factors(n, largest):
    out = []
    while n > largest and n % 2 == 0:
        out.append(2)
        n //= 2
    if n > 1:
        out.append(n)
    return out


def tap_rows(cin):
    return -(-(cin + 2) // 8) * 8


def bases(cin):
    conv = 9 * tap_rows(cin)
    qkv = conv + 18 * LANES
    out = qkv + 3 * LANES
    return conv, qkv, out, out + LANES


def job_plan(rows, unit, cin):
    conv = bases(cin)[0]
    late = -(-conv // unit)
    middle = -(-(conv + 9 * LANES) // unit) - late
    early = rows // unit - late - middle
    sizes = []
    for kind, units in enumerate((late, middle, early)):
        half = (units + 1) // 2
        sizes += [(half, "A", kind), (units - half, "B", kind)]
    plan, at = [], 0
    for units, order, kind in sizes:
        if units:
            plan.append((at * unit, units * unit, order, kind))
        at += units
    return plan


def kernel(
    sizes,
    fields_in,
    velocity_in,
    cot_fields_in,
    cot_velocity_in,
    masks_in,
    context_in,
    window_in,
    lift_in,
    conv_in,
    qkv_in,
    out_in,
    head_in,
    lift_bias_ref,
    head_bias_ref,
    gain_ref,
    shift_ref,
    final_out,
    ys,
    xh,
    xl,
    h0,
    h1,
    a1h,
    a1l,
    a2h,
    a2l,
    dg1,
    dg2,
    h2h,
    h2l,
    qh,
    ql,
    kh,
    kl,
    vh,
    vl,
    probs,
    bh,
    bl,
    h3h,
    h3l,
    norms,
    gk,
    acc,
    tend,
    mask,
    mult,
    w3f,
    w3t,
    lift_t,
    wq3,
    wqt3,
    wo3,
    wot3,
    wh3,
    wht3,
    tap,
    blend,
    dbh,
    dbl,
    gh,
    gl,
    dh3h,
    dh3l,
    th,
    tl,
    lift_th,
    lift_tl,
    flux_parts,
    flux_velocity,
    lift_sums,
    dqkv,
    dh2,
    h2,
    count,
    de1,
    de0,
    sb,
    rb,
    gw,
    rsb,
    norm_acc,
    bias_acc,
    all_out,
    out_sems,
    planes,
    mask_plane,
    context_ref,
    window_ref,
    lift_ref,
    conv_ref,
    qkv_ref,
    out_ref,
    head_ref,
    head_bias_row,
    grad_ref,
    load_sems,
    ar_src,
    ar_buf,
    ar_send,
    ar_recv,
    halo_send,
    halo_recv,
    rs_send,
    rs_recv,
    ag_send,
    ag_recv,
):
    nl, nb, L, W, hid_heads = sizes
    nd = nl * nb
    R = L * W
    R1 = R + 2 * L
    R2 = R + 4 * L
    ch = LANES
    me_l = lax.axis_index("lon")
    me_b = lax.axis_index("batch")
    me = me_l * nb + me_b
    left = (lax.rem(me_l + nl - 1, nl), me_b)
    right = (lax.rem(me_l + 1, nl), me_b)

    def peer(k):
        t = lax.rem(me + k, nd)
        return (t // nb, lax.rem(t, nb))

    low_half = 1 - me_b // max(nb // 2, 1) if nb > 1 else 0
    lon_order = sorted(range(nl), key=lambda hop: -min(hop, nl - hop))
    barrier = pltpu.get_barrier_semaphore()

    def greet(k, c):
        pl.semaphore_signal(barrier, inc=1, device_id=peer(k), device_id_type=MESH)
        return c

    lax.fori_loop(1, nd, greet, 0)

    def sum_start(a, vals):
        ar_src[a] = vals
        ar_buf[a, me] = vals

        def send(k, c):
            to_b = k + low_half * (nb - 1 - 2 * k)
            for hop in lon_order:
                copy = pltpu.make_async_remote_copy(
                    ar_src.at[a],
                    ar_buf.at[a, me],
                    ar_send.at[a],
                    ar_recv.at[a],
                    device_id=(lax.rem(me_l + hop, nl), to_b),
                    device_id_type=MESH,
                )
                if hop == 0:
                    pl.when(to_b != me_b)(copy.start)
                else:
                    copy.start()
            return c

        lax.fori_loop(0, nb, send, 0)

    def sum_wait(a):
        got = ar_buf.at[a, pl.ds(0, nd - 1)]
        pltpu.make_async_copy(got, got, ar_recv.at[a]).wait()
        pltpu.make_async_copy(got, got, ar_send.at[a]).wait()
        return jnp.sum(ar_buf[a], axis=0)

    def side_copy(h, side, src, dst):
        return pltpu.make_async_remote_copy(
            src,
            dst,
            halo_send.at[h, side],
            halo_recv.at[h, side],
            device_id=left if side == 0 else right,
            device_id_type=MESH,
        )

    def halo_copies(h, buf, s, cols):
        n = cols * L
        lo = 2 * L - n
        to_left = side_copy(
            h, 0, buf.at[s, pl.ds(2 * L, n)], buf.at[s, pl.ds(R + 2 * L, n)]
        )
        to_right = side_copy(
            h, 1, buf.at[s, pl.ds(R + 2 * L - n, n)], buf.at[s, pl.ds(lo, n)]
        )
        return to_left, to_right

    def halo_start(h, buf, s, cols):
        for c in halo_copies(h, buf, s, cols):
            c.start()

    def halo_wait(h, buf, s, cols):
        for c in halo_copies(h, buf, s, cols):
            c.wait()

    def lat_of(n):
        return lax.broadcasted_iota(jnp.int32, (n, LANES), 0) % L

    def north(x):
        n = x.shape[0]
        return jnp.where(lat_of(n) == L - 1, 0.0, pltpu.roll(x, n - 1, 0))

    def south(x):
        n = x.shape[0]
        return jnp.where(lat_of(n) == 0, 0.0, pltpu.roll(x, 1, 0))

    def lat_diff(x):
        return 0.5 * (north(x) - south(x))

    def lane_of(n):
        return lax.broadcasted_iota(jnp.int32, (n, LANES), 1)

    def lroll(x, shift):
        return pltpu.roll(x, shift % LANES, 1)

    def rows_of(ref, ranges, base=0):
        parts = [ref[base + a : base + b] for a, b in ranges]
        return parts[0] if len(parts) == 1 else jnp.concatenate(parts, axis=0)

    def put_rows(ref, value, ranges, base=0):
        at = 0
        for a, b in ranges:
            ref[base + a : base + b] = value[at : at + b - a]
            at += b - a

    def conv(hi, lo, ranges, weights):
        cols_h = [rows_of(hi, ranges, j * L) for j in range(3)]
        cols_l = [rows_of(lo, ranges, j * L) for j in range(3)]
        wide = dot(lanes_cat(*cols_h, *cols_l, *cols_h), weights)
        return (
            wide[:, ch : 2 * ch]
            + south(wide[:, :ch])
            + north(wide[:, 2 * ch :])
        )

    def product(hi, lo, weights):
        wide = dot(lanes_cat(hi, lo), weights)
        n = wide.shape[1] // 2
        return wide[:, :n] + wide[:, n:]

    def rows_product(ah, al, gh, gl):
        t = ((0,), (0,))
        return dot(ah, gh, t) + dot(ah, gl, t) + dot(al, gh, t)

    def lat_triple(x):
        return split(lanes_cat(north(x), x, south(x)))

    def conv_back(hi, lo, ranges, weights):
        wider = [(a, b + 2 * L) for a, b in ranges]
        gh, gl = rows_of(hi, wider), rows_of(lo, wider)
        wide = dot(lanes_cat(gh, gl, gh), weights)
        outs, at = [], 0
        for a, b in ranges:
            n = b - a
            outs.append(
                wide[at + 2 * L : at + 2 * L + n, :ch]
                + wide[at + L : at + L + n, ch : 2 * ch]
                + wide[at : at + n, 2 * ch :]
            )
            at += n + 2 * L
        return outs

    def add_conv_grad(base, ah, al, gh, gl, taken=ch):
        for j in range(3):
            part = rows_product(
                ah[j * L : j * L + R], al[j * L : j * L + R], gh, gl
            )
            for i in range(3):
                at = base + (i * 3 + j) * taken
                gw[at : at + taken, :] += part[:taken, i * ch : (i + 1) * ch]

    cin = lift_in.shape[2]
    conv_base, qkv_base, out_base, head_base = bases(cin)

    all_rows = gw.shape[0]
    unit = 8 * nd
    minor, batch_parts = factors(nl, 2), factors(nb, 4)
    axes = [("lon", n) for n in minor] + [("batch", n) for n in batch_parts]
    steps = {"lon": 1, "batch": 1}
    members = []
    for axis, n in axes:
        mine = me_l if axis == "lon" else me_b
        members.append((axis, steps[axis], n, lax.rem(mine // steps[axis], n)))
        steps[axis] *= n
    def stage_of(member):
        axis, step, n, idx = member

        def device_of(q):
            shift = (q - idx) * step
            if axis == "lon":
                return (me_l + shift, me_b)
            return (me_l, me_b + shift)

        return n, idx, device_of

    first, rest = members[:1], members[1:]
    orders = {
        "A": first + rest,
        "B": first + rest[1::-1] + rest[2:],
    }

    def rows_at(at, n):
        return pl.ds(pl.multiple_of(at, 8), n)

    class Job:
        def __init__(self, number, base, size, order):
            self.number = number
            self.result = pltpu.make_async_copy(
                all_out.at[base : base + size],
                final_out.at[base : base + size],
                out_sems.at[number],
            )
            self.stages = stages = [stage_of(m) for m in orders[order]]
            self.regions = []
            off, slot = base, base
            for n, idx, _ in stages:
                part = size // n
                self.regions.append((off, part, slot))
                off = off + idx * part
                slot += (n - 1) * part
                size = part
            self.own, self.size = off, size
            self.done, self.todo = 0, list(self.moves())

        def scatter_start(self, t):
            n, idx, device_of = self.stages[t]
            off, part, slot = self.regions[t]
            for k in range(1, n):
                q = lax.rem(idx + k, n)
                pltpu.make_async_remote_copy(
                    gw.at[rows_at(off + q * part, part)],
                    rsb.at[pl.ds(slot + (n - 1 - k) * part, part)],
                    rs_send.at[self.number, t],
                    rs_recv.at[self.number, t],
                    device_id=device_of(q),
                    device_id_type=MESH,
                ).start()

        def scatter_finish(self, t):
            n, idx, _ = self.stages[t]
            off, part, slot = self.regions[t]
            got = rsb.at[pl.ds(slot, (n - 1) * part)]
            pltpu.make_async_copy(got, got, rs_recv.at[self.number, t]).wait()
            pltpu.make_async_copy(got, got, rs_send.at[self.number, t]).wait()
            mine = off + idx * part
            chunk = math.gcd(part, 128)

            def add(i, c):
                at = pl.multiple_of(i * chunk, 8)
                total = gw[rows_at(mine + at, chunk)]
                for k in range(n - 1):
                    total = total + rsb[rows_at(slot + k * part + at, chunk)]
                gw[rows_at(mine + at, chunk)] = total
                return c

            lax.fori_loop(0, part // chunk, add, 0)

        def gather_start(self, t):
            n, idx, device_of = self.stages[t]
            off, part, _ = self.regions[t]
            if t == len(self.stages) - 1:
                all_out[rows_at(self.own, self.size)] = gw[
                    rows_at(self.own, self.size)
                ]
            mine = all_out.at[rows_at(off + idx * part, part)]
            for k in range(1, n):
                pltpu.make_async_remote_copy(
                    mine,
                    mine,
                    ag_send.at[self.number, t],
                    ag_recv.at[self.number, t],
                    device_id=device_of(lax.rem(idx + k, n)),
                    device_id_type=MESH,
                ).start()

        def gather_finish(self, t):
            n, _, _ = self.stages[t]
            _, part, slot = self.regions[t]
            got = rsb.at[pl.ds(slot, (n - 1) * part)]
            pltpu.make_async_copy(got, got, ag_recv.at[self.number, t]).wait()
            pltpu.make_async_copy(got, got, ag_send.at[self.number, t]).wait()

        def finished(self):
            self.gather_finish(0)
            self.result.start()

        def moves(self):
            for t in range(len(self.stages)):
                yield partial(self.scatter_start, t)
                yield partial(self.scatter_finish, t)
            for t in reversed(range(len(self.stages))):
                yield partial(self.gather_start, t)
                yield partial(self.gather_finish, t) if t else self.finished

    def take_steps(job, n):
        for _ in range(n):
            job.done += 1
            job.todo[job.done - 1]()

    def drain(jobs):
        while any(job.done < len(job.todo) for job in jobs):
            for job in jobs:
                left_over = len(job.todo) - job.done
                take_steps(job, min(left_over, 1 + (job.done % 2 and left_over > 1)))

    jobs, late, middle, early = [], [], [], []
    for k, (base, size, order, kind) in enumerate(job_plan(all_rows, unit, lift_in.shape[2])):
        jobs.append(Job(k, base, size, order))
        (late, middle, early)[kind].append(jobs[-1])
    points = (
        ((early, 1),),
        ((early, 2),),
        ((middle, 1),),
        ((early, 2), (middle, 2)),
        ((late, 1),),
        ((late, 2),),
    )

    def advance(k):
        for some, n in points[k]:
            for job in some:
                take_steps(job, n)

    at_f, at_v, at_cf, at_cv, at_m = (
        k * VARS for k in (0, 1, 3, 4, 6)
    )
    loads = [
        (fields_in, planes.at[at_f * W : at_v * W]),
        (velocity_in, planes.at[at_v * W : at_cf * W]),
        (cot_fields_in, planes.at[at_cf * W : at_cv * W]),
        (cot_velocity_in, planes.at[at_cv * W : at_m * W]),
        (masks_in, mask_plane),
        (context_in, context_ref),
        (lift_in, lift_ref),
        (conv_in, conv_ref),
        (qkv_in, qkv_ref),
        (out_in, out_ref),
        (head_in, head_ref),
        (window_in, window_ref),
    ]
    loads = [
        pltpu.make_async_copy(src, dst, load_sems.at[k])
        for k, (src, dst) in enumerate(loads)
    ]
    for load in loads:
        load.start()
    planes[(at_m + 1) * W :] = jnp.zeros((W, L), f32)
    for load in loads[:6]:
        load.wait()
    planes[at_m * W : (at_m + 1) * W] = mask_plane[...].astype(f32)
    cots = []
    masks_own = []
    for col in range(W):
        at = 2 * L + col * L
        x = planes[pl.ds(col, at_m + 2, stride=W), :].T
        ys[0, at : at + L] = jnp.zeros((L, ch), f32)
        for k in range(3):
            ys[0, at : at + L, k * VARS : (k + 1) * VARS] = x[:, at_f:at_v]
            gk[0, at - 2 * L : at - L, k * VARS : (k + 1) * VARS] = x[:, at_cf:at_cv]
        ys[0, at : at + L, 3 * VARS : 5 * VARS] = x[:, at_v:at_cf]
        gk[0, at - 2 * L : at - L, 3 * VARS : 5 * VARS] = x[:, at_cv:at_m]
        gk[0, at - 2 * L : at - L, 5 * VARS :] = jnp.zeros((L, ch - 5 * VARS), f32)
        ys[0, at : at + L, 5 * VARS : 5 * VARS + context_ref.shape[1]] = context_ref[
            pl.ds(col, L, stride=W), :
        ]
        ys[0, at : at + L, MASK_LANE:] = x[:, at_m : at_m + 1]
    cot = gk[0]
    mask_own = jnp.broadcast_to(
        ys[0, 2 * L : 2 * L + R, MASK_LANE : MASK_LANE + 1], (R, LANES)
    )
    mask[2 * L : 2 * L + R] = mask_own
    count_part = jnp.sum(mask_own, axis=0, keepdims=True)
    for load in loads[6:8]:
        load.wait()

    tap[...] = jnp.zeros_like(tap)
    lift_t[...] = jnp.zeros_like(lift_t)
    for b in range(3):
        for i in range(3):
            for j in range(3):
                if b == 0:
                    tap[: lift_ref.shape[2]] = lift_ref[i, j]
                    w = tap[...]
                else:
                    w = conv_ref[b - 1, i, j]
                hi, lo = split(w)
                for p, part in enumerate((hi, hi, lo)):
                    at = (p * 3 + j) * ch
                    w3f[b, at : at + ch, i * ch : (i + 1) * ch] = part
                hi, lo = split(w.T)
                if b == 0:
                    cols = slice(j * LIFT_BACK, (j + 1) * LIFT_BACK)
                    hi, lo = hi[:, :LIFT_BACK], lo[:, :LIFT_BACK]
                    at, below = i * ch, (3 + i) * ch
                    lift_t[at : at + ch, cols] = hi
                    lift_t[below : below + ch, cols] = hi
                    cols = slice(ch + cols.start, ch + cols.stop)
                    lift_t[at : at + ch, cols] = lo
                    continue
                for p, part in enumerate((hi, hi, lo)):
                    at = (p * 3 + i) * ch
                    w3t[b - 1, at : at + ch, j * ch : (j + 1) * ch] = part

    pair = 2 * L
    last = W // 2 - 1
    all_own = [(0, R)]
    own_edges, own_inner = [(0, pair), (R - pair, R)], [(pair, R - pair)]
    lift_bias = lift_bias_ref[...]

    def stats(h, ranges):
        weighted = h * rows_of(mask, ranges, 2 * L)
        return jnp.concatenate(
            [
                jnp.sum(weighted, axis=0, keepdims=True),
                jnp.sum(weighted * h, axis=0, keepdims=True),
            ],
            axis=0,
        )

    def lift(s, ranges):
        value = conv(xh.at[s], xl.at[s], ranges, w3f[0]) + lift_bias
        put_rows(h0.at[s], value, ranges, 2 * L)
        return stats(value, ranges)

    def lay(s, a, b):
        y = ys[s, L + a : L + b]
        lane = lane_of(b - a)
        lon = 0.5 * (ys[s, 2 * L + a : 2 * L + b] - ys[s, a:b])
        x = jnp.where(
            (lane >= VARS) & (lane < 2 * VARS),
            lat_diff(y),
            jnp.where((lane >= 2 * VARS) & (lane < 3 * VARS), lon, y),
        )
        hi, lo = split(x)
        xh[s, a:b] = hi
        xl[s, a:b] = lo

    def lift_inner(s):
        lay(s, pair, R1 - pair)
        lift_sums[...] = lift(s, own_inner)

    lift_inner(0)
    pl.semaphore_wait(barrier, nd - 1)
    halo_start(0, ys, 0, 2)
    sum_start(4 * SECTIONS, jnp.concatenate([count_part, count_part], axis=0))

    def square(hi, lo):
        return jnp.concatenate(
            [lanes_cat(hi, lo), lanes_cat(hi, jnp.zeros_like(hi))], axis=0
        )

    def put_square(target, w):
        n, m = w.shape
        hi, lo = split(w)
        target[:n, :m] = hi
        target[:n, m:] = lo
        target[n:, :m] = hi
        target[n:, m:] = jnp.zeros_like(hi)

    for load in loads[8:]:
        load.wait()
    put_square(wq3, qkv_ref[...])
    put_square(wqt3, qkv_ref[...].T)
    put_square(wo3, out_ref[...])
    put_square(wot3, out_ref[...].T)
    tap[...] = jnp.zeros_like(tap)
    tap[3 * VARS : 5 * VARS] = head_ref[...]
    put_square(wht3, tap[...])
    put_square(wh3, tap[...].T)
    head_bias_row[...] = jnp.zeros_like(head_bias_row)
    head_bias_row[:, 3 * VARS : 5 * VARS] = head_bias_ref[...]
    for s, weight in enumerate((1.0, 2.0, 2.0, 1.0)):
        gk[s] = cot * (weight * step_size / 6.0)
    grad_ref[...] = cot
    acc[...] = jnp.zeros_like(acc)
    dqkv[...] = jnp.zeros_like(dqkv)
    gw[...] = jnp.zeros_like(gw)
    norm_acc[...] = jnp.zeros_like(norm_acc)
    bias_acc[...] = jnp.zeros_like(bias_acc)

    shape = (2 * pair, HEADS * pair)
    key_of = lax.broadcasted_iota(jnp.int32, shape, 0)
    key_of = key_of - lax.broadcasted_iota(jnp.int32, shape, 1) // L % 2 * L
    for p in range(W // 2):
        entries = lanes_cat(*[window_ref[2 * p], window_ref[2 * p + 1]] * HEADS)
        counted = jnp.zeros(shape, f32)
        for k in range(entries.shape[0]):
            counted = counted + jnp.where(entries[k : k + 1] == key_of, 1.0, 0.0)
        mult[p] = jnp.where(
            counted > 0.0, jnp.log(jnp.maximum(counted, 1.0)), -1e30
        )

    head_rows = lax.broadcasted_iota(jnp.int32, (HEADS * pair, ch), 0) // pair
    head_lanes = lax.broadcasted_iota(jnp.int32, (HEADS * pair, ch), 1) // (ch // HEADS)
    head_mask = jnp.where(head_rows == head_lanes, 1.0, 0.0)
    head_mask_h = head_mask.astype(bf16)
    scale = (ch // HEADS) ** -0.5

    def per_head(x):
        return jnp.concatenate([x] * HEADS, axis=0) * head_mask_h

    def heads_sum(x):
        x = x * head_mask
        return sum(x[h * pair : (h + 1) * pair] for h in range(1, HEADS)) + x[:pair]

    head_bias = head_bias_row[...]
    gains = [gain_ref[0:1], gain_ref[1:2]]
    shifts = [shift_ref[0:1], shift_ref[1:2]]

    def normalise(s, b, sums):
        total_count = count[0:1]
        average = sums[0:1] / total_count
        spread = sums[1:2] / total_count - average * average
        inverse = lax.rsqrt(spread + epsilon)
        norms[s, b, 0:1] = average
        norms[s, b, 1:2] = inverse
        return average, inverse

    def activity(h, b, average, inverse):
        z = (h - average) * inverse * gains[b] + shifts[b]
        below = 0.5 * (1.0 + lax.erf(z * (0.5**0.5)))
        slope = below + z * (
            jnp.exp(-0.5 * z * z) * (1.0 / math.sqrt(2.0 * math.pi))
        )
        return z * below, slope


    def forward(s, carry):
        hb = s * 6
        ext = 2 * pair

        halo_wait(hb, ys, s, 2)
        lay(s, 0, pair)
        lay(s, R1 - pair, R1)
        sum_start(s * 4, lift_sums[...] + lift(s, own_edges))
        halo_start(hb + 1, h0, s, 2)
        y1 = ys[s, L : L + R1]
        lane = lane_of(R1)
        flux = y1 * lroll(y1, -3 * VARS)
        flux = jnp.where(lane < 2 * VARS, flux, 0.0)
        own_lane = lane_of(R)
        t_lat = jnp.where(own_lane < VARS, lat_diff(flux[L : L + R]), 0.0)
        t_lon = jnp.where(
            own_lane >= VARS, 0.5 * (flux[2 * L : 2 * L + R] - flux[:R]), 0.0
        )
        t = -(t_lat + lroll(t_lon, -VARS))
        tend[...] = t + lroll(t, VARS) + lroll(t, 2 * VARS)

        @pl.when(s == 0)
        def _():
            count[...] = sum_wait(4 * SECTIONS)
            for at in (0, R + pair):
                mask[at : at + pair] = jnp.broadcast_to(
                    ys[0, at : at + pair, MASK_LANE : MASK_LANE + 1], (pair, LANES)
                )

        average, inverse = normalise(s, 0, sum_wait(s * 4))
        halo_wait(hb + 1, h0, s, 2)
        act, slope = activity(h0[s, L : L + R1], 0, average, inverse)
        dg1[s] = slope[L : L + R]
        hi, lo = split(act)
        a1h[s] = hi
        a1l[s] = lo
        second = h0[s, 2 * L : 2 * L + R] + conv(
            a1h.at[s], a1l.at[s], all_own, w3f[1]
        )
        h1[s, 2 * L : 2 * L + R] = second
        sum_start(s * 4 + 1, stats(second, all_own))
        halo_start(hb + 2, h1, s, 2)
        average, inverse = normalise(s, 1, sum_wait(s * 4 + 1))
        halo_wait(hb + 2, h1, s, 2)
        act, slope = activity(h1[s], 1, average, inverse)
        dg2[s] = slope[2 * L : 2 * L + R]
        hi, lo = split(act)
        a2h[s] = hi
        a2l[s] = lo

        def second_block(ranges):
            third = rows_of(h1.at[s], ranges, L) + conv(
                a2h.at[s], a2l.at[s], ranges, w3f[2]
            )
            put_rows(h2, third, ranges)
            hi, lo = split(third)
            put_rows(h2h.at[s], hi, ranges)
            put_rows(h2l.at[s], lo, ranges)
            mixing = product(hi, lo, wq3[...])
            hi, lo = split(mixing[:, :ch] * scale)
            put_rows(qh.at[s], hi, ranges)
            put_rows(ql.at[s], lo, ranges)
            hi, lo = split(mixing[:, ch : 2 * ch])
            put_rows(kh.at[s], hi, ranges)
            put_rows(kl.at[s], lo, ranges)
            hi, lo = split(mixing[:, 2 * ch :])
            put_rows(vh.at[s], hi, ranges)
            put_rows(vl.at[s], lo, ranges)

        def attend(pairs):
            scores = []
            for p in pairs:
                at = p * pair
                q_h = per_head(qh[s, at + L : at + L + pair])
                q_l = per_head(ql[s, at + L : at + L + pair])
                k_h = kh[s, at : at + ext]
                k_l = kl[s, at : at + ext]
                scores.append(
                    dot(
                        lanes_cat(k_h, k_l, k_h),
                        lanes_cat(q_h, q_h, q_l),
                        ((1,), (1,)),
                    )
                )
            weights = []
            for p, score in zip(pairs, scores):
                score = score + mult[p]
                e = jnp.exp(score - jnp.max(score, axis=0, keepdims=True))
                e = e * (1.0 / jnp.sum(e, axis=0, keepdims=True))
                probs[s, p] = e
                weights.append(e)
            for p, e in zip(pairs, weights):
                at = p * pair
                p_h, p_l = split(e.T)
                v_h = vh[s, at : at + ext]
                v_l = vl[s, at : at + ext]
                o = product(p_h, p_l, square(v_h, v_l))
                blend[at : at + pair] = heads_sum(o)

        weight = jnp.where((s == 0) | (s == SECTIONS - 1), 1.0, 2.0)
        factor = jnp.where(s == SECTIONS - 2, 1.0, 0.5) * step_size

        def finish(ranges):
            hi, lo = split(rows_of(blend, ranges))
            put_rows(bh.at[s], hi, ranges)
            put_rows(bl.at[s], lo, ranges)
            fourth = rows_of(h2, ranges, L) + product(hi, lo, wo3[...])
            hi, lo = split(fourth)
            put_rows(h3h.at[s], hi, ranges)
            put_rows(h3l.at[s], lo, ranges)
            slope_now = (
                rows_of(tend, ranges)
                + product(hi, lo, wh3[...])
                + head_bias
            )
            put_rows(acc, rows_of(acc, ranges) + weight * slope_now, ranges)
            put_rows(
                ys.at[s + 1],
                rows_of(ys.at[0], ranges, 2 * L) + factor * slope_now,
                ranges,
                2 * L,
            )

        second_block([(0, ext), (R1 - ext, R1)])
        attend([0, last])
        finish(own_edges)

        @pl.when(s < SECTIONS - 1)
        def _():
            halo_start(hb + 6, ys, s + 1, 2)

        second_block([(ext, R1 - ext)])
        attend(range(1, last))
        finish(own_inner)
        pl.when(s < SECTIONS - 1)(lambda: lift_inner(s + 1))
        return carry

    lax.fori_loop(0, SECTIONS, forward, 0)
    acc[...] = ys[0, 2 * L : 2 * L + R] + (step_size / 6.0) * acc[...]

    def norm_back(s, b, h, grad_act, slope, through):
        average = norms[s, b, 0:1]
        inverse = norms[s, b, 1:2]
        dz = grad_act * slope
        hat = (h - average) * inverse
        sums = jnp.concatenate(
            [
                jnp.sum(dz, axis=0, keepdims=True),
                jnp.sum(dz * hat, axis=0, keepdims=True),
            ],
            axis=0,
        )
        return sums, through + dz * (gains[b] * inverse)

    def norm_rest(s, b, h, weight_mask, direct, sums):
        average = norms[s, b, 0:1]
        inverse = norms[s, b, 1:2]
        hat = (h - average) * inverse
        norm_acc[b] += sums
        return direct - weight_mask * (
            gains[b] * inverse / count[0:1]
        ) * (sums[0:1] + hat * sums[1:2])

    def backward(turn, carry):
        s = SECTIONS - 1 - turn
        hb = s * 6
        g_h, g_l = split(gk[s])
        gh[...] = g_h
        gl[...] = g_l

        def head_back(ranges):
            hi, lo = rows_of(gh, ranges), rows_of(gl, ranges)
            grad3 = product(hi, lo, wht3[...])
            hi, lo = split(grad3)
            put_rows(dh2, grad3, ranges, L)
            put_rows(dh3h, hi, ranges)
            put_rows(dh3l, lo, ranges)
            hi, lo = split(product(hi, lo, wot3[...]))
            put_rows(dbh, hi, ranges)
            put_rows(dbl, lo, ranges)

        def attend_back(pairs):
            dps = []
            for p in pairs:
                at = p * pair
                d_h = per_head(dbh[pl.ds(at, pair)])
                d_l = per_head(dbl[pl.ds(at, pair)])
                v_h = vh[s, pl.ds(at, 2 * pair)]
                v_l = vl[s, pl.ds(at, 2 * pair)]
                dps.append(
                    dot(
                        lanes_cat(v_h, v_l, v_h),
                        lanes_cat(d_h, d_h, d_l),
                        ((1,), (1,)),
                    )
                )
            dss = []
            for p, dp in zip(pairs, dps):
                e = probs[s, p]
                dss.append(e * (dp - jnp.sum(e * dp, axis=0, keepdims=True)))
            for p, ds in zip(pairs, dss):
                at = p * pair
                k_h = kh[s, pl.ds(at, 2 * pair)]
                k_l = kl[s, pl.ds(at, 2 * pair)]
                t_h, t_l = split(ds.T)
                o = product(t_h, t_l, square(k_h, k_l))
                dqkv[pl.ds(at + L, pair), :ch] = heads_sum(o) * scale
                q_h = per_head(qh[s, at + L : at + L + pair])
                q_l = per_head(ql[s, at + L : at + L + pair])
                s_h, s_l = split(ds)
                o = dot(s_h, lanes_cat(q_h, q_l))
                o = o[:, :ch] + o[:, ch:] + dot(s_l, q_h)
                dqkv[pl.ds(at, 2 * pair), ch : 2 * ch] += o
                d_h = per_head(dbh[pl.ds(at, pair)])
                d_l = per_head(dbl[pl.ds(at, pair)])
                s_h, s_l = split(probs[s, p])
                o = dot(s_h, lanes_cat(d_h, d_l))
                o = o[:, :ch] + o[:, ch:] + dot(s_l, d_h)
                dqkv[pl.ds(at, 2 * pair), 2 * ch :] += o

        def to_hidden(ranges):
            hi, lo = split(rows_of(dqkv, ranges))
            part = product(hi, lo, wqt3[...])
            put_rows(dh2, rows_of(dh2, ranges) + part, ranges)

        def triple(ranges):
            hi, lo = lat_triple(rows_of(dh2, ranges))
            put_rows(th, hi, ranges)
            put_rows(tl, lo, ranges)

        dh2[:L] = jnp.zeros((L, ch), f32)
        dh2[R1 - L :] = jnp.zeros((L, ch), f32)
        head_back(own_edges)
        attend_back([0, last])
        border = [(0, pair), (R1 - pair, R1)]
        to_hidden(border)
        for side, (a, b) in enumerate(border):
            sb[s, side, :pair] = dh2[a:b]
        sb[s, 0, pair:] = gk[s, :L]
        sb[s, 1, pair:] = gk[s, R - L :]
        edges = [
            side_copy(hb + 3, side, sb.at[s, side], rb.at[s, side])
            for side in range(2)
        ]
        for e in edges:
            e.start()
        head_back(own_inner)
        attend_back(range(1, last))
        to_hidden([(pair, R1 - pair)])
        triple([(pair, R1 - pair)])
        (inner_act,) = conv_back(th, tl, own_inner, w3t[1])
        bias_acc[1:2] += jnp.sum(gk[s], axis=0, keepdims=True)
        part = rows_product(gh[...], gl[...], h3h[s], h3l[s])
        gw[head_base : head_base + HEAD_ROWS] += part[:HEAD_ROWS]
        gw[out_base : out_base + ch] += rows_product(
            bh[s], bl[s], dh3h[...], dh3l[...]
        )
        for e in edges:
            e.wait()
        dh2[:pair] += rb[s, 1, :pair]
        dh2[R1 - pair :] += rb[s, 0, :pair]
        triple(border)
        low_act, high_act = conv_back(th, tl, own_edges, w3t[1])

        grad_act = jnp.concatenate([low_act, inner_act, high_act], axis=0)
        sums, direct = norm_back(
            s, 1, h1[s, 2 * L : 2 * L + R], grad_act, dg2[s], dh2[L : L + R]
        )
        sum_start(s * 4 + 2, sums)
        de1[s, 2 * L : 2 * L + R] = direct
        halo_start(hb + 4, de1, s, 1)
        d_h, d_l = split(dqkv[...])
        wide = rows_product(h2h[s], h2l[s], d_h, d_l)
        for k in range(3):
            at = qkv_base + k * ch
            gw[at : at + ch] += wide[:, k * ch : (k + 1) * ch]
        add_conv_grad(
            conv_base + 9 * ch,
            a2h[s, L : L + R1],
            a2l[s, L : L + R1],
            th[L : L + R],
            tl[L : L + R],
        )
        pl.when(s == 0)(lambda: advance(0))
        sums = sum_wait(s * 4 + 2)
        halo_wait(hb + 4, de1, s, 1)
        pl.when(s == 0)(lambda: advance(1))
        grad1 = norm_rest(
            s, 1, h1[s, L : L + R1], mask[L : L + R1], de1[s, L : L + R1], sums
        )
        t_h, t_l = lat_triple(grad1)
        (grad_act,) = conv_back(t_h, t_l, all_own, w3t[0])
        sums, direct = norm_back(
            s, 0, h0[s, 2 * L : 2 * L + R], grad_act, dg1[s], grad1[L : L + R]
        )
        sum_start(s * 4 + 3, sums)
        de0[s, 2 * L : 2 * L + R] = direct
        halo_start(hb + 5, de0, s, 2)
        add_conv_grad(
            conv_base, a1h[s], a1l[s], t_h[L : L + R], t_l[L : L + R]
        )

        def lift_grad(s):
            add_conv_grad(
                0, xh[s], xl[s], lift_th[...], lift_tl[...], tap_rows(cin)
            )

        pl.when(s < SECTIONS - 1)(lambda: lift_grad(s + 1))
        dqkv[...] = jnp.zeros_like(dqkv)
        lane = lane_of(R)
        g = gk[s]
        g_lon = jnp.concatenate([g[L:], rb[s, 0, pair:]], axis=0)
        g_lon = 0.5 * (
            g_lon - jnp.concatenate([rb[s, 1, pair:], g[: R - L]], axis=0)
        )
        dflux = jnp.where(
            lane < VARS, lat_diff(g), jnp.where(lane < 2 * VARS, g_lon, 0.0)
        )
        y = ys[s, 2 * L : 2 * L + R]
        flux_parts[...] = dflux * lroll(y, -3 * VARS)
        flux_velocity[...] = lroll(dflux * y, 3 * VARS)
        pl.when(s == 0)(lambda: advance(2))
        sums = sum_wait(s * 4 + 3)
        halo_wait(hb + 5, de0, s, 2)

        @pl.when(s == 0)
        def _():
            advance(3)

        grad0 = norm_rest(s, 0, h0[s], mask[...], de0[s], sums)
        bias_acc[0:1] += jnp.sum(grad0[2 * L : 2 * L + R], axis=0, keepdims=True)
        t_h, t_l = lat_triple(grad0)
        lift_th[...] = t_h[2 * L : 2 * L + R]
        lift_tl[...] = t_l[2 * L : 2 * L + R]

        @pl.when(s == 0)
        def _():
            lift_grad(s)
            gw[cin : cin + 2] = bias_acc[...]
            advance(4)

        wide = product(t_h, t_l, lift_t[...])
        dx = (
            wide[2 * L :]
            + lroll(wide[L : L + R1], -LIFT_BACK)
            + lroll(wide[:R1], -2 * LIFT_BACK)
        )
        lane = lane_of(R)
        own = dx[L : L + R]
        lon = 0.5 * (dx[2 * L :] - dx[:R])
        parts = jnp.where(
            lane < VARS,
            own,
            jnp.where(lane < 2 * VARS, -lat_diff(own), -lon),
        )
        parts = parts + flux_parts[...]
        parts = jnp.where(lane < 3 * VARS, parts, 0.0)
        fields_grad = (
            parts
            + lroll(parts, VARS)
            + lroll(parts, 2 * VARS)
            + lroll(parts, -VARS)
            + lroll(parts, -2 * VARS)
        )
        velocity_grad = own + flux_velocity[...]
        gy = jnp.where(
            lane < 3 * VARS,
            fields_grad,
            jnp.where(lane < 5 * VARS, velocity_grad, 0.0),
        )
        grad_ref[...] += gy

        @pl.when(s > 0)
        def _():
            factor = jnp.where(s == SECTIONS - 1, 1.0, 0.5) * step_size
            gk[s - 1] = gk[s - 1] + factor * gy

        return carry

    lax.fori_loop(0, SECTIONS, backward, 0)

    advance(5)
    all_out[gw.shape[0] : gw.shape[0] + 4] = norm_acc[...].reshape(4, ch)
    lane = lane_of(R)
    new, grad = acc[...], grad_ref[...]
    merged = jnp.where(
        lane < at_v,
        new,
        jnp.where(
            lane < at_cf,
            lroll(new, at_v - 3 * VARS),
            jnp.where(
                lane < at_cv, lroll(grad, at_cf), lroll(grad, at_cv - 3 * VARS)
            ),
        ),
    )
    for col in range(W):
        x = merged[col * L : (col + 1) * L].T
        all_out[pl.ds(gw.shape[0] + 8 + col, at_m, stride=W), :] = lanes_cat(
            x[:at_m], jnp.zeros((at_m, ch - L), f32)
        )

    state_result = pltpu.make_async_copy(
        all_out.at[all_rows:], final_out.at[all_rows:], out_sems.at[len(jobs)]
    )
    state_result.start()
    drain(jobs[::-1])
    state_result.wait()
    for job in jobs:
        job.result.wait()


def hand_out(rows, weights, *outs):
    fields = outs[:4]
    lift, lift_bias, gain, shift, conv, qkv, out, head, head_bias = outs[4:]
    ch = LANES
    at = rows + 8
    for ref in fields:
        ref[...] = weights[at : at + ref.shape[0], : ref.shape[1]]
        at += ref.shape[0]
    cin = lift.shape[2]
    vel = slice(3 * VARS, 5 * VARS)
    conv_base, qkv_base, out_base, head_base = bases(cin)
    for k in range(9):
        at = k * tap_rows(cin)
        lift[k // 3, k % 3] = weights[at : at + cin]
        for b in range(2):
            at = conv_base + (b * 9 + k) * ch
            conv[b, k // 3, k % 3] = weights[at : at + ch]
    lift_bias[...] = weights[cin : cin + 1]
    head_bias[...] = weights[cin + 1 : cin + 2, vel]
    for b in range(2):
        at = rows + 2 * b
        shift[b : b + 1] = weights[at : at + 1]
        gain[b : b + 1] = weights[at + 1 : at + 2]
    for k in range(3):
        at = qkv_base + k * ch
        qkv[:, k * ch : (k + 1) * ch] = weights[at : at + ch]
    out[...] = weights[out_base : out_base + ch]
    head[...] = weights[head_base + vel.start : head_base + vel.stop]


def on_device(
    nl,
    nb,
    fields,
    velocity,
    context,
    masks,
    window,
    lift_weight,
    lift_bias,
    norm_gain,
    norm_shift,
    conv_weight,
    attn_qkv,
    attn_out,
    head_weight,
    head_bias,
    cot_fields,
    cot_velocity,
):
    _, L, W, _ = fields.shape
    R, R1, R2 = L * W, L * (W + 2), L * (W + 4)
    ch = LANES
    nd = nl * nb

    def flat(x):
        return x[0].transpose(2, 1, 0).reshape(-1, L)

    S = SECTIONS
    cin = lift_weight.shape[2]
    rows = bases(cin)[-1] + HEAD_ROWS
    rows = -(-rows // (8 * nd)) * 8 * nd
    stage_count = len(factors(nl, 2)) + len(factors(nb, 4))
    job_count = len(job_plan(rows, 8 * nd, lift_weight.shape[2]))
    vm = pltpu.VMEM
    dma = pltpu.SemaphoreType.DMA
    scratch = [
        vm((S + 1, R2, ch), f32),
        vm((S, R1, ch), bf16),
        vm((S, R1, ch), bf16),
        vm((S, R2, ch), f32),
        vm((S, R2, ch), f32),
        vm((S, R1, ch), bf16),
        vm((S, R1, ch), bf16),
        vm((S, R2, ch), bf16),
        vm((S, R2, ch), bf16),
        vm((S, R, ch), f32),
        vm((S, R, ch), f32),
        vm((S, R1, ch), bf16),
        vm((S, R1, ch), bf16),
        vm((S, R1, ch), bf16),
        vm((S, R1, ch), bf16),
        vm((S, R1, ch), bf16),
        vm((S, R1, ch), bf16),
        vm((S, R1, ch), bf16),
        vm((S, R1, ch), bf16),
        vm((S, W // 2, 4 * L, 2 * HEADS * L), f32),
        vm((S, R, ch), bf16),
        vm((S, R, ch), bf16),
        vm((S, R, ch), bf16),
        vm((S, R, ch), bf16),
        vm((S, 2, 8, ch), f32),
        vm((S, R, ch), f32),
        vm((R, ch), f32),
        vm((R, ch), f32),
        vm((R2, ch), f32),
        vm((W // 2, 4 * L, 2 * HEADS * L), f32),
        vm((3, 9 * ch, 3 * ch), bf16),
        vm((2, 9 * ch, 3 * ch), bf16),
        vm((6 * ch, 2 * ch), bf16),
        vm((2 * ch, 6 * ch), bf16),
        vm((6 * ch, 2 * ch), bf16),
        vm((2 * ch, 2 * ch), bf16),
        vm((2 * ch, 2 * ch), bf16),
        vm((2 * ch, 2 * ch), bf16),
        vm((2 * ch, 2 * ch), bf16),
        vm((ch, ch), f32),
        vm((R, ch), f32),
        vm((R, ch), bf16),
        vm((R, ch), bf16),
        vm((R, ch), bf16),
        vm((R, ch), bf16),
        vm((R, ch), bf16),
        vm((R, ch), bf16),
        vm((R1, 3 * ch), bf16),
        vm((R1, 3 * ch), bf16),
        vm((R, 3 * ch), bf16),
        vm((R, 3 * ch), bf16),
        vm((R, ch), f32),
        vm((R, ch), f32),
        vm((2, ch), f32),
        vm((R1, 3 * ch), f32),
        vm((R1, ch), f32),
        vm((R1, ch), f32),
        vm((2, ch), f32),
        vm((S, R2, ch), f32),
        vm((S, R2, ch), f32),
        vm((S, 2, 3 * L, ch), f32),
        vm((S, 2, 3 * L, ch), f32),
        vm((rows, ch), f32),
        vm((rows, ch), f32),
        vm((2, 2, ch), f32),
        vm((2, ch), f32),
        vm((rows + 8 + 6 * VARS * W, ch), f32),
        dma((job_count + 1,)),
        vm((32 * W, L), f32),
        vm((W, L), jnp.int32),
        vm((R, context.shape[-1]), f32),
        vm((W, window.shape[-1], L), jnp.int32),
        vm(lift_weight.shape, f32),
        vm(conv_weight.shape, f32),
        vm(attn_qkv.shape, f32),
        vm(attn_out.shape, f32),
        vm(head_weight.shape[::-1], f32),
        vm((1, ch), f32),
        vm((R, ch), f32),
        dma((12,)),
        vm((4 * S + 1, 2, ch), f32),
        vm((4 * S + 1, nd, 2, ch), f32),
        dma((4 * S + 1,)),
        dma((4 * S + 1,)),
        dma((6 * S, 2)),
        dma((6 * S, 2)),
        dma((job_count, stage_count)),
        dma((job_count, stage_count)),
        dma((job_count, stage_count)),
        dma((job_count, stage_count)),
    ]
    whole = pl.BlockSpec(memory_space=pltpu.VMEM)
    apart = pl.BlockSpec(memory_space=pl.ANY)
    results = pl.pallas_call(
        partial(kernel, (nl, nb, L, W, HEADS)),
        out_shape=jax.ShapeDtypeStruct((rows + 8 + 6 * VARS * W, ch), f32),
        in_specs=[apart] * 12 + [whole] * 4,
        out_specs=apart,
        scratch_shapes=scratch,
        compiler_params=pltpu.CompilerParams(
            collective_id=0, has_side_effects=True, vmem_limit_bytes=60 * 2**20
        ),
    )(
        flat(fields),
        flat(velocity),
        flat(cot_fields),
        flat(cot_velocity),
        masks[0].T,
        context.reshape(R, -1),
        window.transpose(1, 2, 0),
        lift_weight,
        conv_weight,
        attn_qkv,
        attn_out,
        head_weight.T,
        lift_bias[None],
        head_bias[None],
        norm_gain,
        norm_shift,
    )
    pixels = VARS * W
    shapes = (
        (pixels, L),
        (2 * pixels, L),
        (pixels, L),
        (2 * pixels, L),
        lift_weight.shape,
        (1, ch),
        norm_gain.shape,
        norm_shift.shape,
        conv_weight.shape,
        attn_qkv.shape,
        attn_out.shape,
        head_weight.shape[::-1],
        (1, head_bias.shape[0]),
    )
    outs = pl.pallas_call(
        partial(hand_out, rows),
        out_shape=tuple(jax.ShapeDtypeStruct(shape, f32) for shape in shapes),
        in_specs=[whole],
        out_specs=(whole,) * len(shapes),
        compiler_params=pltpu.CompilerParams(vmem_limit_bytes=32 * 2**20),
    )(results)

    def field(x):
        return x.reshape(-1, W, L).transpose(2, 1, 0)[None]

    return (
        *(field(x) for x in outs[:4]),
        outs[4],
        outs[5][0],
        *outs[6:11],
        outs[11].T,
        outs[12][0],
    )


def solution(mesh):
    field = P("batch", None, "lon", None)
    return jax.shard_map(
        partial(on_device, mesh.shape["lon"], mesh.shape["batch"]),
        mesh=mesh,
        in_specs=(
            field,
            field,
            field,
            P("batch", None, "lon"),
            P(None, "lon", None),
            P(),
            P(),
            P(),
            P(),
            P(),
            P(),
            P(),
            P(),
            P(),
            field,
            field,
        ),
        out_specs=(field,) * 4 + (P(),) * 9,
        check_vma=False,
    )
```

```python
from functools import partial
import math

import jax
import jax.numpy as jnp
from jax import lax
from jax.experimental import pallas as pl
from jax.experimental.pallas import tpu as pltpu
from jax.sharding import PartitionSpec as P

HEADS = 4
SECTIONS = 4
LANES = 128
VARS = 5
MASK_LANE = 127
HEAD_ROWS = 32
LIFT_BACK = 32
epsilon = 1e-05
step_size = 0.25
f32 = jnp.float32
bf16 = jnp.bfloat16
MESH = pl.DeviceIdType.MESH


def split(x):
    hi = x.astype(bf16)
    return hi, (x - hi.astype(f32)).astype(bf16)


def dot(a, b, dims=((1,), (0,))):
    return lax.dot_general(a, b, (dims, ((), ())), preferred_element_type=f32)


def lanes_cat(*parts):
    return jnp.concatenate(parts, axis=1)


def factors(n, largest):
    out = []
    while n > largest and n % 2 == 0:
        out.append(2)
        n //= 2
    if n > 1:
        out.append(n)
    return out


def tap_rows(cin):
    return -(-(cin + 2) // 8) * 8


def bases(cin):
    conv = 9 * tap_rows(cin)
    qkv = conv + 18 * LANES
    out = qkv + 3 * LANES
    return conv, qkv, out, out + LANES


def job_plan(rows, unit, cin):
    conv = bases(cin)[0]
    late = -(-conv // unit)
    middle = -(-(conv + 9 * LANES) // unit) - late
    early = rows // unit - late - middle
    sizes = []
    for kind, units in enumerate((late, middle, early)):
        half = (units + 1) // 2
        sizes += [(half, "A", kind), (units - half, "B", kind)]
    plan, at = [], 0
    for units, order, kind in sizes:
        if units:
            plan.append((at * unit, units * unit, order, kind))
        at += units
    return plan


def kernel(
    sizes,
    fields_in,
    velocity_in,
    cot_fields_in,
    cot_velocity_in,
    masks_in,
    context_in,
    window_in,
    lift_in,
    conv_in,
    qkv_in,
    out_in,
    head_in,
    lift_bias_ref,
    head_bias_ref,
    gain_ref,
    shift_ref,
    final_out,
    ys,
    xh,
    xl,
    h0,
    h1,
    a1h,
    a1l,
    a2h,
    a2l,
    dg1,
    dg2,
    h2h,
    h2l,
    qh,
    ql,
    kh,
    kl,
    vh,
    vl,
    probs,
    bh,
    bl,
    h3h,
    h3l,
    norms,
    gk,
    acc,
    tend,
    mask,
    mult,
    w3f,
    w3t,
    lift_t,
    wq3,
    wqt3,
    wo3,
    wot3,
    wh3,
    wht3,
    tap,
    blend,
    dbh,
    dbl,
    gh,
    gl,
    dh3h,
    dh3l,
    th,
    tl,
    lift_th,
    lift_tl,
    flux_parts,
    flux_velocity,
    lift_sums,
    dqkv,
    dh2,
    h2,
    count,
    de1,
    de0,
    sb,
    rb,
    gw,
    rsb,
    norm_acc,
    bias_acc,
    all_out,
    out_sems,
    planes,
    mask_plane,
    context_ref,
    window_ref,
    lift_ref,
    conv_ref,
    qkv_ref,
    out_ref,
    head_ref,
    head_bias_row,
    grad_ref,
    load_sems,
    ar_src,
    ar_buf,
    ar_send,
    ar_recv,
    halo_send,
    halo_recv,
    rs_send,
    rs_recv,
    ag_send,
    ag_recv,
):
    nl, nb, L, W, hid_heads = sizes
    nd = nl * nb
    R = L * W
    R1 = R + 2 * L
    R2 = R + 4 * L
    ch = LANES
    me_l = lax.axis_index("lon")
    me_b = lax.axis_index("batch")
    me = me_l * nb + me_b
    left = (lax.rem(me_l + nl - 1, nl), me_b)
    right = (lax.rem(me_l + 1, nl), me_b)

    def peer(k):
        t = lax.rem(me + k, nd)
        return (t // nb, lax.rem(t, nb))

    low_half = 1 - me_b // max(nb // 2, 1) if nb > 1 else 0
    lon_order = sorted(range(nl), key=lambda hop: -min(hop, nl - hop))
    barrier = pltpu.get_barrier_semaphore()

    def greet(k, c):
        pl.semaphore_signal(barrier, inc=1, device_id=peer(k), device_id_type=MESH)
        return c

    lax.fori_loop(1, nd, greet, 0)

    def sum_start(a, vals):
        ar_src[a] = vals
        ar_buf[a, me] = vals

        def send(k, c):
            to_b = k + low_half * (nb - 1 - 2 * k)
            for hop in lon_order:
                copy = pltpu.make_async_remote_copy(
                    ar_src.at[a],
                    ar_buf.at[a, me],
                    ar_send.at[a],
                    ar_recv.at[a],
                    device_id=(lax.rem(me_l + hop, nl), to_b),
                    device_id_type=MESH,
                )
                if hop == 0:
                    pl.when(to_b != me_b)(copy.start)
                else:
                    copy.start()
            return c

        lax.fori_loop(0, nb, send, 0)

    def sum_wait(a):
        got = ar_buf.at[a, pl.ds(0, nd - 1)]
        pltpu.make_async_copy(got, got, ar_recv.at[a]).wait()
        pltpu.make_async_copy(got, got, ar_send.at[a]).wait()
        return jnp.sum(ar_buf[a], axis=0)

    def side_copy(h, side, src, dst):
        return pltpu.make_async_remote_copy(
            src,
            dst,
            halo_send.at[h, side],
            halo_recv.at[h, side],
            device_id=left if side == 0 else right,
            device_id_type=MESH,
        )

    def halo_copies(h, buf, s, cols):
        n = cols * L
        lo = 2 * L - n
        to_left = side_copy(
            h, 0, buf.at[s, pl.ds(2 * L, n)], buf.at[s, pl.ds(R + 2 * L, n)]
        )
        to_right = side_copy(
            h, 1, buf.at[s, pl.ds(R + 2 * L - n, n)], buf.at[s, pl.ds(lo, n)]
        )
        return to_left, to_right

    def halo_start(h, buf, s, cols):
        for c in halo_copies(h, buf, s, cols):
            c.start()

    def halo_wait(h, buf, s, cols):
        for c in halo_copies(h, buf, s, cols):
            c.wait()

    def lat_of(n):
        return lax.broadcasted_iota(jnp.int32, (n, LANES), 0) % L

    def north(x):
        n = x.shape[0]
        return jnp.where(lat_of(n) == L - 1, 0.0, pltpu.roll(x, n - 1, 0))

    def south(x):
        n = x.shape[0]
        return jnp.where(lat_of(n) == 0, 0.0, pltpu.roll(x, 1, 0))

    def lat_diff(x):
        return 0.5 * (north(x) - south(x))

    def lane_of(n):
        return lax.broadcasted_iota(jnp.int32, (n, LANES), 1)

    def lroll(x, shift):
        return pltpu.roll(x, shift % LANES, 1)

    def rows_of(ref, ranges, base=0):
        parts = [ref[base + a : base + b] for a, b in ranges]
        return parts[0] if len(parts) == 1 else jnp.concatenate(parts, axis=0)

    def put_rows(ref, value, ranges, base=0):
        at = 0
        for a, b in ranges:
            ref[base + a : base + b] = value[at : at + b - a]
            at += b - a

    def conv(hi, lo, ranges, weights):
        cols_h = [rows_of(hi, ranges, j * L) for j in range(3)]
        cols_l = [rows_of(lo, ranges, j * L) for j in range(3)]
        wide = dot(lanes_cat(*cols_h, *cols_l, *cols_h), weights)
        return (
            wide[:, ch : 2 * ch]
            + south(wide[:, :ch])
            + north(wide[:, 2 * ch :])
        )

    def product(hi, lo, weights):
        wide = dot(lanes_cat(hi, lo), weights)
        n = wide.shape[1] // 2
        return wide[:, :n] + wide[:, n:]

    def rows_product(ah, al, gh, gl):
        t = ((0,), (0,))
        return dot(ah, gh, t) + dot(ah, gl, t) + dot(al, gh, t)

    def lat_triple(x):
        return split(lanes_cat(north(x), x, south(x)))

    def conv_back(hi, lo, ranges, weights):
        wider = [(a, b + 2 * L) for a, b in ranges]
        gh, gl = rows_of(hi, wider), rows_of(lo, wider)
        wide = dot(lanes_cat(gh, gl, gh), weights)
        outs, at = [], 0
        for a, b in ranges:
            n = b - a
            outs.append(
                wide[at + 2 * L : at + 2 * L + n, :ch]
                + wide[at + L : at + L + n, ch : 2 * ch]
                + wide[at : at + n, 2 * ch :]
            )
            at += n + 2 * L
        return outs

    def add_conv_grad(base, ah, al, gh, gl, taken=ch):
        for j in range(3):
            part = rows_product(
                ah[j * L : j * L + R], al[j * L : j * L + R], gh, gl
            )
            for i in range(3):
                at = base + (i * 3 + j) * taken
                gw[at : at + taken, :] += part[:taken, i * ch : (i + 1) * ch]

    cin = lift_in.shape[2]
    conv_base, qkv_base, out_base, head_base = bases(cin)

    all_rows = gw.shape[0]
    unit = 8 * nd
    minor, batch_parts = factors(nl, 2), factors(nb, 4)
    axes = [("lon", n) for n in minor] + [("batch", n) for n in batch_parts]
    steps = {"lon": 1, "batch": 1}
    members = []
    for axis, n in axes:
        mine = me_l if axis == "lon" else me_b
        members.append((axis, steps[axis], n, lax.rem(mine // steps[axis], n)))
        steps[axis] *= n
    def stage_of(member):
        axis, step, n, idx = member

        def device_of(q):
            shift = (q - idx) * step
            if axis == "lon":
                return (me_l + shift, me_b)
            return (me_l, me_b + shift)

        return n, idx, device_of

    first, rest = members[:1], members[1:]
    orders = {
        "A": first + rest,
        "B": first + rest[1::-1] + rest[2:],
    }

    def rows_at(at, n):
        return pl.ds(pl.multiple_of(at, 8), n)

    class Job:
        def __init__(self, number, base, size, order):
            self.number = number
            self.result = pltpu.make_async_copy(
                all_out.at[base : base + size],
                final_out.at[base : base + size],
                out_sems.at[number],
            )
            self.stages = stages = [stage_of(m) for m in orders[order]]
            self.regions = []
            off, slot = base, base
            for n, idx, _ in stages:
                part = size // n
                self.regions.append((off, part, slot))
                off = off + idx * part
                slot += (n - 1) * part
                size = part
            self.own, self.size = off, size
            self.done, self.todo = 0, list(self.moves())

        def scatter_start(self, t):
            n, idx, device_of = self.stages[t]
            off, part, slot = self.regions[t]
            for k in range(1, n):
                q = lax.rem(idx + k, n)
                pltpu.make_async_remote_copy(
                    gw.at[rows_at(off + q * part, part)],
                    rsb.at[pl.ds(slot + (n - 1 - k) * part, part)],
                    rs_send.at[self.number, t],
                    rs_recv.at[self.number, t],
                    device_id=device_of(q),
                    device_id_type=MESH,
                ).start()

        def scatter_finish(self, t):
            n, idx, _ = self.stages[t]
            off, part, slot = self.regions[t]
            got = rsb.at[pl.ds(slot, (n - 1) * part)]
            pltpu.make_async_copy(got, got, rs_recv.at[self.number, t]).wait()
            pltpu.make_async_copy(got, got, rs_send.at[self.number, t]).wait()
            mine = off + idx * part
            chunk = math.gcd(part, 128)

            def add(i, c):
                at = pl.multiple_of(i * chunk, 8)
                total = gw[rows_at(mine + at, chunk)]
                for k in range(n - 1):
                    total = total + rsb[rows_at(slot + k * part + at, chunk)]
                gw[rows_at(mine + at, chunk)] = total
                return c

            lax.fori_loop(0, part // chunk, add, 0)

        def gather_start(self, t):
            n, idx, device_of = self.stages[t]
            off, part, _ = self.regions[t]
            if t == len(self.stages) - 1:
                all_out[rows_at(self.own, self.size)] = gw[
                    rows_at(self.own, self.size)
                ]
            mine = all_out.at[rows_at(off + idx * part, part)]
            for k in range(1, n):
                pltpu.make_async_remote_copy(
                    mine,
                    mine,
                    ag_send.at[self.number, t],
                    ag_recv.at[self.number, t],
                    device_id=device_of(lax.rem(idx + k, n)),
                    device_id_type=MESH,
                ).start()

        def gather_finish(self, t):
            n, _, _ = self.stages[t]
            _, part, slot = self.regions[t]
            got = rsb.at[pl.ds(slot, (n - 1) * part)]
            pltpu.make_async_copy(got, got, ag_recv.at[self.number, t]).wait()
            pltpu.make_async_copy(got, got, ag_send.at[self.number, t]).wait()

        def finished(self):
            self.gather_finish(0)
            self.result.start()

        def moves(self):
            for t in range(len(self.stages)):
                yield partial(self.scatter_start, t)
                yield partial(self.scatter_finish, t)
            for t in reversed(range(len(self.stages))):
                yield partial(self.gather_start, t)
                yield partial(self.gather_finish, t) if t else self.finished

    def take_steps(job, n):
        for _ in range(n):
            job.done += 1
            job.todo[job.done - 1]()

    def drain(jobs):
        while any(job.done < len(job.todo) for job in jobs):
            for job in jobs:
                left_over = len(job.todo) - job.done
                take_steps(job, min(left_over, 1 + (job.done % 2 and left_over > 1)))

    jobs, late, middle, early = [], [], [], []
    for k, (base, size, order, kind) in enumerate(job_plan(all_rows, unit, lift_in.shape[2])):
        jobs.append(Job(k, base, size, order))
        (late, middle, early)[kind].append(jobs[-1])
    points = (
        ((early, 1),),
        ((early, 2),),
        ((middle, 1),),
        ((early, 2), (middle, 2)),
        ((late, 1),),
        ((late, 2),),
    )

    def advance(k):
        for some, n in points[k]:
            for job in some:
                take_steps(job, n)

    at_f, at_v, at_cf, at_cv, at_m = (
        k * VARS for k in (0, 1, 3, 4, 6)
    )
    loads = [
        (fields_in, planes.at[at_f * W : at_v * W]),
        (velocity_in, planes.at[at_v * W : at_cf * W]),
        (cot_fields_in, planes.at[at_cf * W : at_cv * W]),
        (cot_velocity_in, planes.at[at_cv * W : at_m * W]),
        (masks_in, mask_plane),
        (context_in, context_ref),
        (lift_in, lift_ref),
        (conv_in, conv_ref),
        (qkv_in, qkv_ref),
        (out_in, out_ref),
        (head_in, head_ref),
        (window_in, window_ref),
    ]
    loads = [
        pltpu.make_async_copy(src, dst, load_sems.at[k])
        for k, (src, dst) in enumerate(loads)
    ]
    for load in loads:
        load.start()
    planes[(at_m + 1) * W :] = jnp.zeros((W, L), f32)
    for load in loads[:6]:
        load.wait()
    planes[at_m * W : (at_m + 1) * W] = mask_plane[...].astype(f32)
    cots = []
    masks_own = []
    for col in range(W):
        at = 2 * L + col * L
        x = planes[pl.ds(col, at_m + 2, stride=W), :].T
        ys[0, at : at + L] = jnp.zeros((L, ch), f32)
        for k in range(3):
            ys[0, at : at + L, k * VARS : (k + 1) * VARS] = x[:, at_f:at_v]
            gk[0, at - 2 * L : at - L, k * VARS : (k + 1) * VARS] = x[:, at_cf:at_cv]
        ys[0, at : at + L, 3 * VARS : 5 * VARS] = x[:, at_v:at_cf]
        gk[0, at - 2 * L : at - L, 3 * VARS : 5 * VARS] = x[:, at_cv:at_m]
        gk[0, at - 2 * L : at - L, 5 * VARS :] = jnp.zeros((L, ch - 5 * VARS), f32)
        ys[0, at : at + L, 5 * VARS : 5 * VARS + context_ref.shape[1]] = context_ref[
            pl.ds(col, L, stride=W), :
        ]
        ys[0, at : at + L, MASK_LANE:] = x[:, at_m : at_m + 1]
    cot = gk[0]
    mask_own = jnp.broadcast_to(
        ys[0, 2 * L : 2 * L + R, MASK_LANE : MASK_LANE + 1], (R, LANES)
    )
    mask[2 * L : 2 * L + R] = mask_own
    count_part = jnp.sum(mask_own, axis=0, keepdims=True)
    for load in loads[6:8]:
        load.wait()

    tap[...] = jnp.zeros_like(tap)
    lift_t[...] = jnp.zeros_like(lift_t)
    for b in range(3):
        for i in range(3):
            for j in range(3):
                if b == 0:
                    tap[: lift_ref.shape[2]] = lift_ref[i, j]
                    w = tap[...]
                else:
                    w = conv_ref[b - 1, i, j]
                hi, lo = split(w)
                for p, part in enumerate((hi, hi, lo)):
                    at = (p * 3 + j) * ch
                    w3f[b, at : at + ch, i * ch : (i + 1) * ch] = part
                hi, lo = split(w.T)
                if b == 0:
                    cols = slice(j * LIFT_BACK, (j + 1) * LIFT_BACK)
                    hi, lo = hi[:, :LIFT_BACK], lo[:, :LIFT_BACK]
                    at, below = i * ch, (3 + i) * ch
                    lift_t[at : at + ch, cols] = hi
                    lift_t[below : below + ch, cols] = hi
                    cols = slice(ch + cols.start, ch + cols.stop)
                    lift_t[at : at + ch, cols] = lo
                    continue
                for p, part in enumerate((hi, hi, lo)):
                    at = (p * 3 + i) * ch
                    w3t[b - 1, at : at + ch, j * ch : (j + 1) * ch] = part

    pair = 2 * L
    last = W // 2 - 1
    all_own = [(0, R)]
    own_edges, own_inner = [(0, pair), (R - pair, R)], [(pair, R - pair)]
    lift_bias = lift_bias_ref[...]

    def stats(h, ranges):
        weighted = h * rows_of(mask, ranges, 2 * L)
        return jnp.concatenate(
            [
                jnp.sum(weighted, axis=0, keepdims=True),
                jnp.sum(weighted * h, axis=0, keepdims=True),
            ],
            axis=0,
        )

    def lift(s, ranges):
        value = conv(xh.at[s], xl.at[s], ranges, w3f[0]) + lift_bias
        put_rows(h0.at[s], value, ranges, 2 * L)
        return stats(value, ranges)

    def lay(s, a, b):
        y = ys[s, L + a : L + b]
        lane = lane_of(b - a)
        lon = 0.5 * (ys[s, 2 * L + a : 2 * L + b] - ys[s, a:b])
        x = jnp.where(
            (lane >= VARS) & (lane < 2 * VARS),
            lat_diff(y),
            jnp.where((lane >= 2 * VARS) & (lane < 3 * VARS), lon, y),
        )
        hi, lo = split(x)
        xh[s, a:b] = hi
        xl[s, a:b] = lo

    def lift_inner(s):
        lay(s, pair, R1 - pair)
        lift_sums[...] = lift(s, own_inner)

    lift_inner(0)
    pl.semaphore_wait(barrier, nd - 1)
    halo_start(0, ys, 0, 2)
    sum_start(4 * SECTIONS, jnp.concatenate([count_part, count_part], axis=0))

    def square(hi, lo):
        return jnp.concatenate(
            [lanes_cat(hi, lo), lanes_cat(hi, jnp.zeros_like(hi))], axis=0
        )

    def put_square(target, w):
        n, m = w.shape
        hi, lo = split(w)
        target[:n, :m] = hi
        target[:n, m:] = lo
        target[n:, :m] = hi
        target[n:, m:] = jnp.zeros_like(hi)

    for load in loads[8:]:
        load.wait()
    put_square(wq3, qkv_ref[...])
    put_square(wqt3, qkv_ref[...].T)
    put_square(wo3, out_ref[...])
    put_square(wot3, out_ref[...].T)
    tap[...] = jnp.zeros_like(tap)
    tap[3 * VARS : 5 * VARS] = head_ref[...]
    put_square(wht3, tap[...])
    put_square(wh3, tap[...].T)
    head_bias_row[...] = jnp.zeros_like(head_bias_row)
    head_bias_row[:, 3 * VARS : 5 * VARS] = head_bias_ref[...]
    for s, weight in enumerate((1.0, 2.0, 2.0, 1.0)):
        gk[s] = cot * (weight * step_size / 6.0)
    grad_ref[...] = cot
    acc[...] = jnp.zeros_like(acc)
    dqkv[...] = jnp.zeros_like(dqkv)
    gw[...] = jnp.zeros_like(gw)
    norm_acc[...] = jnp.zeros_like(norm_acc)
    bias_acc[...] = jnp.zeros_like(bias_acc)

    shape = (2 * pair, HEADS * pair)
    key_of = lax.broadcasted_iota(jnp.int32, shape, 0)
    key_of = key_of - lax.broadcasted_iota(jnp.int32, shape, 1) // L % 2 * L
    for p in range(W // 2):
        entries = lanes_cat(*[window_ref[2 * p], window_ref[2 * p + 1]] * HEADS)
        counted = jnp.zeros(shape, f32)
        for k in range(entries.shape[0]):
            counted = counted + jnp.where(entries[k : k + 1] == key_of, 1.0, 0.0)
        mult[p] = jnp.where(
            counted > 0.0, jnp.log(jnp.maximum(counted, 1.0)), -1e30
        )

    head_rows = lax.broadcasted_iota(jnp.int32, (HEADS * pair, ch), 0) // pair
    head_lanes = lax.broadcasted_iota(jnp.int32, (HEADS * pair, ch), 1) // (ch // HEADS)
    head_mask = jnp.where(head_rows == head_lanes, 1.0, 0.0)
    head_mask_h = head_mask.astype(bf16)
    scale = (ch // HEADS) ** -0.5

    def per_head(x):
        return jnp.concatenate([x] * HEADS, axis=0) * head_mask_h

    def heads_sum(x):
        x = x * head_mask
        return sum(x[h * pair : (h + 1) * pair] for h in range(1, HEADS)) + x[:pair]

    head_bias = head_bias_row[...]
    gains = [gain_ref[0:1], gain_ref[1:2]]
    shifts = [shift_ref[0:1], shift_ref[1:2]]

    def normalise(s, b, sums):
        total_count = count[0:1]
        average = sums[0:1] / total_count
        spread = sums[1:2] / total_count - average * average
        inverse = lax.rsqrt(spread + epsilon)
        norms[s, b, 0:1] = average
        norms[s, b, 1:2] = inverse
        return average, inverse

    def activity(h, b, average, inverse):
        z = (h - average) * inverse * gains[b] + shifts[b]
        below = 0.5 * (1.0 + lax.erf(z * (0.5**0.5)))
        slope = below + z * (
            jnp.exp(-0.5 * z * z) * (1.0 / math.sqrt(2.0 * math.pi))
        )
        return z * below, slope


    def forward(s, carry):
        hb = s * 6
        ext = 2 * pair

        halo_wait(hb, ys, s, 2)
        lay(s, 0, pair)
        lay(s, R1 - pair, R1)
        sum_start(s * 4, lift_sums[...] + lift(s, own_edges))
        halo_start(hb + 1, h0, s, 2)
        y1 = ys[s, L : L + R1]
        lane = lane_of(R1)
        flux = y1 * lroll(y1, -3 * VARS)
        flux = jnp.where(lane < 2 * VARS, flux, 0.0)
        own_lane = lane_of(R)
        t_lat = jnp.where(own_lane < VARS, lat_diff(flux[L : L + R]), 0.0)
        t_lon = jnp.where(
            own_lane >= VARS, 0.5 * (flux[2 * L : 2 * L + R] - flux[:R]), 0.0
        )
        t = -(t_lat + lroll(t_lon, -VARS))
        tend[...] = t + lroll(t, VARS) + lroll(t, 2 * VARS)

        @pl.when(s == 0)
        def _():
            count[...] = sum_wait(4 * SECTIONS)
            for at in (0, R + pair):
                mask[at : at + pair] = jnp.broadcast_to(
                    ys[0, at : at + pair, MASK_LANE : MASK_LANE + 1], (pair, LANES)
                )

        average, inverse = normalise(s, 0, sum_wait(s * 4))
        halo_wait(hb + 1, h0, s, 2)
        act, slope = activity(h0[s, L : L + R1], 0, average, inverse)
        dg1[s] = slope[L : L + R]
        hi, lo = split(act)
        a1h[s] = hi
        a1l[s] = lo
        second = h0[s, 2 * L : 2 * L + R] + conv(
            a1h.at[s], a1l.at[s], all_own, w3f[1]
        )
        h1[s, 2 * L : 2 * L + R] = second
        sum_start(s * 4 + 1, stats(second, all_own))
        halo_start(hb + 2, h1, s, 2)
        average, inverse = normalise(s, 1, sum_wait(s * 4 + 1))
        halo_wait(hb + 2, h1, s, 2)
        act, slope = activity(h1[s], 1, average, inverse)
        dg2[s] = slope[2 * L : 2 * L + R]
        hi, lo = split(act)
        a2h[s] = hi
        a2l[s] = lo

        def second_block(ranges):
            third = rows_of(h1.at[s], ranges, L) + conv(
                a2h.at[s], a2l.at[s], ranges, w3f[2]
            )
            put_rows(h2, third, ranges)
            hi, lo = split(third)
            put_rows(h2h.at[s], hi, ranges)
            put_rows(h2l.at[s], lo, ranges)
            mixing = product(hi, lo, wq3[...])
            hi, lo = split(mixing[:, :ch] * scale)
            put_rows(qh.at[s], hi, ranges)
            put_rows(ql.at[s], lo, ranges)
            hi, lo = split(mixing[:, ch : 2 * ch])
            put_rows(kh.at[s], hi, ranges)
            put_rows(kl.at[s], lo, ranges)
            hi, lo = split(mixing[:, 2 * ch :])
            put_rows(vh.at[s], hi, ranges)
            put_rows(vl.at[s], lo, ranges)

        def attend(pairs):
            scores = []
            for p in pairs:
                at = p * pair
                q_h = per_head(qh[s, at + L : at + L + pair])
                q_l = per_head(ql[s, at + L : at + L + pair])
                k_h = kh[s, at : at + ext]
                k_l = kl[s, at : at + ext]
                scores.append(
                    dot(
                        lanes_cat(k_h, k_l, k_h),
                        lanes_cat(q_h, q_h, q_l),
                        ((1,), (1,)),
                    )
                )
            weights = []
            for p, score in zip(pairs, scores):
                score = score + mult[p]
                e = jnp.exp(score - jnp.max(score, axis=0, keepdims=True))
                e = e * (1.0 / jnp.sum(e, axis=0, keepdims=True))
                probs[s, p] = e
                weights.append(e)
            for p, e in zip(pairs, weights):
                at = p * pair
                p_h, p_l = split(e.T)
                v_h = vh[s, at : at + ext]
                v_l = vl[s, at : at + ext]
                o = product(p_h, p_l, square(v_h, v_l))
                blend[at : at + pair] = heads_sum(o)

        weight = jnp.where((s == 0) | (s == SECTIONS - 1), 1.0, 2.0)
        factor = jnp.where(s == SECTIONS - 2, 1.0, 0.5) * step_size

        def finish(ranges):
            hi, lo = split(rows_of(blend, ranges))
            put_rows(bh.at[s], hi, ranges)
            put_rows(bl.at[s], lo, ranges)
            fourth = rows_of(h2, ranges, L) + product(hi, lo, wo3[...])
            hi, lo = split(fourth)
            put_rows(h3h.at[s], hi, ranges)
            put_rows(h3l.at[s], lo, ranges)
            slope_now = (
                rows_of(tend, ranges)
                + product(hi, lo, wh3[...])
                + head_bias
            )
            put_rows(acc, rows_of(acc, ranges) + weight * slope_now, ranges)
            put_rows(
                ys.at[s + 1],
                rows_of(ys.at[0], ranges, 2 * L) + factor * slope_now,
                ranges,
                2 * L,
            )

        second_block([(0, ext), (R1 - ext, R1)])
        attend([0, last])
        finish(own_edges)

        @pl.when(s < SECTIONS - 1)
        def _():
            halo_start(hb + 6, ys, s + 1, 2)

        second_block([(ext, R1 - ext)])
        attend(range(1, last))
        finish(own_inner)
        pl.when(s < SECTIONS - 1)(lambda: lift_inner(s + 1))
        return carry

    lax.fori_loop(0, SECTIONS, forward, 0)
    acc[...] = ys[0, 2 * L : 2 * L + R] + (step_size / 6.0) * acc[...]

    def norm_back(s, b, h, grad_act, slope, through):
        average = norms[s, b, 0:1]
        inverse = norms[s, b, 1:2]
        dz = grad_act * slope
        hat = (h - average) * inverse
        sums = jnp.concatenate(
            [
                jnp.sum(dz, axis=0, keepdims=True),
                jnp.sum(dz * hat, axis=0, keepdims=True),
            ],
            axis=0,
        )
        return sums, through + dz * (gains[b] * inverse)

    def norm_rest(s, b, h, weight_mask, direct, sums):
        average = norms[s, b, 0:1]
        inverse = norms[s, b, 1:2]
        hat = (h - average) * inverse
        norm_acc[b] += sums
        return direct - weight_mask * (
            gains[b] * inverse / count[0:1]
        ) * (sums[0:1] + hat * sums[1:2])

    def backward(turn, carry):
        s = SECTIONS - 1 - turn
        hb = s * 6
        g_h, g_l = split(gk[s])
        gh[...] = g_h
        gl[...] = g_l

        def head_back(ranges):
            hi, lo = rows_of(gh, ranges), rows_of(gl, ranges)
            grad3 = product(hi, lo, wht3[...])
            hi, lo = split(grad3)
            put_rows(dh2, grad3, ranges, L)
            put_rows(dh3h, hi, ranges)
            put_rows(dh3l, lo, ranges)
            hi, lo = split(product(hi, lo, wot3[...]))
            put_rows(dbh, hi, ranges)
            put_rows(dbl, lo, ranges)

        def attend_back(pairs):
            dps = []
            for p in pairs:
                at = p * pair
                d_h = per_head(dbh[pl.ds(at, pair)])
                d_l = per_head(dbl[pl.ds(at, pair)])
                v_h = vh[s, pl.ds(at, 2 * pair)]
                v_l = vl[s, pl.ds(at, 2 * pair)]
                dps.append(
                    dot(
                        lanes_cat(v_h, v_l, v_h),
                        lanes_cat(d_h, d_h, d_l),
                        ((1,), (1,)),
                    )
                )
            dss = []
            for p, dp in zip(pairs, dps):
                e = probs[s, p]
                dss.append(e * (dp - jnp.sum(e * dp, axis=0, keepdims=True)))
            for p, ds in zip(pairs, dss):
                at = p * pair
                k_h = kh[s, pl.ds(at, 2 * pair)]
                k_l = kl[s, pl.ds(at, 2 * pair)]
                t_h, t_l = split(ds.T)
                o = product(t_h, t_l, square(k_h, k_l))
                dqkv[pl.ds(at + L, pair), :ch] = heads_sum(o) * scale
                q_h = per_head(qh[s, at + L : at + L + pair])
                q_l = per_head(ql[s, at + L : at + L + pair])
                s_h, s_l = split(ds)
                o = dot(s_h, lanes_cat(q_h, q_l))
                o = o[:, :ch] + o[:, ch:] + dot(s_l, q_h)
                dqkv[pl.ds(at, 2 * pair), ch : 2 * ch] += o
                d_h = per_head(dbh[pl.ds(at, pair)])
                d_l = per_head(dbl[pl.ds(at, pair)])
                s_h, s_l = split(probs[s, p])
                o = dot(s_h, lanes_cat(d_h, d_l))
                o = o[:, :ch] + o[:, ch:] + dot(s_l, d_h)
                dqkv[pl.ds(at, 2 * pair), 2 * ch :] += o

        def to_hidden(ranges):
            hi, lo = split(rows_of(dqkv, ranges))
            part = product(hi, lo, wqt3[...])
            put_rows(dh2, rows_of(dh2, ranges) + part, ranges)

        def triple(ranges):
            hi, lo = lat_triple(rows_of(dh2, ranges))
            put_rows(th, hi, ranges)
            put_rows(tl, lo, ranges)

        dh2[:L] = jnp.zeros((L, ch), f32)
        dh2[R1 - L :] = jnp.zeros((L, ch), f32)
        head_back(own_edges)
        attend_back([0, last])
        border = [(0, pair), (R1 - pair, R1)]
        to_hidden(border)
        for side, (a, b) in enumerate(border):
            sb[s, side, :pair] = dh2[a:b]
        sb[s, 0, pair:] = gk[s, :L]
        sb[s, 1, pair:] = gk[s, R - L :]
        edges = [
            side_copy(hb + 3, side, sb.at[s, side], rb.at[s, side])
            for side in range(2)
        ]
        for e in edges:
            e.start()
        head_back(own_inner)
        attend_back(range(1, last))
        to_hidden([(pair, R1 - pair)])
        triple([(pair, R1 - pair)])
        (inner_act,) = conv_back(th, tl, own_inner, w3t[1])
        bias_acc[1:2] += jnp.sum(gk[s], axis=0, keepdims=True)
        for e in edges:
            e.wait()
        dh2[:pair] += rb[s, 1, :pair]
        dh2[R1 - pair :] += rb[s, 0, :pair]
        triple(border)
        low_act, high_act = conv_back(th, tl, own_edges, w3t[1])

        grad_act = jnp.concatenate([low_act, inner_act, high_act], axis=0)
        sums, direct = norm_back(
            s, 1, h1[s, 2 * L : 2 * L + R], grad_act, dg2[s], dh2[L : L + R]
        )
        sum_start(s * 4 + 2, sums)
        de1[s, 2 * L : 2 * L + R] = direct
        halo_start(hb + 4, de1, s, 1)
        part = rows_product(gh[...], gl[...], h3h[s], h3l[s])
        gw[head_base : head_base + HEAD_ROWS] += part[:HEAD_ROWS]
        gw[out_base : out_base + ch] += rows_product(
            bh[s], bl[s], dh3h[...], dh3l[...]
        )
        d_h, d_l = split(dqkv[...])
        wide = rows_product(h2h[s], h2l[s], d_h, d_l)
        for k in range(3):
            at = qkv_base + k * ch
            gw[at : at + ch] += wide[:, k * ch : (k + 1) * ch]
        add_conv_grad(
            conv_base + 9 * ch,
            a2h[s, L : L + R1],
            a2l[s, L : L + R1],
            th[L : L + R],
            tl[L : L + R],
        )
        pl.when(s == 0)(lambda: advance(0))
        sums = sum_wait(s * 4 + 2)
        halo_wait(hb + 4, de1, s, 1)
        pl.when(s == 0)(lambda: advance(1))
        grad1 = norm_rest(
            s, 1, h1[s, L : L + R1], mask[L : L + R1], de1[s, L : L + R1], sums
        )
        t_h, t_l = lat_triple(grad1)
        (grad_act,) = conv_back(t_h, t_l, all_own, w3t[0])
        sums, direct = norm_back(
            s, 0, h0[s, 2 * L : 2 * L + R], grad_act, dg1[s], grad1[L : L + R]
        )
        sum_start(s * 4 + 3, sums)
        de0[s, 2 * L : 2 * L + R] = direct
        halo_start(hb + 5, de0, s, 2)
        add_conv_grad(
            conv_base, a1h[s], a1l[s], t_h[L : L + R], t_l[L : L + R]
        )

        def lift_grad(s):
            add_conv_grad(
                0, xh[s], xl[s], lift_th[...], lift_tl[...], tap_rows(cin)
            )

        pl.when(s < SECTIONS - 1)(lambda: lift_grad(s + 1))
        dqkv[...] = jnp.zeros_like(dqkv)
        lane = lane_of(R)
        g = gk[s]
        g_lon = jnp.concatenate([g[L:], rb[s, 0, pair:]], axis=0)
        g_lon = 0.5 * (
            g_lon - jnp.concatenate([rb[s, 1, pair:], g[: R - L]], axis=0)
        )
        dflux = jnp.where(
            lane < VARS, lat_diff(g), jnp.where(lane < 2 * VARS, g_lon, 0.0)
        )
        y = ys[s, 2 * L : 2 * L + R]
        flux_parts[...] = dflux * lroll(y, -3 * VARS)
        flux_velocity[...] = lroll(dflux * y, 3 * VARS)
        pl.when(s == 0)(lambda: advance(2))
        sums = sum_wait(s * 4 + 3)
        halo_wait(hb + 5, de0, s, 2)

        @pl.when(s == 0)
        def _():
            advance(3)

        grad0 = norm_rest(s, 0, h0[s], mask[...], de0[s], sums)
        bias_acc[0:1] += jnp.sum(grad0[2 * L : 2 * L + R], axis=0, keepdims=True)
        t_h, t_l = lat_triple(grad0)
        lift_th[...] = t_h[2 * L : 2 * L + R]
        lift_tl[...] = t_l[2 * L : 2 * L + R]

        @pl.when(s == 0)
        def _():
            lift_grad(s)
            gw[cin : cin + 2] = bias_acc[...]
            advance(4)

        wide = product(t_h, t_l, lift_t[...])
        dx = (
            wide[2 * L :]
            + lroll(wide[L : L + R1], -LIFT_BACK)
            + lroll(wide[:R1], -2 * LIFT_BACK)
        )
        lane = lane_of(R)
        own = dx[L : L + R]
        lon = 0.5 * (dx[2 * L :] - dx[:R])
        parts = jnp.where(
            lane < VARS,
            own,
            jnp.where(lane < 2 * VARS, -lat_diff(own), -lon),
        )
        parts = parts + flux_parts[...]
        parts = jnp.where(lane < 3 * VARS, parts, 0.0)
        fields_grad = (
            parts
            + lroll(parts, VARS)
            + lroll(parts, 2 * VARS)
            + lroll(parts, -VARS)
            + lroll(parts, -2 * VARS)
        )
        velocity_grad = own + flux_velocity[...]
        gy = jnp.where(
            lane < 3 * VARS,
            fields_grad,
            jnp.where(lane < 5 * VARS, velocity_grad, 0.0),
        )
        grad_ref[...] += gy

        @pl.when(s > 0)
        def _():
            factor = jnp.where(s == SECTIONS - 1, 1.0, 0.5) * step_size
            gk[s - 1] = gk[s - 1] + factor * gy

        return carry

    lax.fori_loop(0, SECTIONS, backward, 0)

    advance(5)
    all_out[gw.shape[0] : gw.shape[0] + 4] = norm_acc[...].reshape(4, ch)
    lane = lane_of(R)
    new, grad = acc[...], grad_ref[...]
    merged = jnp.where(
        lane < at_v,
        new,
        jnp.where(
            lane < at_cf,
            lroll(new, at_v - 3 * VARS),
            jnp.where(
                lane < at_cv, lroll(grad, at_cf), lroll(grad, at_cv - 3 * VARS)
            ),
        ),
    )
    for col in range(W):
        x = merged[col * L : (col + 1) * L].T
        all_out[pl.ds(gw.shape[0] + 8 + col, at_m, stride=W), :] = lanes_cat(
            x[:at_m], jnp.zeros((at_m, ch - L), f32)
        )

    state_result = pltpu.make_async_copy(
        all_out.at[all_rows:], final_out.at[all_rows:], out_sems.at[len(jobs)]
    )
    state_result.start()
    drain(jobs[::-1])
    state_result.wait()
    for job in jobs:
        job.result.wait()


def hand_out(rows, cin, results, *refs):
    fields = refs[:4]
    lift, lift_bias, gain, shift, conv, qkv, out, head, head_bias = refs[4:13]
    weights, sems = refs[13:]
    ch = LANES
    vel = slice(3 * VARS, 5 * VARS)
    conv_base, qkv_base, out_base, head_base = bases(cin)

    def load(k, a, b):
        copy = pltpu.make_async_copy(results.at[a:b], weights.at[a:b], sems.at[k])
        copy.start()
        return copy

    half = conv_base + (qkv_base - conv_base) // 2
    conv_parts = [load(1, conv_base, half), load(2, half, qkv_base)]
    lift_part = load(0, 0, conv_base)
    rest = load(3, qkv_base, weights.shape[0])
    backs = []
    for k, (part, a, b) in enumerate(
        zip(conv_parts, (conv_base, half), (half, qkv_base))
    ):
        part.wait()
        backs.append(
            pltpu.make_async_copy(
                weights.at[a:b], conv.at[a - conv_base : b - conv_base], sems.at[4 + k]
            )
        )
        backs[-1].start()
    lift_part.wait()
    for k in range(9):
        at = k * tap_rows(cin)
        lift[k // 3, k % 3] = weights[at : at + cin]
    lift_bias[...] = weights[cin : cin + 1]
    head_bias[...] = weights[cin + 1 : cin + 2, vel]
    rest.wait()
    for k in range(3):
        at = qkv_base + k * ch
        qkv[:, k * ch : (k + 1) * ch] = weights[at : at + ch]
    out[...] = weights[out_base : out_base + ch]
    head[...] = weights[head_base + vel.start : head_base + vel.stop]
    for b in range(2):
        at = rows + 2 * b
        shift[b : b + 1] = weights[at : at + 1]
        gain[b : b + 1] = weights[at + 1 : at + 2]
    at = rows + 8
    for ref in fields:
        ref[...] = weights[at : at + ref.shape[0], : ref.shape[1]]
        at += ref.shape[0]
    for copy in backs:
        copy.wait()


def on_device(
    nl,
    nb,
    fields,
    velocity,
    context,
    masks,
    window,
    lift_weight,
    lift_bias,
    norm_gain,
    norm_shift,
    conv_weight,
    attn_qkv,
    attn_out,
    head_weight,
    head_bias,
    cot_fields,
    cot_velocity,
):
    _, L, W, _ = fields.shape
    R, R1, R2 = L * W, L * (W + 2), L * (W + 4)
    ch = LANES
    nd = nl * nb

    def flat(x):
        return x[0].transpose(2, 1, 0).reshape(-1, L)

    S = SECTIONS
    cin = lift_weight.shape[2]
    rows = bases(cin)[-1] + HEAD_ROWS
    rows = -(-rows // (8 * nd)) * 8 * nd
    stage_count = len(factors(nl, 2)) + len(factors(nb, 4))
    job_count = len(job_plan(rows, 8 * nd, lift_weight.shape[2]))
    vm = pltpu.VMEM
    dma = pltpu.SemaphoreType.DMA
    scratch = [
        vm((S + 1, R2, ch), f32),
        vm((S, R1, ch), bf16),
        vm((S, R1, ch), bf16),
        vm((S, R2, ch), f32),
        vm((S, R2, ch), f32),
        vm((S, R1, ch), bf16),
        vm((S, R1, ch), bf16),
        vm((S, R2, ch), bf16),
        vm((S, R2, ch), bf16),
        vm((S, R, ch), f32),
        vm((S, R, ch), f32),
        vm((S, R1, ch), bf16),
        vm((S, R1, ch), bf16),
        vm((S, R1, ch), bf16),
        vm((S, R1, ch), bf16),
        vm((S, R1, ch), bf16),
        vm((S, R1, ch), bf16),
        vm((S, R1, ch), bf16),
        vm((S, R1, ch), bf16),
        vm((S, W // 2, 4 * L, 2 * HEADS * L), f32),
        vm((S, R, ch), bf16),
        vm((S, R, ch), bf16),
        vm((S, R, ch), bf16),
        vm((S, R, ch), bf16),
        vm((S, 2, 8, ch), f32),
        vm((S, R, ch), f32),
        vm((R, ch), f32),
        vm((R, ch), f32),
        vm((R2, ch), f32),
        vm((W // 2, 4 * L, 2 * HEADS * L), f32),
        vm((3, 9 * ch, 3 * ch), bf16),
        vm((2, 9 * ch, 3 * ch), bf16),
        vm((6 * ch, 2 * ch), bf16),
        vm((2 * ch, 6 * ch), bf16),
        vm((6 * ch, 2 * ch), bf16),
        vm((2 * ch, 2 * ch), bf16),
        vm((2 * ch, 2 * ch), bf16),
        vm((2 * ch, 2 * ch), bf16),
        vm((2 * ch, 2 * ch), bf16),
        vm((ch, ch), f32),
        vm((R, ch), f32),
        vm((R, ch), bf16),
        vm((R, ch), bf16),
        vm((R, ch), bf16),
        vm((R, ch), bf16),
        vm((R, ch), bf16),
        vm((R, ch), bf16),
        vm((R1, 3 * ch), bf16),
        vm((R1, 3 * ch), bf16),
        vm((R, 3 * ch), bf16),
        vm((R, 3 * ch), bf16),
        vm((R, ch), f32),
        vm((R, ch), f32),
        vm((2, ch), f32),
        vm((R1, 3 * ch), f32),
        vm((R1, ch), f32),
        vm((R1, ch), f32),
        vm((2, ch), f32),
        vm((S, R2, ch), f32),
        vm((S, R2, ch), f32),
        vm((S, 2, 3 * L, ch), f32),
        vm((S, 2, 3 * L, ch), f32),
        vm((rows, ch), f32),
        vm((rows, ch), f32),
        vm((2, 2, ch), f32),
        vm((2, ch), f32),
        vm((rows + 8 + 6 * VARS * W, ch), f32),
        dma((job_count + 1,)),
        vm((32 * W, L), f32),
        vm((W, L), jnp.int32),
        vm((R, context.shape[-1]), f32),
        vm((W, window.shape[-1], L), jnp.int32),
        vm(lift_weight.shape, f32),
        vm(conv_weight.shape, f32),
        vm(attn_qkv.shape, f32),
        vm(attn_out.shape, f32),
        vm(head_weight.shape[::-1], f32),
        vm((1, ch), f32),
        vm((R, ch), f32),
        dma((12,)),
        vm((4 * S + 1, 2, ch), f32),
        vm((4 * S + 1, nd, 2, ch), f32),
        dma((4 * S + 1,)),
        dma((4 * S + 1,)),
        dma((6 * S, 2)),
        dma((6 * S, 2)),
        dma((job_count, stage_count)),
        dma((job_count, stage_count)),
        dma((job_count, stage_count)),
        dma((job_count, stage_count)),
    ]
    whole = pl.BlockSpec(memory_space=pltpu.VMEM)
    apart = pl.BlockSpec(memory_space=pl.ANY)
    results = pl.pallas_call(
        partial(kernel, (nl, nb, L, W, HEADS)),
        out_shape=jax.ShapeDtypeStruct((rows + 8 + 6 * VARS * W, ch), f32),
        in_specs=[apart] * 12 + [whole] * 4,
        out_specs=apart,
        scratch_shapes=scratch,
        compiler_params=pltpu.CompilerParams(
            collective_id=0, has_side_effects=True, vmem_limit_bytes=60 * 2**20
        ),
    )(
        flat(fields),
        flat(velocity),
        flat(cot_fields),
        flat(cot_velocity),
        masks[0].T,
        context.reshape(R, -1),
        window.transpose(1, 2, 0),
        lift_weight,
        conv_weight,
        attn_qkv,
        attn_out,
        head_weight.T,
        lift_bias[None],
        head_bias[None],
        norm_gain,
        norm_shift,
    )
    pixels = VARS * W
    shapes = (
        (pixels, L),
        (2 * pixels, L),
        (pixels, L),
        (2 * pixels, L),
        lift_weight.shape,
        (1, ch),
        norm_gain.shape,
        norm_shift.shape,
        (18 * ch, ch),
        attn_qkv.shape,
        attn_out.shape,
        head_weight.shape[::-1],
        (1, head_bias.shape[0]),
    )
    outs = pl.pallas_call(
        partial(hand_out, rows, cin),
        out_shape=tuple(jax.ShapeDtypeStruct(shape, f32) for shape in shapes),
        in_specs=[apart],
        out_specs=tuple(apart if k == 8 else whole for k in range(13)),
        scratch_shapes=[vm(results.shape, f32), dma((6,))],
        compiler_params=pltpu.CompilerParams(vmem_limit_bytes=60 * 2**20),
    )(results)

    def field(x):
        return x.reshape(-1, W, L).transpose(2, 1, 0)[None]

    return (
        *(field(x) for x in outs[:4]),
        outs[4],
        outs[5][0],
        *outs[6:8],
        outs[8].reshape(conv_weight.shape),
        *outs[9:11],
        outs[11].T,
        outs[12][0],
    )


def solution(mesh):
    field = P("batch", None, "lon", None)
    return jax.shard_map(
        partial(on_device, mesh.shape["lon"], mesh.shape["batch"]),
        mesh=mesh,
        in_specs=(
            field,
            field,
            field,
            P("batch", None, "lon"),
            P(None, "lon", None),
            P(),
            P(),
            P(),
            P(),
            P(),
            P(),
            P(),
            P(),
            P(),
            field,
            field,
        ),
        out_specs=(field,) * 4 + (P(),) * 9,
        check_vma=False,
    )
```
